32 devices in a mesh: seq: 4 (over y, core), exp: 8 (over z, x).
Axes of the slice: x: 2, y: 2, z: 4, core: 2. Of those that a mesh axis runs over, the one named last changes fastest.
Arguments:
- tokens: bfloat16 [4096, 1280], P(('seq', 'exp')), may hold values from -64 to 64
- slot_keys: bfloat16 [1280, 8], P(None, 'exp'), may hold values from -3 to 3
- w_in: bfloat16 [8, 5120, 1280], P('exp', 'seq'), may hold values from -0.15625 to 0.15625
- w_out: bfloat16 [8, 5120, 1280], P('exp', 'seq'), may hold values from -0.078125 to 0.078125
- cotangent: bfloat16 [4096, 1280], P(('seq', 'exp')), may hold values from -6 to 6
Outputs:
- layer_out: bfloat16 [4096, 1280], P(('seq', 'exp'))
- tokens_grad: bfloat16 [4096, 1280], P(('seq', 'exp'))
- keys_grad: float32 [1280, 8], P(None, 'exp')
- w_in_grad: bfloat16 [8, 5120, 1280], P('exp', 'seq')
- w_out_grad: bfloat16 [8, 5120, 1280], P('exp', 'seq')
The draws below stay inside these ranges and needn't reach their ends.
All inputs are finite; a program needn't handle non-finite values.
Results may differ from the reference program's by a relative error of at most 0.03.
Values may be sent and summed in bfloat16 or wider, within the bound.
No kernel may reach another device: no remote copies, remote signals or barrier semaphores. Data moves between devices by JAX's collectives and lax.ppermute only.
A program may use at most 64 MiB of HBM per device.

```python
import math
import jax
import jax.numpy as jnp
from jax import lax

D = 1280
FF = 5120
EXPERTS = 8
TOKENS = 4096


def slot_table(key):
    sub_key = jax.random.fold_in(key, 7)
    normals = jax.random.truncated_normal(sub_key, -6.0, 6.0, (D, EXPERTS), jnp.float32)
    return normals * (3.0 / math.sqrt(D))


def draw_slot_keys(key, part):
    return slot_table(key).astype(jnp.bfloat16)


def draw_tokens(key, part):
    base_key = jax.random.fold_in(key, 11)
    values = jax.random.truncated_normal(base_key, -6.0, 6.0, (TOKENS, D), jnp.float32)
    return jnp.clip(values, -64.0, 64.0).astype(jnp.bfloat16)


def levels(key, dims, cuts, low, largest):
    level = 1.0
    for dim, blocks in cuts:
        steps = jax.random.uniform(jax.random.fold_in(jax.random.fold_in(key, 6), dim), (blocks,), jnp.float32, low / len(cuts), largest / len(cuts))
        level = level * jnp.repeat(jnp.exp(steps), dims[dim] // blocks).reshape((-1,) + (1,) * (len(dims) - 1 - dim))
    return level


def centred(own_key, extent, width, limit, cuts=(), dtype=jnp.bfloat16):
    factor_of = levels(own_key, extent, cuts, -0.22, 0.18) if cuts else 1.0
    result = jax.random.normal(own_key, extent, jnp.float32) * width * factor_of
    return jnp.minimum(jnp.maximum(result, -limit), limit).astype(dtype)


def setup_inputs(seed: int = 0) -> dict:
    keys = jax.random.split(jax.random.key(seed), 6)
    tokens = draw_tokens(jax.random.fold_in(keys[5], 71), 0)
    slot_keys = draw_slot_keys(jax.random.fold_in(keys[5], 71), 0)
    w_in = centred(keys[2], (EXPERTS, FF, D), D ** -0.5, 0.15625, ((0, 8), (1, 4)))
    w_out = centred(keys[3], (EXPERTS, FF, D), FF ** -0.5, 0.078125, ((0, 8), (1, 4)))
    cotangent = centred(keys[4], (TOKENS, D), 1.0, 6.0, ((0, 32),))
    return dict(tokens=tokens, slot_keys=slot_keys, w_in=w_in, w_out=w_out, cotangent=cotangent)


tanh_coeff = 0.7978845608028654
cubic_coeff = 0.044715


def gelu_value(values):
    return 0.5 * values * (1.0 + jnp.tanh(tanh_coeff * (values + cubic_coeff * values * values * values)))


def gelu_slope(values):
    tanh_part = jnp.tanh(tanh_coeff * (values + cubic_coeff * values * values * values))
    return 0.5 * (1.0 + tanh_part) + 0.5 * values * (1.0 - tanh_part * tanh_part) * tanh_coeff * (1.0 + 3.0 * cubic_coeff * values * values)


def expert_forward(inputs):
    w_first, w_second, slot_row = inputs
    pre_act = jnp.dot(w_first, slot_row, preferred_element_type=jnp.float32)
    activation = gelu_value(pre_act).astype(jnp.bfloat16)
    return pre_act, jnp.dot(activation, w_second, preferred_element_type=jnp.float32)


def expert_backward(inputs):
    w_first, w_second, pre_act, slot_row, grad_row = inputs
    activation = gelu_value(pre_act).astype(jnp.bfloat16)
    act_grad = jnp.dot(w_second, grad_row, preferred_element_type=jnp.float32)
    second_grad = (activation.astype(jnp.float32)[:, None] * grad_row.astype(jnp.float32)[None, :]).astype(jnp.bfloat16)
    pre_grad = (act_grad * gelu_slope(pre_act)).astype(jnp.bfloat16)
    first_grad = (pre_grad.astype(jnp.float32)[:, None] * slot_row.astype(jnp.float32)[None, :]).astype(jnp.bfloat16)
    row_grad = jnp.dot(pre_grad, w_first, preferred_element_type=jnp.float32)
    return first_grad, second_grad, row_grad


def reference(tokens, slot_keys, w_in, w_out, cotangent):
    logits = jnp.dot(tokens, slot_keys, preferred_element_type=jnp.float32)
    slot_peak = jnp.max(logits, axis=0, keepdims=True)
    exp_terms = jnp.exp(logits - slot_peak)
    disp_prob = exp_terms / jnp.sum(exp_terms, axis=0, keepdims=True)
    dispatch = disp_prob.astype(jnp.bfloat16)
    slot_in = jnp.dot(dispatch.T, tokens, preferred_element_type=jnp.float32).astype(jnp.bfloat16)
    pre_act, slot_sum = lax.map(expert_forward, (w_in, w_out, slot_in))
    slot_out = slot_sum.astype(jnp.bfloat16)
    row_peak = jnp.max(logits, axis=1, keepdims=True)
    row_terms = jnp.exp(logits - row_peak)
    comb_prob = row_terms / jnp.sum(row_terms, axis=1, keepdims=True)
    combine = comb_prob.astype(jnp.bfloat16)
    layer_out = jnp.dot(combine, slot_out, preferred_element_type=jnp.float32).astype(jnp.bfloat16)
    comb_grad = jnp.dot(cotangent, slot_out.T, preferred_element_type=jnp.float32)
    slot_out_grad = jnp.dot(combine.T, cotangent, preferred_element_type=jnp.float32).astype(jnp.bfloat16)
    w_in_grad, w_out_grad, row_grads = lax.map(expert_backward, (w_in, w_out, pre_act, slot_in, slot_out_grad))
    slot_in_grad = row_grads.astype(jnp.bfloat16)
    disp_grad = jnp.dot(tokens, slot_in_grad.T, preferred_element_type=jnp.float32)
    correction = jnp.sum(disp_prob * disp_grad, axis=0, keepdims=True)
    comb_mean = jnp.sum(comb_prob * comb_grad, axis=1, keepdims=True)
    logit_grad = (comb_prob * (comb_grad - comb_mean) + disp_prob * (disp_grad - correction)).astype(jnp.bfloat16)
    tokens_grad = (jnp.dot(dispatch, slot_in_grad, preferred_element_type=jnp.float32)
                   + jnp.dot(logit_grad, slot_keys.T, preferred_element_type=jnp.float32)).astype(jnp.bfloat16)
    keys_grad = jnp.dot(tokens.T, logit_grad, preferred_element_type=jnp.float32)
    return layer_out, tokens_grad, keys_grad, w_in_grad, w_out_grad
```

```python
import jax
import jax.numpy as jnp
from jax import lax
from jax.sharding import PartitionSpec as P

tanh_coeff = 0.7978845608028654
cubic_coeff = 0.044715
LANES = 128


def gelu_parts(values):
    tanh_part = jnp.tanh(tanh_coeff * (values + cubic_coeff * values * values * values))
    value = 0.5 * values * (1.0 + tanh_part)
    slope = 0.5 * (1.0 + tanh_part) + 0.5 * values * (1.0 - tanh_part * tanh_part) * tanh_coeff * (
        1.0 + 3.0 * cubic_coeff * values * values
    )
    return value, slope


def rounded(values):
    return lax.reduce_precision(values, 8, 7)


def three_terms(values):
    first = rounded(values)
    second = rounded(values - first)
    third = rounded(values - first - second)
    return [term.astype(jnp.bfloat16) for term in (first, second, third)]


def dot(left, right, left_dim, right_dim):
    return lax.dot_general(
        left, right, (((left_dim,), (right_dim,)), ((), ())), preferred_element_type=jnp.float32
    )


def local(tokens, slot_keys, w_in, w_out, cotangent):
    both = ("seq", "exp")
    seq_size, exp_size = lax.axis_size("seq"), lax.axis_size("exp")
    devices = seq_size * exp_size
    experts, hidden, width = w_in.shape
    half = width // 2
    own_tokens = tokens.shape[0]
    side = lax.rem(lax.axis_index("seq"), 2)
    swap = [(i, i ^ 1) for i in range(seq_size)]

    tokens_pair = jnp.concatenate([tokens, lax.ppermute(tokens, "seq", swap)], axis=0)
    cotangent_pair = jnp.concatenate([cotangent, lax.ppermute(cotangent, "seq", swap)], axis=0)
    tokens_half = lax.dynamic_slice_in_dim(tokens_pair, side * half, half, 1)
    cotangent_half = lax.dynamic_slice_in_dim(cotangent_pair, side * half, half, 1)

    keys_all = lax.all_to_all(
        jnp.broadcast_to(slot_keys.T[None], (exp_size, experts, width)), "exp", 0, 0, tiled=True
    ).reshape(exp_size * experts, width)
    slots = exp_size * experts

    logits = dot(keys_all, tokens_pair, 1, 1)
    peak = jnp.max(logits, axis=1, keepdims=True)
    terms = jnp.exp(logits - peak)
    total = jnp.sum(terms, axis=1, keepdims=True)
    terms_high = rounded(terms)
    terms_low = terms - terms_high
    row_terms = jnp.exp(logits - jnp.max(logits, axis=0, keepdims=True))
    comb_prob = row_terms / jnp.sum(row_terms, axis=0, keepdims=True)
    combine = comb_prob.astype(jnp.bfloat16)
    sums = dot(
        jnp.concatenate([terms_high, terms_low], axis=0).astype(jnp.bfloat16), tokens_half, 1, 0
    )
    slot_sums = sums[:slots] + sums[slots:]
    grad_sums = dot(combine, cotangent_half, 1, 0)

    message = jnp.concatenate(
        [
            slot_sums,
            grad_sums,
            jnp.broadcast_to(peak, (slots, LANES // 2)),
            jnp.broadcast_to(total, (slots, LANES // 2)),
        ],
        axis=1,
    )
    parts = lax.all_to_all(
        jnp.broadcast_to(
            message.reshape(1, exp_size, experts, -1), (seq_size, exp_size, experts, message.shape[1])
        ).reshape(devices, experts, -1),
        both,
        0,
        0,
        tiled=True,
    ).reshape(seq_size // 2, 2, exp_size, experts, -1)
    peaks = parts[..., 2 * half]
    totals = parts[..., 2 * half + LANES // 2]
    slot_peak = jnp.max(peaks, axis=(0, 1, 2))
    scale = jnp.exp(peaks - slot_peak)
    slot_total = jnp.sum(totals[:, 0] * scale[:, 0], axis=(0, 1))
    slot_rows = jnp.sum(parts[..., :half] * scale[..., None], axis=(0, 2)) / slot_total[:, None]
    slot_rows = jnp.moveaxis(slot_rows, 0, 1).reshape(experts, width)
    slot_in = slot_rows.astype(jnp.bfloat16)
    slot_out_grad = jnp.sum(parts[..., half : 2 * half], axis=(0, 2))
    slot_out_grad = jnp.moveaxis(slot_out_grad, 0, 1).reshape(experts, width).astype(jnp.bfloat16)

    pre_act = jnp.einsum("efd,ed->ef", w_in, slot_in, preferred_element_type=jnp.float32)
    act_grad = jnp.einsum("efd,ed->ef", w_out, slot_out_grad, preferred_element_type=jnp.float32)
    value, slope = gelu_parts(pre_act)
    activation = value.astype(jnp.bfloat16)
    pre_grad = (act_grad * slope).astype(jnp.bfloat16)
    out_part = jnp.einsum("ef,efd->ed", activation, w_out, preferred_element_type=jnp.float32)
    grad_part = rounded(
        jnp.einsum("ef,efd->ed", pre_grad, w_in, preferred_element_type=jnp.float32)
    )
    corr_part = jnp.sum(slot_rows * grad_part, axis=1)

    scalars = three_terms(slot_peak) + three_terms(slot_total) + three_terms(corr_part)
    scalars = jnp.stack(scalars, axis=1)
    scalars = jnp.pad(scalars, ((0, 0), (0, LANES - scalars.shape[1])))
    rows = jnp.stack(
        [
            jnp.concatenate([out_part.astype(jnp.bfloat16), scalars], axis=1),
            jnp.concatenate([grad_part.astype(jnp.bfloat16), scalars], axis=1),
        ],
        axis=1,
    )
    gathered = lax.all_to_all(
        jnp.broadcast_to(rows[None], (devices,) + rows.shape), both, 0, 0, tiled=True
    )
    gathered = gathered.reshape((seq_size, slots) + rows.shape[1:])
    out_rows = gathered[:, :, 0, :width].reshape(seq_size * slots, width)
    grad_rows = gathered[:, :, 1, :width].reshape(seq_size * slots, width)
    extra = gathered[:, :, 0, width : width + 9].astype(jnp.float32).reshape(seq_size, slots, 3, 3)
    extra = jnp.sum(extra, axis=3)
    peak_all, total_all = extra[0, :, 0, None], extra[0, :, 1, None]
    correction = jnp.sum(extra[:, :, 2], axis=0)[:, None]

    comb_grad = jnp.sum(
        dot(out_rows, cotangent_pair, 1, 1).reshape(seq_size, slots, -1), axis=0
    )
    disp_grad = jnp.sum(dot(grad_rows, tokens_pair, 1, 1).reshape(seq_size, slots, -1), axis=0)
    disp_prob = jnp.exp(logits - peak_all) / total_all
    comb_mean = jnp.sum(comb_prob * comb_grad, axis=0, keepdims=True)
    logit_grad = (
        comb_prob * (comb_grad - comb_mean) + disp_prob * (disp_grad - correction)
    ).astype(jnp.bfloat16)

    keys_part = dot(logit_grad, tokens_half, 1, 0)
    keys_parts = lax.all_to_all(
        jnp.broadcast_to(
            keys_part.reshape(1, exp_size, experts, half), (seq_size, exp_size, experts, half)
        ).reshape(devices, experts, half),
        both,
        0,
        0,
        tiled=True,
    ).reshape(seq_size // 2, 2, exp_size, experts, half)
    keys_rows = jnp.moveaxis(jnp.sum(keys_parts, axis=(0, 2)), 0, 1).reshape(experts, width)
    keys_grad = keys_rows.T

    def tiled_rows(values):
        return jnp.tile(values, (seq_size, 1))

    layer_out = dot(tiled_rows(combine[:, :own_tokens]), out_rows, 0, 0).astype(jnp.bfloat16)
    dispatch = disp_prob[:, :own_tokens].astype(jnp.bfloat16)
    tokens_grad = (
        dot(tiled_rows(dispatch), grad_rows, 0, 0) + dot(logit_grad[:, :own_tokens], keys_all, 0, 0)
    ).astype(jnp.bfloat16)
    w_out_grad = (
        activation.astype(jnp.float32)[:, :, None] * slot_out_grad.astype(jnp.float32)[:, None, :]
    ).astype(jnp.bfloat16)
    w_in_grad = (
        pre_grad.astype(jnp.float32)[:, :, None] * slot_in.astype(jnp.float32)[:, None, :]
    ).astype(jnp.bfloat16)
    return (layer_out, tokens_grad, keys_grad, w_in_grad, w_out_grad)


def solution(mesh):
    return jax.shard_map(
        local,
        mesh=mesh,
        in_specs=(
            P(("seq", "exp"), None),
            P(None, "exp"),
            P("exp", "seq", None),
            P("exp", "seq", None),
            P(("seq", "exp"), None),
        ),
        out_specs=(
            P(("seq", "exp"), None),
            P(("seq", "exp"), None),
            P(None, "exp"),
            P("exp", "seq", None),
            P("exp", "seq", None),
        ),
        check_vma=False,
    )
```

```python
import functools

import jax
import jax.numpy as jnp
from jax import lax
from jax.experimental import pallas as pl
from jax.experimental.pallas import tpu as pltpu
from jax.sharding import PartitionSpec as P

tanh_coeff = 0.7978845608028654
cubic_coeff = 0.044715
LANES = 128


def dot(left, right, left_dim, right_dim):
    return lax.dot_general(
        left, right, (((left_dim,), (right_dim,)), ((), ())), preferred_element_type=jnp.float32
    )


def gelu_parts(values):
    tanh_part = jnp.tanh(tanh_coeff * (values + cubic_coeff * values * values * values))
    value = 0.5 * values * (1.0 + tanh_part)
    slope = 0.5 * (1.0 + tanh_part) + 0.5 * values * (1.0 - tanh_part * tanh_part) * tanh_coeff * (
        1.0 + 3.0 * cubic_coeff * values * values
    )
    return value, slope


def padded(rows, multiple):
    return -(-rows // multiple) * multiple


def bf16_terms(values, count):
    terms = []
    for _ in range(count):
        term = values.astype(jnp.bfloat16).astype(jnp.float32)
        terms.append(term)
        values = values - term
    return terms


def in_lanes(columns, lane):
    row = jnp.zeros((columns[0].shape[0], LANES), jnp.float32)
    for i, column in enumerate(columns):
        row = jnp.where(lane == i, column, row)
    return row


def from_lanes(row, lane, first, count):
    keep = (lane >= first) & (lane < first + count)
    return jnp.sum(jnp.where(keep, row, 0.0), axis=1, keepdims=True)


def lanes_of(rows):
    return lax.broadcasted_iota(jnp.int32, (rows, LANES), 1)


def call(kernel, out_shape, scratch_shapes, inputs, smem=0):
    return pl.pallas_call(
        kernel,
        out_shape=out_shape,
        in_specs=[pl.BlockSpec(memory_space=pltpu.SMEM)] * smem
        + [pl.BlockSpec(memory_space=pltpu.VMEM)] * (len(inputs) - smem),
        out_specs=jax.tree.map(lambda _: pl.BlockSpec(memory_space=pltpu.VMEM), out_shape),
        scratch_shapes=scratch_shapes,
        compiler_params=pltpu.CompilerParams(vmem_limit_bytes=24 * 1024 * 1024),
    )(*inputs)


def keys_kernel(key_ref, out_ref, rows_ref):
    width = key_ref.shape[1]
    rows_ref[...] = jnp.zeros_like(rows_ref)
    key = key_ref[...].astype(jnp.float32)
    for j in range(width // LANES):
        rows_ref[j : j + 1, :] = key[:, j * LANES : (j + 1) * LANES]
    block = rows_ref[...].astype(jnp.bfloat16)
    for i in range(out_ref.shape[0]):
        out_ref[i] = block


def sums_kernel(
    side_ref, keys_ref, tokens_ref, tokens_other_ref, cotangent_ref, cotangent_other_ref,
    message_ref, logits_ref, comb_ref, keys_all_ref, keys_rows_ref, rows_ref,
):
    slots = keys_ref.shape[0]
    width = tokens_ref.shape[1]
    half = width // 2
    chunks = half // LANES
    first = pl.multiple_of(side_ref[0] * half, LANES)

    keys_rows_ref[...] = keys_ref[...].astype(jnp.float32)
    keys = jnp.concatenate(
        [keys_rows_ref[:, j, :] for j in range(width // LANES)], axis=1
    ).astype(jnp.bfloat16)
    keys_all_ref[...] = keys
    logits = jnp.concatenate(
        [dot(keys, tokens_ref[...], 1, 1), dot(keys, tokens_other_ref[...], 1, 1)], axis=1
    )
    logits_ref[...] = logits
    own = tokens_ref.shape[0]

    row_terms = jnp.exp(logits - jnp.max(logits, axis=0, keepdims=True))
    comb_prob = row_terms / jnp.sum(row_terms, axis=0, keepdims=True)
    comb_ref[...] = comb_prob
    combine = comb_prob.astype(jnp.bfloat16)
    grad_sums = dot(combine[:, :own], cotangent_ref[:, pl.ds(first, half)], 1, 0) + dot(
        combine[:, own:], cotangent_other_ref[:, pl.ds(first, half)], 1, 0
    )

    peak = jnp.max(logits, axis=1, keepdims=True)
    terms = jnp.exp(logits - peak)
    total = jnp.sum(terms, axis=1, keepdims=True)
    parts = jnp.concatenate(bf16_terms(terms, 2), axis=0).astype(jnp.bfloat16)
    sums = dot(parts[:, :own], tokens_ref[:, pl.ds(first, half)], 1, 0) + dot(
        parts[:, own:], tokens_other_ref[:, pl.ds(first, half)], 1, 0
    )
    high, low = bf16_terms(sums[:slots] + sums[slots:], 2)
    for j in range(chunks):
        columns = slice(j * LANES, (j + 1) * LANES)
        rows_ref[:, j, :] = high[:, columns]
        rows_ref[:, chunks + j, :] = low[:, columns]
        rows_ref[:, 2 * chunks + j, :] = grad_sums[:, columns]
    stats = in_lanes(bf16_terms(peak, 3) + bf16_terms(total, 3), lanes_of(slots))
    rows_ref[:, 3 * chunks, :] = stats
    for j in range(3 * chunks + 1, rows_ref.shape[1]):
        rows_ref[:, j, :] = jnp.zeros_like(stats)
    block = rows_ref[...].astype(jnp.bfloat16)
    for q in range(message_ref.shape[0] // slots):
        message_ref[q * slots : (q + 1) * slots] = block


def expert_kernel(
    exp_size, parts_ref, w_in_ref, w_out_ref,
    message_ref, slot_in_ref, slot_out_grad_ref, activation_ref, pre_grad_ref, parts_rows_ref, rows_ref,
):
    devices = parts_ref.shape[0]
    seq_size = devices // exp_size
    width = w_in_ref.shape[1]
    chunks = width // LANES
    per_side = chunks // 2
    parts_rows_ref[...] = parts_ref[...].astype(jnp.float32)
    stats = parts_rows_ref[:, 3 * per_side, :]
    lane = lanes_of(devices)
    peaks = from_lanes(stats, lane, 0, 3)
    totals = from_lanes(stats, lane, 3, 3)
    slot_peak = jnp.max(peaks, axis=0, keepdims=True)
    scale = jnp.exp(peaks - slot_peak)

    def of_side(values, side):
        total = values[side * exp_size : (side + 1) * exp_size]
        for q in range(side + 2, seq_size, 2):
            total = total + values[q * exp_size : (q + 1) * exp_size]
        return jnp.sum(total, axis=0, keepdims=True)

    slot_total = of_side(totals * scale, 0)
    slot_chunks, grad_chunks = [[], []], [[], []]
    for j in range(per_side):
        weighted = (parts_rows_ref[:, j, :] + parts_rows_ref[:, per_side + j, :]) * scale
        grads = parts_rows_ref[:, 2 * per_side + j, :]
        for side in range(2):
            slot_chunks[side].append(of_side(weighted, side))
            grad_chunks[side].append(of_side(grads, side))
    slot_row = jnp.concatenate(slot_chunks[0] + slot_chunks[1], axis=1) / slot_total
    slot_in = slot_row.astype(jnp.bfloat16)
    slot_out_grad = jnp.concatenate(grad_chunks[0] + grad_chunks[1], axis=1).astype(jnp.bfloat16)
    slot_in_ref[...] = slot_in
    slot_out_grad_ref[...] = slot_out_grad

    pre_act = dot(slot_in, w_in_ref[...], 1, 1)
    act_grad = dot(slot_out_grad, w_out_ref[...], 1, 1)
    value, slope = gelu_parts(pre_act)
    activation = value.astype(jnp.bfloat16)
    pre_grad = (act_grad * slope).astype(jnp.bfloat16)
    activation_ref[...] = activation
    pre_grad_ref[...] = pre_grad
    out_part = dot(activation, w_out_ref[...], 1, 0)
    grad_part = dot(pre_grad, w_in_ref[...], 1, 0).astype(jnp.bfloat16).astype(jnp.float32)
    correction = jnp.sum(slot_row * grad_part, axis=1, keepdims=True)
    for j in range(chunks):
        columns = slice(j * LANES, (j + 1) * LANES)
        rows_ref[j : j + 1, :] = out_part[:, columns]
        rows_ref[chunks + j : chunks + j + 1, :] = grad_part[:, columns]
    stats = in_lanes(
        bf16_terms(slot_peak, 3) + bf16_terms(slot_total, 3) + bf16_terms(correction, 3), lanes_of(1)
    )
    rows_ref[2 * chunks : 2 * chunks + 1, :] = stats
    for j in range(2 * chunks + 1, rows_ref.shape[0]):
        rows_ref[j : j + 1, :] = jnp.zeros_like(stats)
    block = rows_ref[...].astype(jnp.bfloat16)
    for i in range(devices):
        message_ref[i] = block


def grads_kernel(
    side_ref, parts_ref, logits_ref, comb_ref, tokens_ref, tokens_other_ref, cotangent_ref, cotangent_other_ref,
    message_ref, slot_out_ref, slot_in_grad_ref, dispatch_ref, logit_grad_ref, parts_rows_ref,
):
    devices = parts_ref.shape[0]
    slots, _ = logits_ref.shape
    seq_size = devices // slots
    own, width = tokens_ref.shape
    half = width // 2
    chunks = width // LANES
    first = pl.multiple_of(side_ref[0] * half, LANES)
    parts_rows_ref[...] = parts_ref[...].astype(jnp.float32)
    out_rows = jnp.concatenate([parts_rows_ref[:, j, :] for j in range(chunks)], axis=1)
    grad_rows = jnp.concatenate([parts_rows_ref[:, chunks + j, :] for j in range(chunks)], axis=1)
    stats = parts_rows_ref[:, 2 * chunks, :]
    lane = lanes_of(slots)

    def over_seq(values):
        total = values[:slots]
        for q in range(1, seq_size):
            total = total + values[q * slots : (q + 1) * slots]
        return total

    peak = from_lanes(stats[:slots], lane, 0, 3)
    total = from_lanes(stats[:slots], lane, 3, 3)
    correction = from_lanes(over_seq(stats), lane, 6, 3)
    slot_out_ref[...] = over_seq(out_rows).astype(jnp.bfloat16)
    slot_in_grad_ref[...] = over_seq(grad_rows).astype(jnp.bfloat16)
    out_rows = out_rows.astype(jnp.bfloat16)
    grad_rows = grad_rows.astype(jnp.bfloat16)
    comb_grad = over_seq(
        jnp.concatenate(
            [dot(out_rows, cotangent_ref[...], 1, 1), dot(out_rows, cotangent_other_ref[...], 1, 1)], axis=1
        )
    )
    disp_grad = over_seq(
        jnp.concatenate(
            [dot(grad_rows, tokens_ref[...], 1, 1), dot(grad_rows, tokens_other_ref[...], 1, 1)], axis=1
        )
    )
    comb_prob = comb_ref[...]
    disp_prob = jnp.exp(logits_ref[...] - peak) / total
    comb_mean = jnp.sum(comb_prob * comb_grad, axis=0, keepdims=True)
    logit_grad = (
        comb_prob * (comb_grad - comb_mean) + disp_prob * (disp_grad - correction)
    ).astype(jnp.bfloat16)
    dispatch_ref[...] = disp_prob[:, :own].astype(jnp.bfloat16)
    logit_grad_ref[...] = logit_grad[:, :own]
    keys_part = dot(logit_grad[:, :own], tokens_ref[:, pl.ds(first, half)], 1, 0) + dot(
        logit_grad[:, own:], tokens_other_ref[:, pl.ds(first, half)], 1, 0
    )
    for s in range(slots):
        for q in range(seq_size):
            message_ref[q * slots + s] = keys_part[s : s + 1]


def local(tokens, slot_keys, w_in, w_out, cotangent):
    both = ("seq", "exp")
    seq_size, exp_size = lax.axis_size("seq"), lax.axis_size("exp")
    devices = seq_size * exp_size
    experts, hidden, width = w_in.shape
    assert experts == 1 and seq_size % 2 == 0
    slots = exp_size
    half = width // 2
    own = tokens.shape[0]
    side = lax.rem(lax.axis_index("seq"), 2).astype(jnp.int32).reshape(1)
    swap = [(i, i ^ 1) for i in range(seq_size)]
    f32, bf16 = jnp.float32, jnp.bfloat16
    shape = jax.ShapeDtypeStruct

    key_rows = padded(width // LANES, 16)
    key_message = call(
        keys_kernel,
        shape((exp_size, key_rows, LANES), bf16),
        [pltpu.VMEM((key_rows, LANES), f32)],
        [slot_keys.T],
    )
    keys = lax.all_to_all(key_message, "exp", 0, 0, tiled=True)
    tokens_other = lax.ppermute(tokens, "seq", swap)
    cotangent_other = lax.ppermute(cotangent, "seq", swap)

    sum_rows = padded(3 * half // LANES + 1, 16)
    message, logits, comb_prob, keys_all = call(
        sums_kernel,
        (
            shape((devices, sum_rows, LANES), bf16),
            shape((slots, 2 * own), f32),
            shape((slots, 2 * own), f32),
            shape((slots, width), bf16),
        ),
        [pltpu.VMEM((slots, key_rows, LANES), f32), pltpu.VMEM((slots, sum_rows, LANES), f32)],
        [side, keys, tokens, tokens_other, cotangent, cotangent_other],
        smem=1,
    )
    parts = lax.all_to_all(message, both, 0, 0, tiled=True)

    row_count = padded(2 * width // LANES + 1, 8)
    message, slot_in, slot_out_grad, activation, pre_grad = call(
        functools.partial(expert_kernel, exp_size),
        (
            shape((devices, row_count, LANES), bf16),
            shape((1, width), bf16),
            shape((1, width), bf16),
            shape((1, hidden), bf16),
            shape((1, hidden), bf16),
        ),
        [pltpu.VMEM((devices, sum_rows, LANES), f32), pltpu.VMEM((row_count, LANES), f32)],
        [parts, w_in[0], w_out[0]],
    )
    gathered = lax.all_to_all(message, both, 0, 0, tiled=True)
    w_out_grad = (
        activation.astype(f32)[:, :, None] * slot_out_grad.astype(f32)[:, None, :]
    ).astype(bf16)
    w_in_grad = (pre_grad.astype(f32)[:, :, None] * slot_in.astype(f32)[:, None, :]).astype(bf16)

    message, slot_out, slot_in_grad, dispatch, logit_grad = call(
        grads_kernel,
        (
            shape((devices, 1, half), f32),
            shape((slots, width), bf16),
            shape((slots, width), bf16),
            shape((slots, own), bf16),
            shape((slots, own), bf16),
        ),
        [pltpu.VMEM((devices, row_count, LANES), f32)],
        [side, gathered, logits, comb_prob, tokens, tokens_other, cotangent, cotangent_other],
        smem=1,
    )
    keys_parts = lax.all_to_all(message, both, 0, 0, tiled=True)
    layer_out = dot(comb_prob[:, :own].astype(bf16), slot_out, 0, 0).astype(bf16)
    tokens_grad = (dot(dispatch, slot_in_grad, 0, 0) + dot(logit_grad, keys_all, 0, 0)).astype(bf16)
    keys_parts = keys_parts.reshape(seq_size // 2, 2, exp_size, half)
    keys_grad = jnp.sum(keys_parts, axis=(0, 2)).reshape(1, width).T
    return (layer_out, tokens_grad, keys_grad, w_in_grad, w_out_grad)


def solution(mesh):
    return jax.shard_map(
        local,
        mesh=mesh,
        in_specs=(
            P(("seq", "exp"), None),
            P(None, "exp"),
            P("exp", "seq", None),
            P("exp", "seq", None),
            P(("seq", "exp"), None),
        ),
        out_specs=(
            P(("seq", "exp"), None),
            P(("seq", "exp"), None),
            P(None, "exp"),
            P("exp", "seq", None),
            P("exp", "seq", None),
        ),
        check_vma=False,
    )
```

```python
import functools

import jax
import jax.numpy as jnp
from jax import lax
from jax.experimental import pallas as pl
from jax.experimental.pallas import tpu as pltpu
from jax.sharding import PartitionSpec as P

tanh_coeff = 0.7978845608028654
cubic_coeff = 0.044715
LANES = 128


def dot(left, right, left_dim, right_dim):
    return lax.dot_general(
        left, right, (((left_dim,), (right_dim,)), ((), ())), preferred_element_type=jnp.float32
    )


def gelu_parts(values):
    tanh_part = jnp.tanh(tanh_coeff * (values + cubic_coeff * values * values * values))
    value = 0.5 * values * (1.0 + tanh_part)
    slope = 0.5 * (1.0 + tanh_part) + 0.5 * values * (1.0 - tanh_part * tanh_part) * tanh_coeff * (
        1.0 + 3.0 * cubic_coeff * values * values
    )
    return value, slope


def padded(rows, multiple):
    return -(-rows // multiple) * multiple


def bf16_terms(values, count):
    terms = []
    for _ in range(count):
        term = values.astype(jnp.bfloat16).astype(jnp.float32)
        terms.append(term)
        values = values - term
    return terms


def in_lanes(columns, lane):
    row = jnp.zeros((columns[0].shape[0], LANES), jnp.float32)
    for i, column in enumerate(columns):
        row = jnp.where(lane == i, column, row)
    return row


def from_lanes(row, lane, first, count):
    keep = (lane >= first) & (lane < first + count)
    return jnp.sum(jnp.where(keep, row, 0.0), axis=1, keepdims=True)


def lanes_of(rows):
    return lax.broadcasted_iota(jnp.int32, (rows, LANES), 1)


def call(kernel, out_shape, scratch_shapes, inputs):
    return pl.pallas_call(
        kernel,
        out_shape=out_shape,
        in_specs=[pl.BlockSpec(memory_space=pltpu.VMEM)] * len(inputs),
        out_specs=jax.tree.map(lambda _: pl.BlockSpec(memory_space=pltpu.VMEM), out_shape),
        scratch_shapes=scratch_shapes,
        compiler_params=pltpu.CompilerParams(vmem_limit_bytes=24 * 1024 * 1024),
    )(*inputs)


def keys_kernel(key_ref, out_ref, rows_ref):
    width = key_ref.shape[1]
    rows_ref[...] = jnp.zeros_like(rows_ref)
    key = key_ref[...].astype(jnp.float32)
    for j in range(width // LANES):
        rows_ref[j : j + 1, :] = key[:, j * LANES : (j + 1) * LANES]
    block = rows_ref[...].astype(jnp.bfloat16)
    for i in range(out_ref.shape[0]):
        out_ref[i] = block


def sums_kernel(
    keys_ref, tokens_ref, tokens_other_ref, cotangent_ref, cotangent_other_ref,
    message_ref, logits_ref, comb_ref, keys_all_ref, keys_rows_ref, rows_ref,
):
    slots = keys_ref.shape[0]
    width = tokens_ref.shape[1]
    half = width // 2
    chunks = half // LANES
    first = pl.multiple_of(lax.rem(lax.axis_index("seq"), 2) * half, LANES)

    keys_rows_ref[...] = keys_ref[...].astype(jnp.float32)
    keys = jnp.concatenate(
        [keys_rows_ref[:, j, :] for j in range(width // LANES)], axis=1
    ).astype(jnp.bfloat16)
    keys_all_ref[...] = keys
    logits = jnp.concatenate(
        [dot(keys, tokens_ref[...], 1, 1), dot(keys, tokens_other_ref[...], 1, 1)], axis=1
    )
    logits_ref[...] = logits
    own = tokens_ref.shape[0]

    row_terms = jnp.exp(logits - jnp.max(logits, axis=0, keepdims=True))
    comb_prob = row_terms / jnp.sum(row_terms, axis=0, keepdims=True)
    comb_ref[...] = comb_prob
    combine = comb_prob.astype(jnp.bfloat16)
    grad_sums = dot(combine[:, :own], cotangent_ref[:, pl.ds(first, half)], 1, 0) + dot(
        combine[:, own:], cotangent_other_ref[:, pl.ds(first, half)], 1, 0
    )

    peak = jnp.max(logits, axis=1, keepdims=True)
    terms = jnp.exp(logits - peak)
    total = jnp.sum(terms, axis=1, keepdims=True)
    parts = jnp.concatenate(bf16_terms(terms, 2), axis=0).astype(jnp.bfloat16)
    sums = dot(parts[:, :own], tokens_ref[:, pl.ds(first, half)], 1, 0) + dot(
        parts[:, own:], tokens_other_ref[:, pl.ds(first, half)], 1, 0
    )
    high, low = bf16_terms(sums[:slots] + sums[slots:], 2)
    for j in range(chunks):
        columns = slice(j * LANES, (j + 1) * LANES)
        rows_ref[:, j, :] = high[:, columns]
        rows_ref[:, chunks + j, :] = low[:, columns]
        rows_ref[:, 2 * chunks + j, :] = grad_sums[:, columns]
    stats = in_lanes(bf16_terms(peak, 3) + bf16_terms(total, 3), lanes_of(slots))
    rows_ref[:, 3 * chunks, :] = stats
    for j in range(3 * chunks + 1, rows_ref.shape[1]):
        rows_ref[:, j, :] = jnp.zeros_like(stats)
    block = rows_ref[...].astype(jnp.bfloat16)
    for q in range(message_ref.shape[0] // slots):
        message_ref[q * slots : (q + 1) * slots] = block


def expert_kernel(
    exp_size, parts_ref, w_in_ref, w_out_ref,
    message_ref, slot_in_ref, slot_out_grad_ref, activation_ref, pre_grad_ref, parts_rows_ref, rows_ref,
):
    devices = parts_ref.shape[0]
    seq_size = devices // exp_size
    width = w_in_ref.shape[1]
    chunks = width // LANES
    per_side = chunks // 2
    parts_rows_ref[...] = parts_ref[...].astype(jnp.float32)
    stats = parts_rows_ref[:, 3 * per_side, :]
    lane = lanes_of(devices)
    peaks = from_lanes(stats, lane, 0, 3)
    totals = from_lanes(stats, lane, 3, 3)
    slot_peak = jnp.max(peaks, axis=0, keepdims=True)
    scale = jnp.exp(peaks - slot_peak)

    def of_side(values, side):
        total = values[side * exp_size : (side + 1) * exp_size]
        for q in range(side + 2, seq_size, 2):
            total = total + values[q * exp_size : (q + 1) * exp_size]
        return jnp.sum(total, axis=0, keepdims=True)

    slot_total = of_side(totals * scale, 0)
    slot_chunks, grad_chunks = [[], []], [[], []]
    for j in range(per_side):
        weighted = (parts_rows_ref[:, j, :] + parts_rows_ref[:, per_side + j, :]) * scale
        grads = parts_rows_ref[:, 2 * per_side + j, :]
        for side in range(2):
            slot_chunks[side].append(of_side(weighted, side))
            grad_chunks[side].append(of_side(grads, side))
    slot_row = jnp.concatenate(slot_chunks[0] + slot_chunks[1], axis=1) / slot_total
    slot_in = slot_row.astype(jnp.bfloat16)
    slot_out_grad = jnp.concatenate(grad_chunks[0] + grad_chunks[1], axis=1).astype(jnp.bfloat16)
    slot_in_ref[...] = slot_in
    slot_out_grad_ref[...] = slot_out_grad

    pre_act = dot(slot_in, w_in_ref[...], 1, 1)
    act_grad = dot(slot_out_grad, w_out_ref[...], 1, 1)
    value, slope = gelu_parts(pre_act)
    activation = value.astype(jnp.bfloat16)
    pre_grad = (act_grad * slope).astype(jnp.bfloat16)
    activation_ref[...] = activation
    pre_grad_ref[...] = pre_grad
    out_part = dot(activation, w_out_ref[...], 1, 0)
    grad_part = dot(pre_grad, w_in_ref[...], 1, 0).astype(jnp.bfloat16).astype(jnp.float32)
    correction = jnp.sum(slot_row * grad_part, axis=1, keepdims=True)
    for j in range(chunks):
        columns = slice(j * LANES, (j + 1) * LANES)
        rows_ref[j : j + 1, :] = out_part[:, columns]
        rows_ref[chunks + j : chunks + j + 1, :] = grad_part[:, columns]
    stats = in_lanes(
        bf16_terms(slot_peak, 3) + bf16_terms(slot_total, 3) + bf16_terms(correction, 3), lanes_of(1)
    )
    rows_ref[2 * chunks : 2 * chunks + 1, :] = stats
    for j in range(2 * chunks + 1, rows_ref.shape[0]):
        rows_ref[j : j + 1, :] = jnp.zeros_like(stats)
    block = rows_ref[...].astype(jnp.bfloat16)
    for i in range(devices):
        message_ref[i] = block


def grads_kernel(
    parts_ref, logits_ref, comb_ref, tokens_ref, tokens_other_ref, cotangent_ref, cotangent_other_ref,
    message_ref, slot_out_ref, slot_in_grad_ref, dispatch_ref, logit_grad_ref, parts_rows_ref,
):
    devices = parts_ref.shape[0]
    slots, _ = logits_ref.shape
    seq_size = devices // slots
    own, width = tokens_ref.shape
    half = width // 2
    chunks = width // LANES
    first = pl.multiple_of(lax.rem(lax.axis_index("seq"), 2) * half, LANES)
    parts_rows_ref[...] = parts_ref[...].astype(jnp.float32)
    out_rows = jnp.concatenate([parts_rows_ref[:, j, :] for j in range(chunks)], axis=1)
    grad_rows = jnp.concatenate([parts_rows_ref[:, chunks + j, :] for j in range(chunks)], axis=1)
    stats = parts_rows_ref[:, 2 * chunks, :]
    lane = lanes_of(slots)

    def over_seq(values):
        total = values[:slots]
        for q in range(1, seq_size):
            total = total + values[q * slots : (q + 1) * slots]
        return total

    peak = from_lanes(stats[:slots], lane, 0, 3)
    total = from_lanes(stats[:slots], lane, 3, 3)
    correction = from_lanes(over_seq(stats), lane, 6, 3)
    slot_out_ref[...] = over_seq(out_rows).astype(jnp.bfloat16)
    slot_in_grad_ref[...] = over_seq(grad_rows).astype(jnp.bfloat16)
    out_rows = out_rows.astype(jnp.bfloat16)
    grad_rows = grad_rows.astype(jnp.bfloat16)
    comb_grad = over_seq(
        jnp.concatenate(
            [dot(out_rows, cotangent_ref[...], 1, 1), dot(out_rows, cotangent_other_ref[...], 1, 1)], axis=1
        )
    )
    disp_grad = over_seq(
        jnp.concatenate(
            [dot(grad_rows, tokens_ref[...], 1, 1), dot(grad_rows, tokens_other_ref[...], 1, 1)], axis=1
        )
    )
    comb_prob = comb_ref[...]
    disp_prob = jnp.exp(logits_ref[...] - peak) / total
    comb_mean = jnp.sum(comb_prob * comb_grad, axis=0, keepdims=True)
    logit_grad = (
        comb_prob * (comb_grad - comb_mean) + disp_prob * (disp_grad - correction)
    ).astype(jnp.bfloat16)
    dispatch_ref[...] = disp_prob[:, :own].astype(jnp.bfloat16)
    logit_grad_ref[...] = logit_grad[:, :own]
    keys_part = dot(logit_grad[:, :own], tokens_ref[:, pl.ds(first, half)], 1, 0) + dot(
        logit_grad[:, own:], tokens_other_ref[:, pl.ds(first, half)], 1, 0
    )
    for s in range(slots):
        for q in range(seq_size):
            message_ref[q * slots + s] = keys_part[s : s + 1]


def local(tokens, slot_keys, w_in, w_out, cotangent):
    both = ("seq", "exp")
    seq_size, exp_size = lax.axis_size("seq"), lax.axis_size("exp")
    devices = seq_size * exp_size
    experts, hidden, width = w_in.shape
    assert experts == 1 and seq_size % 2 == 0
    slots = exp_size
    half = width // 2
    own = tokens.shape[0]
    swap = [(i, i ^ 1) for i in range(seq_size)]
    f32, bf16 = jnp.float32, jnp.bfloat16
    shape = jax.ShapeDtypeStruct

    stay = [(i, i) for i in range(seq_size)]
    w_in_near = lax.ppermute(w_in, "seq", stay)
    w_out_near = lax.ppermute(w_out, "seq", stay)
    tokens_near = lax.ppermute(tokens, "seq", stay)
    cotangent_near = lax.ppermute(cotangent, "seq", stay)
    key_rows = padded(width // LANES, 16)
    key_message = call(
        keys_kernel,
        shape((exp_size, key_rows, LANES), bf16),
        [pltpu.VMEM((key_rows, LANES), f32)],
        [slot_keys.T],
    )
    keys = lax.all_to_all(key_message, "exp", 0, 0, tiled=True)
    tokens_other = lax.ppermute(tokens, "seq", swap)
    cotangent_other = lax.ppermute(cotangent, "seq", swap)

    sum_rows = padded(3 * half // LANES + 1, 16)
    message, logits, comb_prob, keys_all = call(
        sums_kernel,
        (
            shape((devices, sum_rows, LANES), bf16),
            shape((slots, 2 * own), f32),
            shape((slots, 2 * own), f32),
            shape((slots, width), bf16),
        ),
        [pltpu.VMEM((slots, key_rows, LANES), f32), pltpu.VMEM((slots, sum_rows, LANES), f32)],
        [keys, tokens_near, tokens_other, cotangent_near, cotangent_other],
    )
    parts = lax.all_to_all(message, both, 0, 0, tiled=True)

    row_count = padded(2 * width // LANES + 1, 8)
    message, slot_in, slot_out_grad, activation, pre_grad = call(
        functools.partial(expert_kernel, exp_size),
        (
            shape((devices, row_count, LANES), bf16),
            shape((1, width), bf16),
            shape((1, width), bf16),
            shape((1, hidden), bf16),
            shape((1, hidden), bf16),
        ),
        [pltpu.VMEM((devices, sum_rows, LANES), f32), pltpu.VMEM((row_count, LANES), f32)],
        [parts, w_in_near[0], w_out_near[0]],
    )
    gathered = lax.all_to_all(message, both, 0, 0, tiled=True)
    w_out_grad = (
        activation.astype(f32)[:, :, None] * slot_out_grad.astype(f32)[:, None, :]
    ).astype(bf16)
    w_in_grad = (pre_grad.astype(f32)[:, :, None] * slot_in.astype(f32)[:, None, :]).astype(bf16)

    message, slot_out, slot_in_grad, dispatch, logit_grad = call(
        grads_kernel,
        (
            shape((devices, 1, half), f32),
            shape((slots, width), bf16),
            shape((slots, width), bf16),
            shape((slots, own), bf16),
            shape((slots, own), bf16),
        ),
        [pltpu.VMEM((devices, row_count, LANES), f32)],
        [gathered, logits, comb_prob, tokens_near, tokens_other, cotangent_near, cotangent_other],
    )
    keys_parts = lax.all_to_all(message, both, 0, 0, tiled=True)
    layer_out = dot(comb_prob[:, :own].astype(bf16), slot_out, 0, 0).astype(bf16)
    tokens_grad = (dot(dispatch, slot_in_grad, 0, 0) + dot(logit_grad, keys_all, 0, 0)).astype(bf16)
    keys_parts = keys_parts.reshape(seq_size // 2, 2, exp_size, half)
    keys_grad = jnp.sum(keys_parts, axis=(0, 2)).reshape(1, width).T
    return (layer_out, tokens_grad, keys_grad, w_in_grad, w_out_grad)


def solution(mesh):
    return jax.shard_map(
        local,
        mesh=mesh,
        in_specs=(
            P(("seq", "exp"), None),
            P(None, "exp"),
            P("exp", "seq", None),
            P("exp", "seq", None),
            P(("seq", "exp"), None),
        ),
        out_specs=(
            P(("seq", "exp"), None),
            P(("seq", "exp"), None),
            P(None, "exp"),
            P("exp", "seq", None),
            P("exp", "seq", None),
        ),
        check_vma=False,
    )
```

```python
import functools

import jax
import jax.numpy as jnp
from jax import lax
from jax.experimental import pallas as pl
from jax.experimental.pallas import tpu as pltpu
from jax.sharding import PartitionSpec as P

tanh_coeff = 0.7978845608028654
cubic_coeff = 0.044715
LANES = 128


def dot(left, right, left_dim, right_dim):
    return lax.dot_general(
        left, right, (((left_dim,), (right_dim,)), ((), ())), preferred_element_type=jnp.float32
    )


def gelu_parts(values):
    tanh_part = jnp.tanh(tanh_coeff * (values + cubic_coeff * values * values * values))
    value = 0.5 * values * (1.0 + tanh_part)
    slope = 0.5 * (1.0 + tanh_part) + 0.5 * values * (1.0 - tanh_part * tanh_part) * tanh_coeff * (
        1.0 + 3.0 * cubic_coeff * values * values
    )
    return value, slope


def padded(rows, multiple):
    return -(-rows // multiple) * multiple


def bf16_terms(values, count):
    terms = []
    for _ in range(count):
        term = values.astype(jnp.bfloat16).astype(jnp.float32)
        terms.append(term)
        values = values - term
    return terms


def in_lanes(columns, lane):
    row = jnp.zeros((columns[0].shape[0], LANES), jnp.float32)
    for i, column in enumerate(columns):
        row = jnp.where(lane == i, column, row)
    return row


def from_lanes(row, lane, first, count):
    keep = (lane >= first) & (lane < first + count)
    return jnp.sum(jnp.where(keep, row, 0.0), axis=1, keepdims=True)


def block_of(rows):
    return 256 if rows % 256 == 0 else rows


def lanes_of(rows):
    return lax.broadcasted_iota(jnp.int32, (rows, LANES), 1)


def call(kernel, out_shape, scratch_shapes, inputs, unplaced=0, room=24 * 1024 * 1024):
    spaces = [pltpu.VMEM] * (len(inputs) - unplaced) + [pltpu.HBM] * unplaced
    return pl.pallas_call(
        kernel,
        out_shape=out_shape,
        in_specs=[pl.BlockSpec(memory_space=space) for space in spaces],
        out_specs=jax.tree.map(lambda _: pl.BlockSpec(memory_space=pltpu.VMEM), out_shape),
        scratch_shapes=scratch_shapes,
        compiler_params=pltpu.CompilerParams(vmem_limit_bytes=room),
    )(*inputs)


def keys_kernel(key_ref, out_ref, rows_ref):
    width = key_ref.shape[1]
    rows_ref[...] = jnp.zeros_like(rows_ref)
    key = key_ref[...].astype(jnp.float32)
    for j in range(width // LANES):
        rows_ref[j : j + 1, :] = key[:, j * LANES : (j + 1) * LANES]
    block = rows_ref[...].astype(jnp.bfloat16)
    for i in range(out_ref.shape[0]):
        out_ref[i] = block


def sums_kernel(
    keys_ref, tokens_other_ref, cotangent_other_ref, tokens_far_ref, cotangent_far_ref,
    message_ref, logits_ref, comb_ref, keys_all_ref,
    tokens_ref, cotangent_ref, keys_rows_ref, rows_ref, sems,
):
    tokens_copy = pltpu.make_async_copy(tokens_far_ref, tokens_ref, sems.at[0])
    cotangent_copy = pltpu.make_async_copy(cotangent_far_ref, cotangent_ref, sems.at[1])
    tokens_copy.start()
    cotangent_copy.start()
    slots = keys_ref.shape[0]
    width = tokens_ref.shape[1]
    half = width // 2
    chunks = half // LANES
    first = pl.multiple_of(lax.rem(lax.axis_index("seq"), 2) * half, LANES)

    keys_rows_ref[...] = keys_ref[...].astype(jnp.float32)
    keys = jnp.concatenate(
        [keys_rows_ref[:, j, :] for j in range(width // LANES)], axis=1
    ).astype(jnp.bfloat16)
    keys_all_ref[...] = keys
    other_logits = dot(keys, tokens_other_ref[...], 1, 1)
    tokens_copy.wait()
    logits = jnp.concatenate([dot(keys, tokens_ref[...], 1, 1), other_logits], axis=1)
    logits_ref[...] = logits
    own = tokens_ref.shape[0]

    row_terms = jnp.exp(logits - jnp.max(logits, axis=0, keepdims=True))
    comb_prob = row_terms / jnp.sum(row_terms, axis=0, keepdims=True)
    comb_ref[...] = comb_prob
    combine = comb_prob.astype(jnp.bfloat16)
    cotangent_copy.wait()
    grad_sums = dot(combine[:, :own], cotangent_ref[:, pl.ds(first, half)], 1, 0) + dot(
        combine[:, own:], cotangent_other_ref[:, pl.ds(first, half)], 1, 0
    )

    peak = jnp.max(logits, axis=1, keepdims=True)
    terms = jnp.exp(logits - peak)
    total = jnp.sum(terms, axis=1, keepdims=True)
    parts = jnp.concatenate(bf16_terms(terms, 2), axis=0).astype(jnp.bfloat16)
    sums = dot(parts[:, :own], tokens_ref[:, pl.ds(first, half)], 1, 0) + dot(
        parts[:, own:], tokens_other_ref[:, pl.ds(first, half)], 1, 0
    )
    high, low = bf16_terms(sums[:slots] + sums[slots:], 2)
    for j in range(chunks):
        columns = slice(j * LANES, (j + 1) * LANES)
        rows_ref[:, j, :] = high[:, columns]
        rows_ref[:, chunks + j, :] = low[:, columns]
        rows_ref[:, 2 * chunks + j, :] = grad_sums[:, columns]
    stats = in_lanes(bf16_terms(peak, 3) + bf16_terms(total, 3), lanes_of(slots))
    rows_ref[:, 3 * chunks, :] = stats
    for j in range(3 * chunks + 1, rows_ref.shape[1]):
        rows_ref[:, j, :] = jnp.zeros_like(stats)
    block = rows_ref[...].astype(jnp.bfloat16)
    for q in range(message_ref.shape[0] // slots):
        message_ref[q * slots : (q + 1) * slots] = block


def expert_kernel(
    exp_size, parts_ref, w_in_far_ref, w_out_far_ref,
    message_ref, slot_in_ref, slot_out_grad_ref, activation_ref, pre_grad_ref,
    w_in_ref, w_out_ref, parts_rows_ref, rows_ref, sems,
):
    hidden = w_in_ref.shape[0]
    block_rows = block_of(hidden)
    blocks = [pl.ds(i * block_rows, block_rows) for i in range(hidden // block_rows)]
    copies = [
        [pltpu.make_async_copy(far.at[rows], near.at[rows], sems.at[w, i]) for i, rows in enumerate(blocks)]
        for w, (far, near) in enumerate([(w_in_far_ref, w_in_ref), (w_out_far_ref, w_out_ref)])
    ]
    for pair in copies:
        for copy in pair:
            copy.start()
    devices = parts_ref.shape[0]
    seq_size = devices // exp_size
    width = w_in_ref.shape[1]
    chunks = width // LANES
    per_side = chunks // 2
    parts_rows_ref[...] = parts_ref[...].astype(jnp.float32)
    stats = parts_rows_ref[:, 3 * per_side, :]
    lane = lanes_of(devices)
    peaks = from_lanes(stats, lane, 0, 3)
    totals = from_lanes(stats, lane, 3, 3)
    slot_peak = jnp.max(peaks, axis=0, keepdims=True)
    scale = jnp.exp(peaks - slot_peak)

    def of_side(values, side):
        total = values[side * exp_size : (side + 1) * exp_size]
        for q in range(side + 2, seq_size, 2):
            total = total + values[q * exp_size : (q + 1) * exp_size]
        return jnp.sum(total, axis=0, keepdims=True)

    slot_total = of_side(totals * scale, 0)
    slot_chunks, grad_chunks = [[], []], [[], []]
    for j in range(per_side):
        weighted = (parts_rows_ref[:, j, :] + parts_rows_ref[:, per_side + j, :]) * scale
        grads = parts_rows_ref[:, 2 * per_side + j, :]
        for side in range(2):
            slot_chunks[side].append(of_side(weighted, side))
            grad_chunks[side].append(of_side(grads, side))
    slot_row = jnp.concatenate(slot_chunks[0] + slot_chunks[1], axis=1) / slot_total
    slot_in = slot_row.astype(jnp.bfloat16)
    slot_out_grad = jnp.concatenate(grad_chunks[0] + grad_chunks[1], axis=1).astype(jnp.bfloat16)
    slot_in_ref[...] = slot_in
    slot_out_grad_ref[...] = slot_out_grad

    def times_rows(row, copies_of, w_ref):
        outs = []
        for copy, rows in zip(copies_of, blocks):
            copy.wait()
            outs.append(dot(row, w_ref[rows, :], 1, 1))
        return jnp.concatenate(outs, axis=1)

    pre_act = times_rows(slot_in, copies[0], w_in_ref)
    act_grad = times_rows(slot_out_grad, copies[1], w_out_ref)
    value, slope = gelu_parts(pre_act)
    activation = value.astype(jnp.bfloat16)
    pre_grad = (act_grad * slope).astype(jnp.bfloat16)
    activation_ref[...] = activation
    pre_grad_ref[...] = pre_grad
    out_part = dot(activation, w_out_ref[...], 1, 0)
    grad_part = dot(pre_grad, w_in_ref[...], 1, 0).astype(jnp.bfloat16).astype(jnp.float32)
    correction = jnp.sum(slot_row * grad_part, axis=1, keepdims=True)
    for j in range(chunks):
        columns = slice(j * LANES, (j + 1) * LANES)
        rows_ref[j : j + 1, :] = out_part[:, columns]
        rows_ref[chunks + j : chunks + j + 1, :] = grad_part[:, columns]
    stats = in_lanes(
        bf16_terms(slot_peak, 3) + bf16_terms(slot_total, 3) + bf16_terms(correction, 3), lanes_of(1)
    )
    rows_ref[2 * chunks : 2 * chunks + 1, :] = stats
    for j in range(2 * chunks + 1, rows_ref.shape[0]):
        rows_ref[j : j + 1, :] = jnp.zeros_like(stats)
    block = rows_ref[...].astype(jnp.bfloat16)
    for i in range(devices):
        message_ref[i] = block


def grads_kernel(
    parts_ref, logits_ref, comb_ref, tokens_ref, tokens_other_ref, cotangent_ref, cotangent_other_ref,
    message_ref, slot_out_ref, slot_in_grad_ref, dispatch_ref, logit_grad_ref, parts_rows_ref,
):
    devices = parts_ref.shape[0]
    slots, _ = logits_ref.shape
    seq_size = devices // slots
    own, width = tokens_ref.shape
    half = width // 2
    chunks = width // LANES
    first = pl.multiple_of(lax.rem(lax.axis_index("seq"), 2) * half, LANES)
    parts_rows_ref[...] = parts_ref[...].astype(jnp.float32)
    out_rows = jnp.concatenate([parts_rows_ref[:, j, :] for j in range(chunks)], axis=1)
    grad_rows = jnp.concatenate([parts_rows_ref[:, chunks + j, :] for j in range(chunks)], axis=1)
    stats = parts_rows_ref[:, 2 * chunks, :]
    lane = lanes_of(slots)

    def over_seq(values):
        total = values[:slots]
        for q in range(1, seq_size):
            total = total + values[q * slots : (q + 1) * slots]
        return total

    peak = from_lanes(stats[:slots], lane, 0, 3)
    total = from_lanes(stats[:slots], lane, 3, 3)
    correction = from_lanes(over_seq(stats), lane, 6, 3)
    slot_out_ref[...] = over_seq(out_rows).astype(jnp.bfloat16)
    slot_in_grad_ref[...] = over_seq(grad_rows).astype(jnp.bfloat16)
    out_rows = out_rows.astype(jnp.bfloat16)
    grad_rows = grad_rows.astype(jnp.bfloat16)
    comb_grad = over_seq(
        jnp.concatenate(
            [dot(out_rows, cotangent_ref[...], 1, 1), dot(out_rows, cotangent_other_ref[...], 1, 1)], axis=1
        )
    )
    disp_grad = over_seq(
        jnp.concatenate(
            [dot(grad_rows, tokens_ref[...], 1, 1), dot(grad_rows, tokens_other_ref[...], 1, 1)], axis=1
        )
    )
    comb_prob = comb_ref[...]
    disp_prob = jnp.exp(logits_ref[...] - peak) / total
    comb_mean = jnp.sum(comb_prob * comb_grad, axis=0, keepdims=True)
    logit_grad = (
        comb_prob * (comb_grad - comb_mean) + disp_prob * (disp_grad - correction)
    ).astype(jnp.bfloat16)
    dispatch_ref[...] = disp_prob[:, :own].astype(jnp.bfloat16)
    logit_grad_ref[...] = logit_grad[:, :own]
    keys_part = dot(logit_grad[:, :own], tokens_ref[:, pl.ds(first, half)], 1, 0) + dot(
        logit_grad[:, own:], tokens_other_ref[:, pl.ds(first, half)], 1, 0
    )
    for s in range(slots):
        for q in range(seq_size):
            message_ref[q * slots + s] = keys_part[s : s + 1]


def local(tokens, slot_keys, w_in, w_out, cotangent):
    both = ("seq", "exp")
    seq_size, exp_size = lax.axis_size("seq"), lax.axis_size("exp")
    devices = seq_size * exp_size
    experts, hidden, width = w_in.shape
    assert experts == 1 and seq_size % 2 == 0
    slots = exp_size
    half = width // 2
    own = tokens.shape[0]
    swap = [(i, i ^ 1) for i in range(seq_size)]
    f32, bf16 = jnp.float32, jnp.bfloat16
    shape = jax.ShapeDtypeStruct

    key_rows = padded(width // LANES, 16)
    key_message = call(
        keys_kernel,
        shape((exp_size, key_rows, LANES), bf16),
        [pltpu.VMEM((key_rows, LANES), f32)],
        [slot_keys.T],
    )
    keys = lax.all_to_all(key_message, "exp", 0, 0, tiled=True)
    tokens_other = lax.ppermute(tokens, "seq", swap)
    cotangent_other = lax.ppermute(cotangent, "seq", swap)

    sum_rows = padded(3 * half // LANES + 1, 16)
    message, logits, comb_prob, keys_all = call(
        sums_kernel,
        (
            shape((devices, sum_rows, LANES), bf16),
            shape((slots, 2 * own), f32),
            shape((slots, 2 * own), f32),
            shape((slots, width), bf16),
        ),
        [
            pltpu.VMEM(tokens.shape, bf16),
            pltpu.VMEM(cotangent.shape, bf16),
            pltpu.VMEM((slots, key_rows, LANES), f32),
            pltpu.VMEM((slots, sum_rows, LANES), f32),
            pltpu.SemaphoreType.DMA((2,)),
        ],
        [keys, tokens_other, cotangent_other, tokens, cotangent],
        unplaced=2,
        room=(64 * 1024 - 11300) * 1024,
    )
    parts = lax.all_to_all(message, both, 0, 0, tiled=True)

    row_count = padded(2 * width // LANES + 1, 8)
    message, slot_in, slot_out_grad, activation, pre_grad = call(
        functools.partial(expert_kernel, exp_size),
        (
            shape((devices, row_count, LANES), bf16),
            shape((1, width), bf16),
            shape((1, width), bf16),
            shape((1, hidden), bf16),
            shape((1, hidden), bf16),
        ),
        [
            pltpu.VMEM((hidden, width), bf16),
            pltpu.VMEM((hidden, width), bf16),
            pltpu.VMEM((devices, sum_rows, LANES), f32),
            pltpu.VMEM((row_count, LANES), f32),
            pltpu.SemaphoreType.DMA((2, hidden // block_of(hidden))),
        ],
        [parts, w_in[0], w_out[0]],
        unplaced=2,
        room=(64 * 1024 - 13300) * 1024,
    )
    gathered = lax.all_to_all(message, both, 0, 0, tiled=True)
    w_out_grad = (
        activation.astype(f32)[:, :, None] * slot_out_grad.astype(f32)[:, None, :]
    ).astype(bf16)
    w_in_grad = (pre_grad.astype(f32)[:, :, None] * slot_in.astype(f32)[:, None, :]).astype(bf16)

    message, slot_out, slot_in_grad, dispatch, logit_grad = call(
        grads_kernel,
        (
            shape((devices, 1, half), f32),
            shape((slots, width), bf16),
            shape((slots, width), bf16),
            shape((slots, own), bf16),
            shape((slots, own), bf16),
        ),
        [pltpu.VMEM((devices, row_count, LANES), f32)],
        [gathered, logits, comb_prob, tokens, tokens_other, cotangent, cotangent_other],
    )
    keys_parts = lax.all_to_all(message, both, 0, 0, tiled=True)
    layer_out = dot(comb_prob[:, :own].astype(bf16), slot_out, 0, 0).astype(bf16)
    tokens_grad = (dot(dispatch, slot_in_grad, 0, 0) + dot(logit_grad, keys_all, 0, 0)).astype(bf16)
    keys_parts = keys_parts.reshape(seq_size // 2, 2, exp_size, half)
    keys_grad = jnp.sum(keys_parts, axis=(0, 2)).reshape(1, width).T
    return (layer_out, tokens_grad, keys_grad, w_in_grad, w_out_grad)


def solution(mesh):
    return jax.shard_map(
        local,
        mesh=mesh,
        in_specs=(
            P(("seq", "exp"), None),
            P(None, "exp"),
            P("exp", "seq", None),
            P("exp", "seq", None),
            P(("seq", "exp"), None),
        ),
        out_specs=(
            P(("seq", "exp"), None),
            P(("seq", "exp"), None),
            P(None, "exp"),
            P("exp", "seq", None),
            P("exp", "seq", None),
        ),
        check_vma=False,
    )
```

```python
import functools

import jax
import jax.numpy as jnp
from jax import lax
from jax.experimental import pallas as pl
from jax.experimental.pallas import tpu as pltpu
from jax.sharding import PartitionSpec as P

tanh_coeff = 0.7978845608028654
cubic_coeff = 0.044715
LANES = 128


def dot(left, right, left_dim, right_dim):
    return lax.dot_general(
        left, right, (((left_dim,), (right_dim,)), ((), ())), preferred_element_type=jnp.float32
    )


def gelu_parts(values):
    tanh_part = jnp.tanh(tanh_coeff * (values + cubic_coeff * values * values * values))
    value = 0.5 * values * (1.0 + tanh_part)
    slope = 0.5 * (1.0 + tanh_part) + 0.5 * values * (1.0 - tanh_part * tanh_part) * tanh_coeff * (
        1.0 + 3.0 * cubic_coeff * values * values
    )
    return value, slope


def padded(rows, multiple):
    return -(-rows // multiple) * multiple


def bf16_terms(values, count):
    terms = []
    for _ in range(count):
        term = values.astype(jnp.bfloat16).astype(jnp.float32)
        terms.append(term)
        values = values - term
    return terms


def in_lanes(columns, lane):
    row = jnp.zeros((columns[0].shape[0], LANES), jnp.float32)
    for i, column in enumerate(columns):
        row = jnp.where(lane == i, column, row)
    return row


def from_lanes(row, lane, first, count):
    keep = (lane >= first) & (lane < first + count)
    return jnp.sum(jnp.where(keep, row, 0.0), axis=1, keepdims=True)


def lanes_of(rows):
    return lax.broadcasted_iota(jnp.int32, (rows, LANES), 1)


def call(kernel, out_shape, scratch_shapes, inputs, unplaced=0, room=24 * 1024 * 1024):
    spaces = [pltpu.VMEM] * (len(inputs) - unplaced) + [pltpu.HBM] * unplaced
    return pl.pallas_call(
        kernel,
        out_shape=out_shape,
        in_specs=[pl.BlockSpec(memory_space=space) for space in spaces],
        out_specs=jax.tree.map(lambda _: pl.BlockSpec(memory_space=pltpu.VMEM), out_shape),
        scratch_shapes=scratch_shapes,
        compiler_params=pltpu.CompilerParams(vmem_limit_bytes=room),
    )(*inputs)


def keys_kernel(key_ref, out_ref, rows_ref):
    width = key_ref.shape[1]
    rows_ref[...] = jnp.zeros_like(rows_ref)
    key = key_ref[...].astype(jnp.float32)
    for j in range(width // LANES):
        rows_ref[j : j + 1, :] = key[:, j * LANES : (j + 1) * LANES]
    block = rows_ref[...].astype(jnp.bfloat16)
    for i in range(out_ref.shape[0]):
        out_ref[i] = block


def sums_kernel(
    keys_ref, tokens_other_ref, cotangent_other_ref, tokens_far_ref, cotangent_far_ref,
    message_ref, logits_ref, comb_ref, keys_all_ref,
    tokens_ref, cotangent_ref, keys_rows_ref, rows_ref, sems,
):
    tokens_copy = pltpu.make_async_copy(tokens_far_ref, tokens_ref, sems.at[0])
    cotangent_copy = pltpu.make_async_copy(cotangent_far_ref, cotangent_ref, sems.at[1])
    tokens_copy.start()
    cotangent_copy.start()
    slots = keys_ref.shape[0]
    width = tokens_ref.shape[1]
    half = width // 2
    chunks = half // LANES
    first = pl.multiple_of(lax.rem(lax.axis_index("seq"), 2) * half, LANES)

    keys_rows_ref[...] = keys_ref[...].astype(jnp.float32)
    keys = jnp.concatenate(
        [keys_rows_ref[:, j, :] for j in range(width // LANES)], axis=1
    ).astype(jnp.bfloat16)
    keys_all_ref[...] = keys
    other_logits = dot(keys, tokens_other_ref[...], 1, 1)
    tokens_copy.wait()
    logits = jnp.concatenate([dot(keys, tokens_ref[...], 1, 1), other_logits], axis=1)
    logits_ref[...] = logits
    own = tokens_ref.shape[0]

    row_terms = jnp.exp(logits - jnp.max(logits, axis=0, keepdims=True))
    comb_prob = row_terms / jnp.sum(row_terms, axis=0, keepdims=True)
    comb_ref[...] = comb_prob
    combine = comb_prob.astype(jnp.bfloat16)
    cotangent_copy.wait()
    grad_sums = dot(combine[:, :own], cotangent_ref[:, pl.ds(first, half)], 1, 0) + dot(
        combine[:, own:], cotangent_other_ref[:, pl.ds(first, half)], 1, 0
    )

    peak = jnp.max(logits, axis=1, keepdims=True)
    terms = jnp.exp(logits - peak)
    total = jnp.sum(terms, axis=1, keepdims=True)
    parts = jnp.concatenate(bf16_terms(terms, 2), axis=0).astype(jnp.bfloat16)
    sums = dot(parts[:, :own], tokens_ref[:, pl.ds(first, half)], 1, 0) + dot(
        parts[:, own:], tokens_other_ref[:, pl.ds(first, half)], 1, 0
    )
    high, low = bf16_terms(sums[:slots] + sums[slots:], 2)
    for j in range(chunks):
        columns = slice(j * LANES, (j + 1) * LANES)
        rows_ref[:, j, :] = high[:, columns]
        rows_ref[:, chunks + j, :] = low[:, columns]
        rows_ref[:, 2 * chunks + j, :] = grad_sums[:, columns]
    stats = in_lanes(bf16_terms(peak, 3) + bf16_terms(total, 3), lanes_of(slots))
    rows_ref[:, 3 * chunks, :] = stats
    for j in range(3 * chunks + 1, rows_ref.shape[1]):
        rows_ref[:, j, :] = jnp.zeros_like(stats)
    block = rows_ref[...].astype(jnp.bfloat16)
    for q in range(message_ref.shape[0] // slots):
        message_ref[q * slots : (q + 1) * slots] = block


def expert_kernel(
    exp_size, parts_ref, w_in_ref, w_out_ref,
    message_ref, slot_in_ref, slot_out_grad_ref, hidden_rows_ref, parts_rows_ref, rows_ref,
):
    devices = parts_ref.shape[0]
    seq_size = devices // exp_size
    width = w_in_ref.shape[1]
    chunks = width // LANES
    per_side = chunks // 2
    parts_rows_ref[...] = parts_ref[...].astype(jnp.float32)
    stats = parts_rows_ref[:, 3 * per_side, :]
    lane = lanes_of(devices)
    peaks = from_lanes(stats, lane, 0, 3)
    totals = from_lanes(stats, lane, 3, 3)
    slot_peak = jnp.max(peaks, axis=0, keepdims=True)
    scale = jnp.exp(peaks - slot_peak)

    def of_side(values, side):
        total = values[side * exp_size : (side + 1) * exp_size]
        for q in range(side + 2, seq_size, 2):
            total = total + values[q * exp_size : (q + 1) * exp_size]
        return jnp.sum(total, axis=0, keepdims=True)

    slot_total = of_side(totals * scale, 0)
    slot_chunks, grad_chunks = [[], []], [[], []]
    for j in range(per_side):
        weighted = (parts_rows_ref[:, j, :] + parts_rows_ref[:, per_side + j, :]) * scale
        grads = parts_rows_ref[:, 2 * per_side + j, :]
        for side in range(2):
            slot_chunks[side].append(of_side(weighted, side))
            grad_chunks[side].append(of_side(grads, side))
    slot_row = jnp.concatenate(slot_chunks[0] + slot_chunks[1], axis=1) / slot_total
    slot_in = slot_row.astype(jnp.bfloat16)
    slot_out_grad = jnp.concatenate(grad_chunks[0] + grad_chunks[1], axis=1).astype(jnp.bfloat16)
    slot_in_ref[...] = slot_in
    slot_out_grad_ref[...] = slot_out_grad

    pre_act = dot(slot_in, w_in_ref[...], 1, 1)
    act_grad = dot(slot_out_grad, w_out_ref[...], 1, 1)
    value, slope = gelu_parts(pre_act)
    activation = value.astype(jnp.bfloat16)
    pre_grad = (act_grad * slope).astype(jnp.bfloat16)
    hidden_rows_ref[...] = jnp.concatenate([value, act_grad * slope], axis=0).astype(jnp.bfloat16)
    out_part = dot(activation, w_out_ref[...], 1, 0)
    grad_part = dot(pre_grad, w_in_ref[...], 1, 0).astype(jnp.bfloat16).astype(jnp.float32)
    correction = jnp.sum(slot_row * grad_part, axis=1, keepdims=True)
    for j in range(chunks):
        columns = slice(j * LANES, (j + 1) * LANES)
        rows_ref[j : j + 1, :] = out_part[:, columns]
        rows_ref[chunks + j : chunks + j + 1, :] = grad_part[:, columns]
    stats = in_lanes(
        bf16_terms(slot_peak, 3) + bf16_terms(slot_total, 3) + bf16_terms(correction, 3), lanes_of(1)
    )
    rows_ref[2 * chunks : 2 * chunks + 1, :] = stats
    for j in range(2 * chunks + 1, rows_ref.shape[0]):
        rows_ref[j : j + 1, :] = jnp.zeros_like(stats)
    block = rows_ref[...].astype(jnp.bfloat16)
    for i in range(devices):
        message_ref[i] = block


def grads_kernel(
    parts_ref, logits_ref, comb_ref, tokens_ref, tokens_other_ref, cotangent_ref, cotangent_other_ref,
    message_ref, slot_out_ref, slot_in_grad_ref, dispatch_ref, logit_grad_ref, parts_rows_ref,
):
    devices = parts_ref.shape[0]
    slots, _ = logits_ref.shape
    seq_size = devices // slots
    own, width = tokens_ref.shape
    half = width // 2
    chunks = width // LANES
    first = pl.multiple_of(lax.rem(lax.axis_index("seq"), 2) * half, LANES)
    parts_rows_ref[...] = parts_ref[...].astype(jnp.float32)
    out_rows = jnp.concatenate([parts_rows_ref[:, j, :] for j in range(chunks)], axis=1)
    grad_rows = jnp.concatenate([parts_rows_ref[:, chunks + j, :] for j in range(chunks)], axis=1)
    stats = parts_rows_ref[:, 2 * chunks, :]
    lane = lanes_of(slots)

    def over_seq(values):
        total = values[:slots]
        for q in range(1, seq_size):
            total = total + values[q * slots : (q + 1) * slots]
        return total

    peak = from_lanes(stats[:slots], lane, 0, 3)
    total = from_lanes(stats[:slots], lane, 3, 3)
    correction = from_lanes(over_seq(stats), lane, 6, 3)
    slot_out_ref[...] = over_seq(out_rows).astype(jnp.bfloat16)
    slot_in_grad_ref[...] = over_seq(grad_rows).astype(jnp.bfloat16)
    out_rows = out_rows.astype(jnp.bfloat16)
    grad_rows = grad_rows.astype(jnp.bfloat16)
    comb_grad = over_seq(
        jnp.concatenate(
            [dot(out_rows, cotangent_ref[...], 1, 1), dot(out_rows, cotangent_other_ref[...], 1, 1)], axis=1
        )
    )
    disp_grad = over_seq(
        jnp.concatenate(
            [dot(grad_rows, tokens_ref[...], 1, 1), dot(grad_rows, tokens_other_ref[...], 1, 1)], axis=1
        )
    )
    comb_prob = comb_ref[...]
    disp_prob = jnp.exp(logits_ref[...] - peak) / total
    comb_mean = jnp.sum(comb_prob * comb_grad, axis=0, keepdims=True)
    logit_grad = (
        comb_prob * (comb_grad - comb_mean) + disp_prob * (disp_grad - correction)
    ).astype(jnp.bfloat16)
    dispatch_ref[...] = disp_prob[:, :own].astype(jnp.bfloat16)
    logit_grad_ref[...] = logit_grad[:, :own]
    keys_part = dot(logit_grad[:, :own], tokens_ref[:, pl.ds(first, half)], 1, 0) + dot(
        logit_grad[:, own:], tokens_other_ref[:, pl.ds(first, half)], 1, 0
    )
    for s in range(slots):
        for q in range(seq_size):
            message_ref[q * slots + s] = keys_part[s : s + 1]


def local(tokens, slot_keys, w_in, w_out, cotangent):
    both = ("seq", "exp")
    seq_size, exp_size = lax.axis_size("seq"), lax.axis_size("exp")
    devices = seq_size * exp_size
    experts, hidden, width = w_in.shape
    assert experts == 1 and seq_size % 2 == 0
    slots = exp_size
    half = width // 2
    own = tokens.shape[0]
    swap = [(i, i ^ 1) for i in range(seq_size)]
    f32, bf16 = jnp.float32, jnp.bfloat16
    shape = jax.ShapeDtypeStruct

    key_rows = padded(width // LANES, 16)
    key_message = call(
        keys_kernel,
        shape((exp_size, key_rows, LANES), bf16),
        [pltpu.VMEM((key_rows, LANES), f32)],
        [slot_keys.T],
    )
    keys = lax.all_to_all(key_message, "exp", 0, 0, tiled=True)
    tokens_other = lax.ppermute(tokens, "seq", swap)
    cotangent_other = lax.ppermute(cotangent, "seq", swap)
    w_in_other = lax.ppermute(w_in, "seq", swap)
    w_out_other = lax.ppermute(w_out, "seq", swap)

    sum_rows = padded(3 * half // LANES + 1, 16)
    message, logits, comb_prob, keys_all = call(
        sums_kernel,
        (
            shape((devices, sum_rows, LANES), bf16),
            shape((slots, 2 * own), f32),
            shape((slots, 2 * own), f32),
            shape((slots, width), bf16),
        ),
        [
            pltpu.VMEM(tokens.shape, bf16),
            pltpu.VMEM(cotangent.shape, bf16),
            pltpu.VMEM((slots, key_rows, LANES), f32),
            pltpu.VMEM((slots, sum_rows, LANES), f32),
            pltpu.SemaphoreType.DMA((2,)),
        ],
        [keys, tokens_other, cotangent_other, tokens, cotangent],
        unplaced=2,
        room=(64 * 1024 - 11300) * 1024,
    )
    parts = lax.all_to_all(message, both, 0, 0, tiled=True)

    row_count = padded(2 * width // LANES + 1, 8)
    message, slot_in, slot_out_grad, hidden_rows = call(
        functools.partial(expert_kernel, exp_size),
        (
            shape((devices, row_count, LANES), bf16),
            shape((1, width), bf16),
            shape((1, width), bf16),
            shape((2, hidden), bf16),
        ),
        [pltpu.VMEM((devices, sum_rows, LANES), f32), pltpu.VMEM((row_count, LANES), f32)],
        [parts, w_in_other[0], w_out_other[0]],
    )
    gathered = lax.all_to_all(message, both, 0, 0, tiled=True)
    own_rows = lax.ppermute(hidden_rows, "seq", swap)
    activation, pre_grad = own_rows[:1], own_rows[1:]
    w_out_grad = (
        activation.astype(f32)[:, :, None] * slot_out_grad.astype(f32)[:, None, :]
    ).astype(bf16)
    w_in_grad = (pre_grad.astype(f32)[:, :, None] * slot_in.astype(f32)[:, None, :]).astype(bf16)

    message, slot_out, slot_in_grad, dispatch, logit_grad = call(
        grads_kernel,
        (
            shape((devices, 1, half), f32),
            shape((slots, width), bf16),
            shape((slots, width), bf16),
            shape((slots, own), bf16),
            shape((slots, own), bf16),
        ),
        [pltpu.VMEM((devices, row_count, LANES), f32)],
        [gathered, logits, comb_prob, tokens, tokens_other, cotangent, cotangent_other],
    )
    keys_parts = lax.all_to_all(message, both, 0, 0, tiled=True)
    layer_out = dot(comb_prob[:, :own].astype(bf16), slot_out, 0, 0).astype(bf16)
    tokens_grad = (dot(dispatch, slot_in_grad, 0, 0) + dot(logit_grad, keys_all, 0, 0)).astype(bf16)
    keys_parts = keys_parts.reshape(seq_size // 2, 2, exp_size, half)
    keys_grad = jnp.sum(keys_parts, axis=(0, 2)).reshape(1, width).T
    return (layer_out, tokens_grad, keys_grad, w_in_grad, w_out_grad)


def solution(mesh):
    return jax.shard_map(
        local,
        mesh=mesh,
        in_specs=(
            P(("seq", "exp"), None),
            P(None, "exp"),
            P("exp", "seq", None),
            P("exp", "seq", None),
            P(("seq", "exp"), None),
        ),
        out_specs=(
            P(("seq", "exp"), None),
            P(("seq", "exp"), None),
            P(None, "exp"),
            P("exp", "seq", None),
            P("exp", "seq", None),
        ),
        check_vma=False,
    )
```

```python
import functools

import jax
import jax.numpy as jnp
from jax import lax
from jax.experimental import pallas as pl
from jax.experimental.pallas import tpu as pltpu
from jax.sharding import PartitionSpec as P

tanh_coeff = 0.7978845608028654
cubic_coeff = 0.044715
LANES = 128
VECTOR_SHARE = 0.65


def dot(left, right, left_dim, right_dim):
    return lax.dot_general(
        left, right, (((left_dim,), (right_dim,)), ((), ())), preferred_element_type=jnp.float32
    )


def gelu_parts(values):
    tanh_part = jnp.tanh(tanh_coeff * (values + cubic_coeff * values * values * values))
    value = 0.5 * values * (1.0 + tanh_part)
    slope = 0.5 * (1.0 + tanh_part) + 0.5 * values * (1.0 - tanh_part * tanh_part) * tanh_coeff * (
        1.0 + 3.0 * cubic_coeff * values * values
    )
    return value, slope


def padded(rows, multiple):
    return -(-rows // multiple) * multiple


def bf16_terms(values, count):
    terms = []
    for _ in range(count):
        term = values.astype(jnp.bfloat16).astype(jnp.float32)
        terms.append(term)
        values = values - term
    return terms


def in_lanes(columns, lane):
    row = jnp.zeros((columns[0].shape[0], LANES), jnp.float32)
    for i, column in enumerate(columns):
        row = jnp.where(lane == i, column, row)
    return row


def from_lanes(row, lane, first, count):
    keep = (lane >= first) & (lane < first + count)
    return jnp.sum(jnp.where(keep, row, 0.0), axis=1, keepdims=True)


def lanes_of(rows):
    return lax.broadcasted_iota(jnp.int32, (rows, LANES), 1)


def call(kernel, out_shape, scratch_shapes, inputs, unplaced=0, room=24 * 1024 * 1024):
    spaces = [pltpu.VMEM] * (len(inputs) - unplaced) + [pltpu.HBM] * unplaced
    return pl.pallas_call(
        kernel,
        out_shape=out_shape,
        in_specs=[pl.BlockSpec(memory_space=space) for space in spaces],
        out_specs=jax.tree.map(lambda _: pl.BlockSpec(memory_space=pltpu.VMEM), out_shape),
        scratch_shapes=scratch_shapes,
        compiler_params=pltpu.CompilerParams(vmem_limit_bytes=room),
    )(*inputs)


def keys_kernel(key_ref, out_ref, rows_ref):
    width = key_ref.shape[1]
    rows_ref[...] = jnp.zeros_like(rows_ref)
    key = key_ref[...].astype(jnp.float32)
    for j in range(width // LANES):
        rows_ref[j : j + 1, :] = key[:, j * LANES : (j + 1) * LANES]
    block = rows_ref[...].astype(jnp.bfloat16)
    for i in range(out_ref.shape[0]):
        out_ref[i] = block


def sums_kernel(
    keys_ref, tokens_other_ref, cotangent_other_ref, tokens_far_ref, cotangent_far_ref,
    message_ref, logits_ref, comb_ref, keys_all_ref,
    tokens_ref, cotangent_ref, keys_rows_ref, rows_ref, sems,
):
    tokens_copy = pltpu.make_async_copy(tokens_far_ref, tokens_ref, sems.at[0])
    cotangent_copy = pltpu.make_async_copy(cotangent_far_ref, cotangent_ref, sems.at[1])
    tokens_copy.start()
    cotangent_copy.start()
    slots = keys_ref.shape[0]
    width = tokens_ref.shape[1]
    half = width // 2
    chunks = half // LANES
    first = pl.multiple_of(lax.rem(lax.axis_index("seq"), 2) * half, LANES)

    keys_rows_ref[...] = keys_ref[...].astype(jnp.float32)
    keys = jnp.concatenate(
        [keys_rows_ref[:, j, :] for j in range(width // LANES)], axis=1
    ).astype(jnp.bfloat16)
    keys_all_ref[...] = keys
    other_logits = dot(keys, tokens_other_ref[...], 1, 1)
    tokens_copy.wait()
    logits = jnp.concatenate([dot(keys, tokens_ref[...], 1, 1), other_logits], axis=1)
    logits_ref[...] = logits
    own = tokens_ref.shape[0]

    row_terms = jnp.exp(logits - jnp.max(logits, axis=0, keepdims=True))
    comb_prob = row_terms / jnp.sum(row_terms, axis=0, keepdims=True)
    comb_ref[...] = comb_prob
    combine = comb_prob.astype(jnp.bfloat16)
    cotangent_copy.wait()
    grad_sums = dot(combine[:, :own], cotangent_ref[:, pl.ds(first, half)], 1, 0) + dot(
        combine[:, own:], cotangent_other_ref[:, pl.ds(first, half)], 1, 0
    )

    peak = jnp.max(logits, axis=1, keepdims=True)
    terms = jnp.exp(logits - peak)
    total = jnp.sum(terms, axis=1, keepdims=True)
    parts = jnp.concatenate(bf16_terms(terms, 2), axis=0).astype(jnp.bfloat16)
    sums = dot(parts[:, :own], tokens_ref[:, pl.ds(first, half)], 1, 0) + dot(
        parts[:, own:], tokens_other_ref[:, pl.ds(first, half)], 1, 0
    )
    high, low = bf16_terms(sums[:slots] + sums[slots:], 2)
    for j in range(chunks):
        columns = slice(j * LANES, (j + 1) * LANES)
        rows_ref[:, j, :] = high[:, columns]
        rows_ref[:, chunks + j, :] = low[:, columns]
        rows_ref[:, 2 * chunks + j, :] = grad_sums[:, columns]
    stats = in_lanes(bf16_terms(peak, 3) + bf16_terms(total, 3), lanes_of(slots))
    rows_ref[:, 3 * chunks, :] = stats
    for j in range(3 * chunks + 1, rows_ref.shape[1]):
        rows_ref[:, j, :] = jnp.zeros_like(stats)
    block = rows_ref[...].astype(jnp.bfloat16)
    for q in range(message_ref.shape[0] // slots):
        message_ref[q * slots : (q + 1) * slots] = block


def lane_sums_times(row, w_ref, first, count):
    row_chunks = [
        row[:, j * LANES : (j + 1) * LANES].astype(jnp.float32) for j in range(row.shape[1] // LANES)
    ]
    highs, lows = [], []
    for start in range(first, first + count, 16):
        total = None
        for j, chunk in enumerate(row_chunks):
            term = w_ref[start : start + 16, j * LANES : (j + 1) * LANES].astype(jnp.float32) * chunk
            total = term if total is None else total + term
        high = total.astype(jnp.bfloat16)
        highs.append(high)
        lows.append((total - high.astype(jnp.float32)).astype(jnp.bfloat16))
    ones = jnp.ones((8, LANES), jnp.bfloat16)
    sums = dot(ones, jnp.concatenate(highs, axis=0), 1, 1) + dot(ones, jnp.concatenate(lows, axis=0), 1, 1)
    return sums[:1]


def rows_times(pairs):
    results, taken = [], 0
    for row, w_ref in pairs:
        rows = w_ref.shape[0]
        block = LANES if rows % LANES == 0 else rows
        outs = []
        for first in range(0, rows, block):
            taken += VECTOR_SHARE
            if taken >= 1.0 and block == LANES:
                taken -= 1.0
                outs.append(lane_sums_times(row, w_ref, first, block))
            else:
                outs.append(dot(row, w_ref[first : first + block, :], 1, 1))
        results.append(jnp.concatenate(outs, axis=1))
    return results


def expert_kernel(
    exp_size, parts_ref, w_in_ref, w_out_ref,
    message_ref, slot_in_ref, slot_out_grad_ref, hidden_rows_ref, parts_rows_ref, rows_ref,
):
    devices = parts_ref.shape[0]
    seq_size = devices // exp_size
    width = w_in_ref.shape[1]
    chunks = width // LANES
    per_side = chunks // 2
    parts_rows_ref[...] = parts_ref[...].astype(jnp.float32)
    stats = parts_rows_ref[:, 3 * per_side, :]
    lane = lanes_of(devices)
    peaks = from_lanes(stats, lane, 0, 3)
    totals = from_lanes(stats, lane, 3, 3)
    slot_peak = jnp.max(peaks, axis=0, keepdims=True)
    scale = jnp.exp(peaks - slot_peak)

    def of_side(values, side):
        total = values[side * exp_size : (side + 1) * exp_size]
        for q in range(side + 2, seq_size, 2):
            total = total + values[q * exp_size : (q + 1) * exp_size]
        return jnp.sum(total, axis=0, keepdims=True)

    slot_total = of_side(totals * scale, 0)
    slot_chunks, grad_chunks = [[], []], [[], []]
    for j in range(per_side):
        weighted = (parts_rows_ref[:, j, :] + parts_rows_ref[:, per_side + j, :]) * scale
        grads = parts_rows_ref[:, 2 * per_side + j, :]
        for side in range(2):
            slot_chunks[side].append(of_side(weighted, side))
            grad_chunks[side].append(of_side(grads, side))
    slot_row = jnp.concatenate(slot_chunks[0] + slot_chunks[1], axis=1) / slot_total
    slot_in = slot_row.astype(jnp.bfloat16)
    slot_out_grad = jnp.concatenate(grad_chunks[0] + grad_chunks[1], axis=1).astype(jnp.bfloat16)
    slot_in_ref[...] = slot_in
    slot_out_grad_ref[...] = slot_out_grad

    pre_act, act_grad = rows_times([(slot_in, w_in_ref), (slot_out_grad, w_out_ref)])
    value, slope = gelu_parts(pre_act)
    activation = value.astype(jnp.bfloat16)
    pre_grad = (act_grad * slope).astype(jnp.bfloat16)
    hidden_rows_ref[...] = jnp.concatenate([value, act_grad * slope], axis=0).astype(jnp.bfloat16)
    out_part = dot(activation, w_out_ref[...], 1, 0)
    grad_part = dot(pre_grad, w_in_ref[...], 1, 0).astype(jnp.bfloat16).astype(jnp.float32)
    correction = jnp.sum(slot_row * grad_part, axis=1, keepdims=True)
    for j in range(chunks):
        columns = slice(j * LANES, (j + 1) * LANES)
        rows_ref[j : j + 1, :] = out_part[:, columns]
        rows_ref[chunks + j : chunks + j + 1, :] = grad_part[:, columns]
    stats = in_lanes(
        bf16_terms(slot_peak, 3) + bf16_terms(slot_total, 3) + bf16_terms(correction, 3), lanes_of(1)
    )
    rows_ref[2 * chunks : 2 * chunks + 1, :] = stats
    for j in range(2 * chunks + 1, rows_ref.shape[0]):
        rows_ref[j : j + 1, :] = jnp.zeros_like(stats)
    block = rows_ref[...].astype(jnp.bfloat16)
    for i in range(devices):
        message_ref[i] = block


def grads_kernel(
    parts_ref, logits_ref, comb_ref, tokens_ref, tokens_other_ref, cotangent_ref, cotangent_other_ref,
    message_ref, slot_out_ref, slot_in_grad_ref, dispatch_ref, logit_grad_ref, parts_rows_ref,
):
    devices = parts_ref.shape[0]
    slots, _ = logits_ref.shape
    seq_size = devices // slots
    own, width = tokens_ref.shape
    half = width // 2
    chunks = width // LANES
    first = pl.multiple_of(lax.rem(lax.axis_index("seq"), 2) * half, LANES)
    parts_rows_ref[...] = parts_ref[...].astype(jnp.float32)
    out_rows = jnp.concatenate([parts_rows_ref[:, j, :] for j in range(chunks)], axis=1)
    grad_rows = jnp.concatenate([parts_rows_ref[:, chunks + j, :] for j in range(chunks)], axis=1)
    stats = parts_rows_ref[:, 2 * chunks, :]
    lane = lanes_of(slots)

    def over_seq(values):
        total = values[:slots]
        for q in range(1, seq_size):
            total = total + values[q * slots : (q + 1) * slots]
        return total

    peak = from_lanes(stats[:slots], lane, 0, 3)
    total = from_lanes(stats[:slots], lane, 3, 3)
    correction = from_lanes(over_seq(stats), lane, 6, 3)
    slot_out_ref[...] = over_seq(out_rows).astype(jnp.bfloat16)
    slot_in_grad_ref[...] = over_seq(grad_rows).astype(jnp.bfloat16)
    out_rows = out_rows.astype(jnp.bfloat16)
    grad_rows = grad_rows.astype(jnp.bfloat16)
    comb_grad = over_seq(
        jnp.concatenate(
            [dot(out_rows, cotangent_ref[...], 1, 1), dot(out_rows, cotangent_other_ref[...], 1, 1)], axis=1
        )
    )
    disp_grad = over_seq(
        jnp.concatenate(
            [dot(grad_rows, tokens_ref[...], 1, 1), dot(grad_rows, tokens_other_ref[...], 1, 1)], axis=1
        )
    )
    comb_prob = comb_ref[...]
    disp_prob = jnp.exp(logits_ref[...] - peak) / total
    comb_mean = jnp.sum(comb_prob * comb_grad, axis=0, keepdims=True)
    logit_grad = (
        comb_prob * (comb_grad - comb_mean) + disp_prob * (disp_grad - correction)
    ).astype(jnp.bfloat16)
    dispatch_ref[...] = disp_prob[:, :own].astype(jnp.bfloat16)
    logit_grad_ref[...] = logit_grad[:, :own]
    keys_part = dot(logit_grad[:, :own], tokens_ref[:, pl.ds(first, half)], 1, 0) + dot(
        logit_grad[:, own:], tokens_other_ref[:, pl.ds(first, half)], 1, 0
    )
    for s in range(slots):
        for q in range(seq_size):
            message_ref[q * slots + s] = keys_part[s : s + 1]


def local(tokens, slot_keys, w_in, w_out, cotangent):
    both = ("seq", "exp")
    seq_size, exp_size = lax.axis_size("seq"), lax.axis_size("exp")
    devices = seq_size * exp_size
    experts, hidden, width = w_in.shape
    assert experts == 1 and seq_size % 2 == 0
    slots = exp_size
    half = width // 2
    own = tokens.shape[0]
    swap = [(i, i ^ 1) for i in range(seq_size)]
    f32, bf16 = jnp.float32, jnp.bfloat16
    shape = jax.ShapeDtypeStruct

    key_rows = padded(width // LANES, 16)
    key_message = call(
        keys_kernel,
        shape((exp_size, key_rows, LANES), bf16),
        [pltpu.VMEM((key_rows, LANES), f32)],
        [slot_keys.T],
    )
    tokens_other = lax.ppermute(tokens, "seq", swap)
    cotangent_other = lax.ppermute(cotangent, "seq", swap)
    keys = lax.all_to_all(key_message, "exp", 0, 0, tiled=True)
    keys, w_in_late, w_out_late, tokens_other, cotangent_other = lax.optimization_barrier((keys, w_in, w_out, tokens_other, cotangent_other))
    w_in_other = lax.ppermute(w_in_late, "seq", swap)
    w_out_other = lax.ppermute(w_out_late, "seq", swap)

    sum_rows = padded(3 * half // LANES + 1, 16)
    message, logits, comb_prob, keys_all = call(
        sums_kernel,
        (
            shape((devices, sum_rows, LANES), bf16),
            shape((slots, 2 * own), f32),
            shape((slots, 2 * own), f32),
            shape((slots, width), bf16),
        ),
        [
            pltpu.VMEM(tokens.shape, bf16),
            pltpu.VMEM(cotangent.shape, bf16),
            pltpu.VMEM((slots, key_rows, LANES), f32),
            pltpu.VMEM((slots, sum_rows, LANES), f32),
            pltpu.SemaphoreType.DMA((2,)),
        ],
        [keys, tokens_other, cotangent_other, tokens, cotangent],
        unplaced=2,
        room=(64 * 1024 - 11300) * 1024,
    )
    parts = lax.all_to_all(message, both, 0, 0, tiled=True)

    row_count = padded(2 * width // LANES + 1, 8)
    message, slot_in, slot_out_grad, hidden_rows = call(
        functools.partial(expert_kernel, exp_size),
        (
            shape((devices, row_count, LANES), bf16),
            shape((1, width), bf16),
            shape((1, width), bf16),
            shape((2, hidden), bf16),
        ),
        [pltpu.VMEM((devices, sum_rows, LANES), f32), pltpu.VMEM((row_count, LANES), f32)],
        [parts, w_in_other[0], w_out_other[0]],
    )
    gathered = lax.all_to_all(message, both, 0, 0, tiled=True)
    own_rows = lax.ppermute(hidden_rows, "seq", swap)
    activation, pre_grad = own_rows[:1], own_rows[1:]
    w_out_grad = (
        activation.astype(f32)[:, :, None] * slot_out_grad.astype(f32)[:, None, :]
    ).astype(bf16)
    w_in_grad = (pre_grad.astype(f32)[:, :, None] * slot_in.astype(f32)[:, None, :]).astype(bf16)

    message, slot_out, slot_in_grad, dispatch, logit_grad = call(
        grads_kernel,
        (
            shape((devices, 1, half), f32),
            shape((slots, width), bf16),
            shape((slots, width), bf16),
            shape((slots, own), bf16),
            shape((slots, own), bf16),
        ),
        [pltpu.VMEM((devices, row_count, LANES), f32)],
        [gathered, logits, comb_prob, tokens, tokens_other, cotangent, cotangent_other],
    )
    keys_parts = lax.all_to_all(message, both, 0, 0, tiled=True)
    layer_out = dot(comb_prob[:, :own].astype(bf16), slot_out, 0, 0).astype(bf16)
    tokens_grad = (dot(dispatch, slot_in_grad, 0, 0) + dot(logit_grad, keys_all, 0, 0)).astype(bf16)
    keys_parts = keys_parts.reshape(seq_size // 2, 2, exp_size, half)
    keys_grad = jnp.sum(keys_parts, axis=(0, 2)).reshape(1, width).T
    return (layer_out, tokens_grad, keys_grad, w_in_grad, w_out_grad)


def solution(mesh):
    return jax.shard_map(
        local,
        mesh=mesh,
        in_specs=(
            P(("seq", "exp"), None),
            P(None, "exp"),
            P("exp", "seq", None),
            P("exp", "seq", None),
            P(("seq", "exp"), None),
        ),
        out_specs=(
            P(("seq", "exp"), None),
            P(("seq", "exp"), None),
            P(None, "exp"),
            P("exp", "seq", None),
            P("exp", "seq", None),
        ),
        check_vma=False,
    )
```

```python
import functools

import jax
import jax.numpy as jnp
from jax import lax
from jax.experimental import pallas as pl
from jax.experimental.pallas import tpu as pltpu
from jax.sharding import PartitionSpec as P

tanh_coeff = 0.7978845608028654
cubic_coeff = 0.044715
LANES = 128
VECTOR_SHARE = 0.65


def dot(left, right, left_dim, right_dim):
    return lax.dot_general(
        left, right, (((left_dim,), (right_dim,)), ((), ())), preferred_element_type=jnp.float32
    )


def gelu_parts(values):
    tanh_part = jnp.tanh(tanh_coeff * (values + cubic_coeff * values * values * values))
    value = 0.5 * values * (1.0 + tanh_part)
    slope = 0.5 * (1.0 + tanh_part) + 0.5 * values * (1.0 - tanh_part * tanh_part) * tanh_coeff * (
        1.0 + 3.0 * cubic_coeff * values * values
    )
    return value, slope


def padded(rows, multiple):
    return -(-rows // multiple) * multiple


def bf16_terms(values, count):
    terms = []
    for _ in range(count):
        term = values.astype(jnp.bfloat16).astype(jnp.float32)
        terms.append(term)
        values = values - term
    return terms


def in_lanes(columns, lane):
    row = jnp.zeros((columns[0].shape[0], LANES), jnp.float32)
    for i, column in enumerate(columns):
        row = jnp.where(lane == i, column, row)
    return row


def from_lanes(row, lane, first, count):
    keep = (lane >= first) & (lane < first + count)
    return jnp.sum(jnp.where(keep, row, 0.0), axis=1, keepdims=True)


def lanes_of(rows):
    return lax.broadcasted_iota(jnp.int32, (rows, LANES), 1)


def call(kernel, out_shape, scratch_shapes, inputs, far=0, far_out=0):
    near = len(inputs) - far
    spaces = [pltpu.VMEM] * near + [pltpu.HBM] * far
    inputs = inputs[:near] + [pltpu.with_memory_space_constraint(x, pltpu.HBM) for x in inputs[near:]]
    outs = len(out_shape)
    out_spaces = [pltpu.VMEM] * (outs - far_out) + [pltpu.HBM] * far_out
    return pl.pallas_call(
        kernel,
        out_shape=out_shape,
        in_specs=[pl.BlockSpec(memory_space=space) for space in spaces],
        out_specs=tuple(pl.BlockSpec(memory_space=space) for space in out_spaces),
        scratch_shapes=scratch_shapes,
        compiler_params=pltpu.CompilerParams(vmem_limit_bytes=24 * 1024 * 1024),
    )(*inputs)


def keys_kernel(
    key_in_ref, tokens_in_ref, cotangent_in_ref, out_ref, tokens_ref, cotangent_ref, key_ref, rows_ref, sems
):
    copies = [
        pltpu.make_async_copy(source, target, sems.at[i])
        for i, (source, target) in enumerate(
            [(key_in_ref, key_ref), (tokens_in_ref, tokens_ref), (cotangent_in_ref, cotangent_ref)]
        )
    ]
    for copy in copies:
        copy.start()
    width = key_ref.shape[1]
    copies[0].wait()
    rows_ref[...] = jnp.zeros_like(rows_ref)
    key = key_ref[...].astype(jnp.float32)
    for j in range(width // LANES):
        rows_ref[j : j + 1, :] = key[:, j * LANES : (j + 1) * LANES]
    block = rows_ref[...].astype(jnp.bfloat16)
    for i in range(out_ref.shape[0]):
        out_ref[i] = block
    copies[1].wait()
    copies[2].wait()


def sums_kernel(
    keys_ref, tokens_ref, tokens_other_ref, cotangent_ref, cotangent_other_ref,
    message_ref, logits_ref, comb_ref, keys_all_ref, keys_rows_ref, rows_ref,
):
    slots = keys_ref.shape[0]
    width = tokens_ref.shape[1]
    half = width // 2
    chunks = half // LANES
    first = pl.multiple_of(lax.rem(lax.axis_index("seq"), 2) * half, LANES)

    keys_rows_ref[...] = keys_ref[...].astype(jnp.float32)
    keys = jnp.concatenate(
        [keys_rows_ref[:, j, :] for j in range(width // LANES)], axis=1
    ).astype(jnp.bfloat16)
    keys_all_ref[...] = keys
    other_logits = dot(keys, tokens_other_ref[...], 1, 1)
    logits = jnp.concatenate([dot(keys, tokens_ref[...], 1, 1), other_logits], axis=1)
    logits_ref[...] = logits
    own = tokens_ref.shape[0]

    row_terms = jnp.exp(logits - jnp.max(logits, axis=0, keepdims=True))
    comb_prob = row_terms / jnp.sum(row_terms, axis=0, keepdims=True)
    comb_ref[...] = comb_prob
    combine = comb_prob.astype(jnp.bfloat16)
    grad_sums = dot(combine[:, :own], cotangent_ref[:, pl.ds(first, half)], 1, 0) + dot(
        combine[:, own:], cotangent_other_ref[:, pl.ds(first, half)], 1, 0
    )

    peak = jnp.max(logits, axis=1, keepdims=True)
    terms = jnp.exp(logits - peak)
    total = jnp.sum(terms, axis=1, keepdims=True)
    parts = jnp.concatenate(bf16_terms(terms, 2), axis=0).astype(jnp.bfloat16)
    sums = dot(parts[:, :own], tokens_ref[:, pl.ds(first, half)], 1, 0) + dot(
        parts[:, own:], tokens_other_ref[:, pl.ds(first, half)], 1, 0
    )
    high, low = bf16_terms(sums[:slots] + sums[slots:], 2)
    for j in range(chunks):
        columns = slice(j * LANES, (j + 1) * LANES)
        rows_ref[:, j, :] = high[:, columns]
        rows_ref[:, chunks + j, :] = low[:, columns]
        rows_ref[:, 2 * chunks + j, :] = grad_sums[:, columns]
    stats = in_lanes(bf16_terms(peak, 3) + bf16_terms(total, 3), lanes_of(slots))
    rows_ref[:, 3 * chunks, :] = stats
    for j in range(3 * chunks + 1, rows_ref.shape[1]):
        rows_ref[:, j, :] = jnp.zeros_like(stats)
    block = rows_ref[...].astype(jnp.bfloat16)
    for q in range(message_ref.shape[0] // slots):
        message_ref[q * slots : (q + 1) * slots] = block


def lane_sums_times(row, w_ref, first, count):
    row_chunks = [
        row[:, j * LANES : (j + 1) * LANES].astype(jnp.float32) for j in range(row.shape[1] // LANES)
    ]
    highs, lows = [], []
    for start in range(first, first + count, 16):
        total = None
        for j, chunk in enumerate(row_chunks):
            term = w_ref[start : start + 16, j * LANES : (j + 1) * LANES].astype(jnp.float32) * chunk
            total = term if total is None else total + term
        high = total.astype(jnp.bfloat16)
        highs.append(high)
        lows.append((total - high.astype(jnp.float32)).astype(jnp.bfloat16))
    ones = jnp.ones((8, LANES), jnp.bfloat16)
    sums = dot(ones, jnp.concatenate(highs, axis=0), 1, 1) + dot(ones, jnp.concatenate(lows, axis=0), 1, 1)
    return sums[:1]


def rows_times(pairs):
    results, taken = [], 0
    for row, w_ref in pairs:
        rows = w_ref.shape[0]
        block = LANES if rows % LANES == 0 else rows
        outs = []
        for first in range(0, rows, block):
            taken += VECTOR_SHARE
            if taken >= 1.0 and block == LANES:
                taken -= 1.0
                outs.append(lane_sums_times(row, w_ref, first, block))
            else:
                outs.append(dot(row, w_ref[first : first + block, :], 1, 1))
        results.append(jnp.concatenate(outs, axis=1))
    return results


def expert_kernel(
    exp_size, parts_ref, w_in_ref, w_out_ref,
    message_ref, slot_in_ref, slot_out_grad_ref, hidden_rows_ref, parts_rows_ref, rows_ref,
):
    devices = parts_ref.shape[0]
    seq_size = devices // exp_size
    width = w_in_ref.shape[1]
    chunks = width // LANES
    per_side = chunks // 2
    parts_rows_ref[...] = parts_ref[...].astype(jnp.float32)
    stats = parts_rows_ref[:, 3 * per_side, :]
    lane = lanes_of(devices)
    peaks = from_lanes(stats, lane, 0, 3)
    totals = from_lanes(stats, lane, 3, 3)
    slot_peak = jnp.max(peaks, axis=0, keepdims=True)
    scale = jnp.exp(peaks - slot_peak)

    def of_side(values, side):
        total = values[side * exp_size : (side + 1) * exp_size]
        for q in range(side + 2, seq_size, 2):
            total = total + values[q * exp_size : (q + 1) * exp_size]
        return jnp.sum(total, axis=0, keepdims=True)

    slot_total = of_side(totals * scale, 0)
    slot_chunks, grad_chunks = [[], []], [[], []]
    for j in range(per_side):
        weighted = (parts_rows_ref[:, j, :] + parts_rows_ref[:, per_side + j, :]) * scale
        grads = parts_rows_ref[:, 2 * per_side + j, :]
        for side in range(2):
            slot_chunks[side].append(of_side(weighted, side))
            grad_chunks[side].append(of_side(grads, side))
    slot_row = jnp.concatenate(slot_chunks[0] + slot_chunks[1], axis=1) / slot_total
    slot_in = slot_row.astype(jnp.bfloat16)
    slot_out_grad = jnp.concatenate(grad_chunks[0] + grad_chunks[1], axis=1).astype(jnp.bfloat16)
    slot_in_ref[...] = slot_in
    slot_out_grad_ref[...] = slot_out_grad

    pre_act, act_grad = rows_times([(slot_in, w_in_ref), (slot_out_grad, w_out_ref)])
    value, slope = gelu_parts(pre_act)
    activation = value.astype(jnp.bfloat16)
    pre_grad = (act_grad * slope).astype(jnp.bfloat16)
    hidden_rows_ref[...] = jnp.concatenate([value, act_grad * slope], axis=0).astype(jnp.bfloat16)
    out_part = dot(activation, w_out_ref[...], 1, 0)
    grad_part = dot(pre_grad, w_in_ref[...], 1, 0).astype(jnp.bfloat16).astype(jnp.float32)
    correction = jnp.sum(slot_row * grad_part, axis=1, keepdims=True)
    for j in range(chunks):
        columns = slice(j * LANES, (j + 1) * LANES)
        rows_ref[j : j + 1, :] = out_part[:, columns]
        rows_ref[chunks + j : chunks + j + 1, :] = grad_part[:, columns]
    stats = in_lanes(
        bf16_terms(slot_peak, 3) + bf16_terms(slot_total, 3) + bf16_terms(correction, 3), lanes_of(1)
    )
    rows_ref[2 * chunks : 2 * chunks + 1, :] = stats
    for j in range(2 * chunks + 1, rows_ref.shape[0]):
        rows_ref[j : j + 1, :] = jnp.zeros_like(stats)
    block = rows_ref[...].astype(jnp.bfloat16)
    for i in range(devices):
        message_ref[i] = block


def grads_kernel(
    parts_ref, logits_ref, comb_ref, tokens_ref, tokens_other_ref, cotangent_ref, cotangent_other_ref,
    message_ref, slot_out_ref, slot_in_grad_ref, factors_ref, parts_rows_ref,
):
    devices = parts_ref.shape[0]
    slots, _ = logits_ref.shape
    seq_size = devices // slots
    own, width = tokens_ref.shape
    half = width // 2
    chunks = width // LANES
    first = pl.multiple_of(lax.rem(lax.axis_index("seq"), 2) * half, LANES)
    parts_rows_ref[...] = parts_ref[...].astype(jnp.float32)
    out_rows = jnp.concatenate([parts_rows_ref[:, j, :] for j in range(chunks)], axis=1)
    grad_rows = jnp.concatenate([parts_rows_ref[:, chunks + j, :] for j in range(chunks)], axis=1)
    stats = parts_rows_ref[:, 2 * chunks, :]
    lane = lanes_of(slots)

    def over_seq(values):
        total = values[:slots]
        for q in range(1, seq_size):
            total = total + values[q * slots : (q + 1) * slots]
        return total

    peak = from_lanes(stats[:slots], lane, 0, 3)
    total = from_lanes(stats[:slots], lane, 3, 3)
    correction = from_lanes(over_seq(stats), lane, 6, 3)
    slot_out_ref[...] = over_seq(out_rows).astype(jnp.bfloat16)
    slot_in_grad_ref[...] = over_seq(grad_rows).astype(jnp.bfloat16)
    out_rows = out_rows.astype(jnp.bfloat16)
    grad_rows = grad_rows.astype(jnp.bfloat16)
    comb_grad = over_seq(
        jnp.concatenate(
            [dot(out_rows, cotangent_ref[...], 1, 1), dot(out_rows, cotangent_other_ref[...], 1, 1)], axis=1
        )
    )
    disp_grad = over_seq(
        jnp.concatenate(
            [dot(grad_rows, tokens_ref[...], 1, 1), dot(grad_rows, tokens_other_ref[...], 1, 1)], axis=1
        )
    )
    comb_prob = comb_ref[...]
    disp_prob = jnp.exp(logits_ref[...] - peak) / total
    comb_mean = jnp.sum(comb_prob * comb_grad, axis=0, keepdims=True)
    logit_grad = (
        comb_prob * (comb_grad - comb_mean) + disp_prob * (disp_grad - correction)
    ).astype(jnp.bfloat16)
    factors = [comb_prob[:, :own], disp_prob[:, :own], logit_grad[:, :own]]
    for i, factor in enumerate(factors):
        factors_ref[i * slots : (i + 1) * slots] = factor.astype(jnp.bfloat16).astype(jnp.float32)
    keys_part = dot(logit_grad[:, :own], tokens_ref[:, pl.ds(first, half)], 1, 0) + dot(
        logit_grad[:, own:], tokens_other_ref[:, pl.ds(first, half)], 1, 0
    )
    for s in range(slots):
        for q in range(seq_size):
            message_ref[q * slots + s] = keys_part[s : s + 1]


def block_of(rows):
    return 128 if rows % 128 == 0 else rows


def weight_grads_kernel(hidden_rows_ref, slot_in_ref, slot_out_grad_ref, w_in_grad_ref, w_out_grad_ref, near_ref, sems):
    hidden = near_ref.shape[1]
    block = block_of(hidden)
    hidden_rows = hidden_rows_ref[...].astype(jnp.float32)
    copies = []
    for w, (hidden_index, row_ref, far_ref) in enumerate(
        [(0, slot_out_grad_ref, w_out_grad_ref), (1, slot_in_ref, w_in_grad_ref)]
    ):
        row = row_ref[...].astype(jnp.float32)
        for i in range(hidden // block):
            rows = pl.ds(i * block, block)
            part = hidden_rows[hidden_index : hidden_index + 1, i * block : (i + 1) * block]
            column = jnp.transpose(jnp.broadcast_to(part, (8, block)))[:, :1]
            near_ref[w, rows, :] = (column * row).astype(jnp.bfloat16)
            copy = pltpu.make_async_copy(near_ref.at[w, rows], far_ref.at[0, rows], sems.at[w, i])
            copy.start()
            copies.append(copy)
    for copy in copies:
        copy.wait()


def outputs_kernel(factors_ref, slot_out_ref, slot_in_grad_ref, keys_ref, layer_out_ref, tokens_grad_ref):
    slots = slot_out_ref.shape[0]
    combine = jnp.transpose(factors_ref[:slots, :]).astype(jnp.bfloat16)
    layer_out_ref[...] = dot(combine, slot_out_ref[...], 1, 0).astype(jnp.bfloat16)
    others = jnp.transpose(factors_ref[slots:, :]).astype(jnp.bfloat16)
    rows = jnp.concatenate(
        [slot_in_grad_ref[...].astype(jnp.float32), keys_ref[...].astype(jnp.float32)], axis=0
    ).astype(jnp.bfloat16)
    tokens_grad_ref[...] = dot(others, rows, 1, 0).astype(jnp.bfloat16)


def local(tokens, slot_keys, w_in, w_out, cotangent):
    both = ("seq", "exp")
    seq_size, exp_size = lax.axis_size("seq"), lax.axis_size("exp")
    devices = seq_size * exp_size
    experts, hidden, width = w_in.shape
    assert experts == 1 and seq_size % 2 == 0
    slots = exp_size
    half = width // 2
    own = tokens.shape[0]
    swap = [(i, i ^ 1) for i in range(seq_size)]
    f32, bf16 = jnp.float32, jnp.bfloat16
    shape = jax.ShapeDtypeStruct

    key_rows = padded(width // LANES, 16)
    key_message, tokens_near, cotangent_near = call(
        keys_kernel,
        (
            shape((exp_size, key_rows, LANES), bf16),
            shape(tokens.shape, bf16),
            shape(cotangent.shape, bf16),
        ),
        [pltpu.VMEM((1, width), bf16), pltpu.VMEM((key_rows, LANES), f32), pltpu.SemaphoreType.DMA((3,))],
        [slot_keys.T, tokens, cotangent],
        far=3,
    )
    tokens_other = lax.ppermute(tokens, "seq", swap)
    cotangent_other = lax.ppermute(cotangent, "seq", swap)
    keys = lax.all_to_all(key_message, "exp", 0, 0, tiled=True)
    keys, w_in_late, w_out_late, tokens_other, cotangent_other = lax.optimization_barrier((keys, w_in, w_out, tokens_other, cotangent_other))
    w_in_other = lax.ppermute(w_in_late, "seq", swap)
    w_out_other = lax.ppermute(w_out_late, "seq", swap)

    sum_rows = padded(3 * half // LANES + 1, 16)
    message, logits, comb_prob, keys_all = call(
        sums_kernel,
        (
            shape((devices, sum_rows, LANES), bf16),
            shape((slots, 2 * own), f32),
            shape((slots, 2 * own), f32),
            shape((slots, width), bf16),
        ),
        [
            pltpu.VMEM((slots, key_rows, LANES), f32),
            pltpu.VMEM((slots, sum_rows, LANES), f32),
        ],
        [keys, tokens_near, tokens_other, cotangent_near, cotangent_other],
    )
    parts = lax.all_to_all(message, both, 0, 0, tiled=True)

    row_count = padded(2 * width // LANES + 1, 8)
    message, slot_in, slot_out_grad, hidden_rows = call(
        functools.partial(expert_kernel, exp_size),
        (
            shape((devices, row_count, LANES), bf16),
            shape((1, width), bf16),
            shape((1, width), bf16),
            shape((2, hidden), bf16),
        ),
        [pltpu.VMEM((devices, sum_rows, LANES), f32), pltpu.VMEM((row_count, LANES), f32)],
        [parts, w_in_other[0], w_out_other[0]],
    )
    gathered = lax.all_to_all(message, both, 0, 0, tiled=True)
    own_rows = lax.ppermute(hidden_rows, "seq", swap)
    w_in_grad, w_out_grad = call(
        weight_grads_kernel,
        (shape((1, hidden, width), bf16), shape((1, hidden, width), bf16)),
        [
            pltpu.VMEM((2, hidden, width), bf16),
            pltpu.SemaphoreType.DMA((2, hidden // block_of(hidden))),
        ],
        [own_rows, slot_in, slot_out_grad],
        far_out=2,
    )
    gathered, w_in_grad, w_out_grad = lax.optimization_barrier((gathered, w_in_grad, w_out_grad))

    message, slot_out, slot_in_grad, factors = call(
        grads_kernel,
        (
            shape((devices, 1, half), f32),
            shape((slots, width), bf16),
            shape((slots, width), bf16),
            shape((3 * slots, own), f32),
        ),
        [pltpu.VMEM((devices, row_count, LANES), f32)],
        [gathered, logits, comb_prob, tokens_near, tokens_other, cotangent_near, cotangent_other],
    )
    keys_parts = lax.all_to_all(message, both, 0, 0, tiled=True)
    layer_out, tokens_grad = call(
        outputs_kernel,
        (shape((own, width), bf16), shape((own, width), bf16)),
        [],
        [factors, slot_out, slot_in_grad, keys_all],
    )
    keys_parts = keys_parts.reshape(seq_size // 2, 2, exp_size, half)
    keys_grad = jnp.sum(keys_parts, axis=(0, 2)).reshape(1, width).T
    return (layer_out, tokens_grad, keys_grad, w_in_grad, w_out_grad)


def solution(mesh):
    return jax.shard_map(
        local,
        mesh=mesh,
        in_specs=(
            P(("seq", "exp"), None),
            P(None, "exp"),
            P("exp", "seq", None),
            P("exp", "seq", None),
            P(("seq", "exp"), None),
        ),
        out_specs=(
            P(("seq", "exp"), None),
            P(("seq", "exp"), None),
            P(None, "exp"),
            P("exp", "seq", None),
            P("exp", "seq", None),
        ),
        check_vma=False,
    )
```

```python
import functools

import jax
import jax.numpy as jnp
from jax import lax
from jax.experimental import pallas as pl
from jax.experimental.pallas import tpu as pltpu
from jax.sharding import PartitionSpec as P

tanh_coeff = 0.7978845608028654
cubic_coeff = 0.044715
LANES = 128
VECTOR_SHARE = 0.65


def dot(left, right, left_dim, right_dim):
    return lax.dot_general(
        left, right, (((left_dim,), (right_dim,)), ((), ())), preferred_element_type=jnp.float32
    )


def gelu_parts(values):
    tanh_part = jnp.tanh(tanh_coeff * (values + cubic_coeff * values * values * values))
    value = 0.5 * values * (1.0 + tanh_part)
    slope = 0.5 * (1.0 + tanh_part) + 0.5 * values * (1.0 - tanh_part * tanh_part) * tanh_coeff * (
        1.0 + 3.0 * cubic_coeff * values * values
    )
    return value, slope


def padded(rows, multiple):
    return -(-rows // multiple) * multiple


def bf16_terms(values, count):
    terms = []
    for _ in range(count):
        term = values.astype(jnp.bfloat16).astype(jnp.float32)
        terms.append(term)
        values = values - term
    return terms


def in_lanes(columns, lane):
    row = jnp.zeros((columns[0].shape[0], LANES), jnp.float32)
    for i, column in enumerate(columns):
        row = jnp.where(lane == i, column, row)
    return row


def from_lanes(row, lane, first, count):
    keep = (lane >= first) & (lane < first + count)
    return jnp.sum(jnp.where(keep, row, 0.0), axis=1, keepdims=True)


def lanes_of(rows):
    return lax.broadcasted_iota(jnp.int32, (rows, LANES), 1)


def call(kernel, out_shape, scratch_shapes, inputs, far=0, far_out=0):
    near = len(inputs) - far
    spaces = [pltpu.VMEM] * near + [pltpu.HBM] * far
    inputs = inputs[:near] + [pltpu.with_memory_space_constraint(x, pltpu.HBM) for x in inputs[near:]]
    outs = len(out_shape)
    out_spaces = [pltpu.VMEM] * (outs - far_out) + [pltpu.HBM] * far_out
    return pl.pallas_call(
        kernel,
        out_shape=out_shape,
        in_specs=[pl.BlockSpec(memory_space=space) for space in spaces],
        out_specs=tuple(pl.BlockSpec(memory_space=space) for space in out_spaces),
        scratch_shapes=scratch_shapes,
        compiler_params=pltpu.CompilerParams(vmem_limit_bytes=24 * 1024 * 1024),
    )(*inputs)


def keys_kernel(
    key_in_ref, tokens_in_ref, cotangent_in_ref, out_ref, tokens_ref, cotangent_ref, key_ref, rows_ref, sems
):
    copies = [
        pltpu.make_async_copy(source, target, sems.at[i])
        for i, (source, target) in enumerate(
            [(key_in_ref, key_ref), (tokens_in_ref, tokens_ref), (cotangent_in_ref, cotangent_ref)]
        )
    ]
    for copy in copies:
        copy.start()
    width = key_ref.shape[1]
    copies[0].wait()
    rows_ref[...] = jnp.zeros_like(rows_ref)
    key = key_ref[...].astype(jnp.float32)
    for j in range(width // LANES):
        rows_ref[j : j + 1, :] = key[:, j * LANES : (j + 1) * LANES]
    block = rows_ref[...].astype(jnp.bfloat16)
    for i in range(out_ref.shape[0]):
        out_ref[i] = block
    copies[1].wait()
    copies[2].wait()


def sums_kernel(
    keys_ref, tokens_ref, tokens_other_ref, cotangent_ref, cotangent_other_ref,
    message_ref, logits_ref, comb_ref, keys_all_ref, keys_rows_ref, rows_ref,
):
    slots = keys_ref.shape[0]
    width = tokens_ref.shape[1]
    half = width // 2
    chunks = half // LANES
    first = pl.multiple_of(lax.rem(lax.axis_index("seq"), 2) * half, LANES)

    keys_rows_ref[...] = keys_ref[...].astype(jnp.float32)
    keys = jnp.concatenate(
        [keys_rows_ref[:, j, :] for j in range(width // LANES)], axis=1
    ).astype(jnp.bfloat16)
    keys_all_ref[...] = keys
    other_logits = dot(keys, tokens_other_ref[...], 1, 1)
    logits = jnp.concatenate([dot(keys, tokens_ref[...], 1, 1), other_logits], axis=1)
    logits_ref[...] = logits
    own = tokens_ref.shape[0]

    row_terms = jnp.exp(logits - jnp.max(logits, axis=0, keepdims=True))
    comb_prob = row_terms / jnp.sum(row_terms, axis=0, keepdims=True)
    comb_ref[...] = comb_prob
    combine = comb_prob.astype(jnp.bfloat16)
    grad_sums = dot(combine[:, :own], cotangent_ref[:, pl.ds(first, half)], 1, 0) + dot(
        combine[:, own:], cotangent_other_ref[:, pl.ds(first, half)], 1, 0
    )

    peak = jnp.max(logits, axis=1, keepdims=True)
    terms = jnp.exp(logits - peak)
    total = jnp.sum(terms, axis=1, keepdims=True)
    parts = jnp.concatenate(bf16_terms(terms, 2), axis=0).astype(jnp.bfloat16)
    sums = dot(parts[:, :own], tokens_ref[:, pl.ds(first, half)], 1, 0) + dot(
        parts[:, own:], tokens_other_ref[:, pl.ds(first, half)], 1, 0
    )
    high, low = bf16_terms(sums[:slots] + sums[slots:], 2)
    for j in range(chunks):
        columns = slice(j * LANES, (j + 1) * LANES)
        rows_ref[:, j, :] = high[:, columns]
        rows_ref[:, chunks + j, :] = low[:, columns]
        rows_ref[:, 2 * chunks + j, :] = grad_sums[:, columns]
    stats = in_lanes(bf16_terms(peak, 3) + bf16_terms(total, 3), lanes_of(slots))
    rows_ref[:, 3 * chunks, :] = stats
    for j in range(3 * chunks + 1, rows_ref.shape[1]):
        rows_ref[:, j, :] = jnp.zeros_like(stats)
    block = rows_ref[...].astype(jnp.bfloat16)
    for q in range(message_ref.shape[0] // slots):
        message_ref[q * slots : (q + 1) * slots] = block


def lane_sums_times(row, w_ref, first, count):
    row_chunks = [
        row[:, j * LANES : (j + 1) * LANES].astype(jnp.float32) for j in range(row.shape[1] // LANES)
    ]
    highs, lows = [], []
    for start in range(first, first + count, 16):
        total = None
        for j, chunk in enumerate(row_chunks):
            term = w_ref[start : start + 16, j * LANES : (j + 1) * LANES].astype(jnp.float32) * chunk
            total = term if total is None else total + term
        high = total.astype(jnp.bfloat16)
        highs.append(high)
        lows.append((total - high.astype(jnp.float32)).astype(jnp.bfloat16))
    ones = jnp.ones((8, LANES), jnp.bfloat16)
    sums = dot(ones, jnp.concatenate(highs, axis=0), 1, 1) + dot(ones, jnp.concatenate(lows, axis=0), 1, 1)
    return sums[:1]


def rows_times(pairs):
    results, taken = [], 0
    for row, w_ref in pairs:
        rows = w_ref.shape[0]
        block = LANES if rows % LANES == 0 else rows
        outs = []
        for first in range(0, rows, block):
            taken += VECTOR_SHARE
            if taken >= 1.0 and block == LANES:
                taken -= 1.0
                outs.append(lane_sums_times(row, w_ref, first, block))
            else:
                outs.append(dot(row, w_ref[first : first + block, :], 1, 1))
        results.append(jnp.concatenate(outs, axis=1))
    return results


def expert_kernel(
    exp_size, parts_ref, w_in_ref, w_out_ref,
    message_ref, slot_in_ref, slot_out_grad_ref, hidden_rows_ref, parts_rows_ref, rows_ref,
):
    devices = parts_ref.shape[0]
    seq_size = devices // exp_size
    width = w_in_ref.shape[1]
    chunks = width // LANES
    per_side = chunks // 2
    parts_rows_ref[...] = parts_ref[...].astype(jnp.float32)
    stats = parts_rows_ref[:, 3 * per_side, :]
    lane = lanes_of(devices)
    peaks = from_lanes(stats, lane, 0, 3)
    totals = from_lanes(stats, lane, 3, 3)
    slot_peak = jnp.max(peaks, axis=0, keepdims=True)
    scale = jnp.exp(peaks - slot_peak)

    def of_side(values, side):
        total = values[side * exp_size : (side + 1) * exp_size]
        for q in range(side + 2, seq_size, 2):
            total = total + values[q * exp_size : (q + 1) * exp_size]
        return jnp.sum(total, axis=0, keepdims=True)

    slot_total = of_side(totals * scale, 0)
    slot_chunks, grad_chunks = [[], []], [[], []]
    for j in range(per_side):
        weighted = (parts_rows_ref[:, j, :] + parts_rows_ref[:, per_side + j, :]) * scale
        grads = parts_rows_ref[:, 2 * per_side + j, :]
        for side in range(2):
            slot_chunks[side].append(of_side(weighted, side))
            grad_chunks[side].append(of_side(grads, side))
    slot_row = jnp.concatenate(slot_chunks[0] + slot_chunks[1], axis=1) / slot_total
    slot_in = slot_row.astype(jnp.bfloat16)
    slot_out_grad = jnp.concatenate(grad_chunks[0] + grad_chunks[1], axis=1).astype(jnp.bfloat16)
    slot_in_ref[...] = slot_in
    slot_out_grad_ref[...] = slot_out_grad

    pre_act, act_grad = rows_times([(slot_in, w_in_ref), (slot_out_grad, w_out_ref)])
    value, slope = gelu_parts(pre_act)
    activation = value.astype(jnp.bfloat16)
    pre_grad = (act_grad * slope).astype(jnp.bfloat16)
    hidden_rows_ref[...] = jnp.concatenate([value, act_grad * slope], axis=0).astype(jnp.bfloat16)
    out_part = dot(activation, w_out_ref[...], 1, 0)
    grad_part = dot(pre_grad, w_in_ref[...], 1, 0).astype(jnp.bfloat16).astype(jnp.float32)
    correction = jnp.sum(slot_row * grad_part, axis=1, keepdims=True)
    for j in range(chunks):
        columns = slice(j * LANES, (j + 1) * LANES)
        rows_ref[j : j + 1, :] = out_part[:, columns]
        rows_ref[chunks + j : chunks + j + 1, :] = grad_part[:, columns]
    stats = in_lanes(
        bf16_terms(slot_peak, 3) + bf16_terms(slot_total, 3) + bf16_terms(correction, 3), lanes_of(1)
    )
    rows_ref[2 * chunks : 2 * chunks + 1, :] = stats
    for j in range(2 * chunks + 1, rows_ref.shape[0]):
        rows_ref[j : j + 1, :] = jnp.zeros_like(stats)
    block = rows_ref[...].astype(jnp.bfloat16)
    for i in range(devices):
        message_ref[i] = block


def grads_kernel(
    parts_ref, logits_ref, comb_ref, tokens_ref, tokens_other_ref, cotangent_ref, cotangent_other_ref,
    message_ref, slot_out_ref, slot_in_grad_ref, factors_ref, parts_rows_ref,
):
    devices = parts_ref.shape[0]
    slots, _ = logits_ref.shape
    seq_size = devices // slots
    own, width = tokens_ref.shape
    half = width // 2
    chunks = width // LANES
    first = pl.multiple_of(lax.rem(lax.axis_index("seq"), 2) * half, LANES)
    parts_rows_ref[...] = parts_ref[...].astype(jnp.float32)
    out_rows = jnp.concatenate([parts_rows_ref[:, j, :] for j in range(chunks)], axis=1)
    grad_rows = jnp.concatenate([parts_rows_ref[:, chunks + j, :] for j in range(chunks)], axis=1)
    stats = parts_rows_ref[:, 2 * chunks, :]
    lane = lanes_of(slots)

    def over_seq(values):
        total = values[:slots]
        for q in range(1, seq_size):
            total = total + values[q * slots : (q + 1) * slots]
        return total

    peak = from_lanes(stats[:slots], lane, 0, 3)
    total = from_lanes(stats[:slots], lane, 3, 3)
    correction = from_lanes(over_seq(stats), lane, 6, 3)
    slot_out_ref[...] = over_seq(out_rows).astype(jnp.bfloat16)
    slot_in_grad_ref[...] = over_seq(grad_rows).astype(jnp.bfloat16)
    out_rows = out_rows.astype(jnp.bfloat16)
    grad_rows = grad_rows.astype(jnp.bfloat16)
    comb_grad = over_seq(
        jnp.concatenate(
            [dot(out_rows, cotangent_ref[...], 1, 1), dot(out_rows, cotangent_other_ref[...], 1, 1)], axis=1
        )
    )
    disp_grad = over_seq(
        jnp.concatenate(
            [dot(grad_rows, tokens_ref[...], 1, 1), dot(grad_rows, tokens_other_ref[...], 1, 1)], axis=1
        )
    )
    comb_prob = comb_ref[...]
    disp_prob = jnp.exp(logits_ref[...] - peak) / total
    comb_mean = jnp.sum(comb_prob * comb_grad, axis=0, keepdims=True)
    logit_grad = (
        comb_prob * (comb_grad - comb_mean) + disp_prob * (disp_grad - correction)
    ).astype(jnp.bfloat16)
    factors = [comb_prob[:, :own], disp_prob[:, :own], logit_grad[:, :own]]
    for i, factor in enumerate(factors):
        factors_ref[i * slots : (i + 1) * slots] = factor.astype(jnp.bfloat16).astype(jnp.float32)
    keys_part = dot(logit_grad[:, :own], tokens_ref[:, pl.ds(first, half)], 1, 0) + dot(
        logit_grad[:, own:], tokens_other_ref[:, pl.ds(first, half)], 1, 0
    )
    for s in range(slots):
        for q in range(seq_size):
            message_ref[q * slots + s] = keys_part[s : s + 1]


def block_of(rows):
    return 128 if rows % 128 == 0 else rows


def weight_grads_kernel(hidden_rows_ref, slot_in_ref, slot_out_grad_ref, w_in_grad_ref, w_out_grad_ref, near_ref, sems):
    hidden = near_ref.shape[1]
    block = block_of(hidden)
    hidden_rows = hidden_rows_ref[...].astype(jnp.float32)
    copies = []
    for w, (hidden_index, row_ref, far_ref) in enumerate(
        [(0, slot_out_grad_ref, w_out_grad_ref), (1, slot_in_ref, w_in_grad_ref)]
    ):
        row = row_ref[...].astype(jnp.float32)
        for i in range(hidden // block):
            rows = pl.ds(i * block, block)
            part = hidden_rows[hidden_index : hidden_index + 1, i * block : (i + 1) * block]
            column = jnp.transpose(jnp.broadcast_to(part, (8, block)))[:, :1]
            near_ref[w, rows, :] = (column * row).astype(jnp.bfloat16)
            copy = pltpu.make_async_copy(near_ref.at[w, rows], far_ref.at[0, rows], sems.at[w, i])
            copy.start()
            copies.append(copy)
    for copy in copies:
        copy.wait()


def outputs_kernel(
    keys_parts_ref, factors_ref, slot_out_ref, slot_in_grad_ref, keys_ref,
    layer_out_ref, tokens_grad_ref, keys_grad_ref, layer_near_ref, tokens_near_ref, keys_near_ref, sems,
):
    slots = slot_out_ref.shape[0]
    half = keys_parts_ref.shape[2]
    copies = [
        pltpu.make_async_copy(near, far, sems.at[i])
        for i, (near, far) in enumerate(
            [(layer_near_ref, layer_out_ref), (tokens_near_ref, tokens_grad_ref), (keys_near_ref, keys_grad_ref)]
        )
    ]
    for side in range(2):
        total = keys_parts_ref[side * slots : (side + 1) * slots, 0, :]
        for first in range((side + 2) * slots, keys_parts_ref.shape[0], 2 * slots):
            total = total + keys_parts_ref[first : first + slots, 0, :]
        keys_near_ref[:, side * half : (side + 1) * half] = jnp.sum(total, axis=0, keepdims=True)
    copies[2].start()
    combine = jnp.transpose(factors_ref[:slots, :]).astype(jnp.bfloat16)
    layer_near_ref[...] = dot(combine, slot_out_ref[...], 1, 0).astype(jnp.bfloat16)
    copies[0].start()
    others = jnp.transpose(factors_ref[slots:, :]).astype(jnp.bfloat16)
    rows = jnp.concatenate(
        [slot_in_grad_ref[...].astype(jnp.float32), keys_ref[...].astype(jnp.float32)], axis=0
    ).astype(jnp.bfloat16)
    tokens_near_ref[...] = dot(others, rows, 1, 0).astype(jnp.bfloat16)
    copies[1].start()
    for copy in copies:
        copy.wait()


def local(tokens, slot_keys, w_in, w_out, cotangent):
    both = ("seq", "exp")
    seq_size, exp_size = lax.axis_size("seq"), lax.axis_size("exp")
    devices = seq_size * exp_size
    experts, hidden, width = w_in.shape
    assert experts == 1 and seq_size % 2 == 0
    slots = exp_size
    half = width // 2
    own = tokens.shape[0]
    swap = [(i, i ^ 1) for i in range(seq_size)]
    f32, bf16 = jnp.float32, jnp.bfloat16
    shape = jax.ShapeDtypeStruct

    key_rows = padded(width // LANES, 16)
    key_message, tokens_near, cotangent_near = call(
        keys_kernel,
        (
            shape((exp_size, key_rows, LANES), bf16),
            shape(tokens.shape, bf16),
            shape(cotangent.shape, bf16),
        ),
        [pltpu.VMEM((1, width), bf16), pltpu.VMEM((key_rows, LANES), f32), pltpu.SemaphoreType.DMA((3,))],
        [slot_keys.T, tokens, cotangent],
        far=3,
    )
    tokens_other = lax.ppermute(tokens, "seq", swap)
    cotangent_other = lax.ppermute(cotangent, "seq", swap)
    keys = lax.all_to_all(key_message, "exp", 0, 0, tiled=True)
    keys, w_in_late, w_out_late, tokens_other, cotangent_other = lax.optimization_barrier((keys, w_in, w_out, tokens_other, cotangent_other))
    w_in_other = lax.ppermute(w_in_late, "seq", swap)
    w_out_other = lax.ppermute(w_out_late, "seq", swap)

    sum_rows = padded(3 * half // LANES + 1, 16)
    message, logits, comb_prob, keys_all = call(
        sums_kernel,
        (
            shape((devices, sum_rows, LANES), bf16),
            shape((slots, 2 * own), f32),
            shape((slots, 2 * own), f32),
            shape((slots, width), bf16),
        ),
        [
            pltpu.VMEM((slots, key_rows, LANES), f32),
            pltpu.VMEM((slots, sum_rows, LANES), f32),
        ],
        [keys, tokens_near, tokens_other, cotangent_near, cotangent_other],
    )
    parts = lax.all_to_all(message, both, 0, 0, tiled=True)

    row_count = padded(2 * width // LANES + 1, 8)
    message, slot_in, slot_out_grad, hidden_rows = call(
        functools.partial(expert_kernel, exp_size),
        (
            shape((devices, row_count, LANES), bf16),
            shape((1, width), bf16),
            shape((1, width), bf16),
            shape((2, hidden), bf16),
        ),
        [pltpu.VMEM((devices, sum_rows, LANES), f32), pltpu.VMEM((row_count, LANES), f32)],
        [parts, w_in_other[0], w_out_other[0]],
    )
    gathered = lax.all_to_all(message, both, 0, 0, tiled=True)
    own_rows = lax.ppermute(hidden_rows, "seq", swap)
    w_in_grad, w_out_grad = call(
        weight_grads_kernel,
        (shape((1, hidden, width), bf16), shape((1, hidden, width), bf16)),
        [
            pltpu.VMEM((2, hidden, width), bf16),
            pltpu.SemaphoreType.DMA((2, hidden // block_of(hidden))),
        ],
        [own_rows, slot_in, slot_out_grad],
        far_out=2,
    )
    gathered, w_in_grad, w_out_grad = lax.optimization_barrier((gathered, w_in_grad, w_out_grad))

    message, slot_out, slot_in_grad, factors = call(
        grads_kernel,
        (
            shape((devices, 1, half), f32),
            shape((slots, width), bf16),
            shape((slots, width), bf16),
            shape((3 * slots, own), f32),
        ),
        [pltpu.VMEM((devices, row_count, LANES), f32)],
        [gathered, logits, comb_prob, tokens_near, tokens_other, cotangent_near, cotangent_other],
    )
    keys_parts = lax.all_to_all(message, both, 0, 0, tiled=True)
    layer_out, tokens_grad, keys_grad = call(
        outputs_kernel,
        (shape((own, width), bf16), shape((own, width), bf16), shape((1, width), f32)),
        [
            pltpu.VMEM((own, width), bf16),
            pltpu.VMEM((own, width), bf16),
            pltpu.VMEM((1, width), f32),
            pltpu.SemaphoreType.DMA((3,)),
        ],
        [keys_parts, factors, slot_out, slot_in_grad, keys_all],
        far_out=3,
    )
    return (layer_out, tokens_grad, keys_grad.T, w_in_grad, w_out_grad)


def solution(mesh):
    return jax.shard_map(
        local,
        mesh=mesh,
        in_specs=(
            P(("seq", "exp"), None),
            P(None, "exp"),
            P("exp", "seq", None),
            P("exp", "seq", None),
            P(("seq", "exp"), None),
        ),
        out_specs=(
            P(("seq", "exp"), None),
            P(("seq", "exp"), None),
            P(None, "exp"),
            P("exp", "seq", None),
            P("exp", "seq", None),
        ),
        check_vma=False,
    )
```

```python
import functools

import jax
import jax.numpy as jnp
from jax import lax
from jax.experimental import pallas as pl
from jax.experimental.pallas import tpu as pltpu
from jax.sharding import PartitionSpec as P

tanh_coeff = 0.7978845608028654
cubic_coeff = 0.044715
LANES = 128
VECTOR_SHARE = 0.65
SUM_SHARE = 0.45


def dot(left, right, left_dim, right_dim):
    return lax.dot_general(
        left, right, (((left_dim,), (right_dim,)), ((), ())), preferred_element_type=jnp.float32
    )


def gelu_parts(values):
    tanh_part = jnp.tanh(tanh_coeff * (values + cubic_coeff * values * values * values))
    value = 0.5 * values * (1.0 + tanh_part)
    slope = 0.5 * (1.0 + tanh_part) + 0.5 * values * (1.0 - tanh_part * tanh_part) * tanh_coeff * (
        1.0 + 3.0 * cubic_coeff * values * values
    )
    return value, slope


def padded(rows, multiple):
    return -(-rows // multiple) * multiple


def bf16_terms(values, count):
    terms = []
    for _ in range(count):
        term = values.astype(jnp.bfloat16).astype(jnp.float32)
        terms.append(term)
        values = values - term
    return terms


def in_lanes(columns, lane):
    row = jnp.zeros((columns[0].shape[0], LANES), jnp.float32)
    for i, column in enumerate(columns):
        row = jnp.where(lane == i, column, row)
    return row


def from_lanes(row, lane, first, count):
    keep = (lane >= first) & (lane < first + count)
    return jnp.sum(jnp.where(keep, row, 0.0), axis=1, keepdims=True)


def lanes_of(rows):
    return lax.broadcasted_iota(jnp.int32, (rows, LANES), 1)


def call(kernel, out_shape, scratch_shapes, inputs, far=0, far_out=0):
    near = len(inputs) - far
    spaces = [pltpu.VMEM] * near + [pltpu.HBM] * far
    inputs = inputs[:near] + [pltpu.with_memory_space_constraint(x, pltpu.HBM) for x in inputs[near:]]
    outs = len(out_shape)
    out_spaces = [pltpu.VMEM] * (outs - far_out) + [pltpu.HBM] * far_out
    return pl.pallas_call(
        kernel,
        out_shape=out_shape,
        in_specs=[pl.BlockSpec(memory_space=space) for space in spaces],
        out_specs=tuple(pl.BlockSpec(memory_space=space) for space in out_spaces),
        scratch_shapes=scratch_shapes,
        compiler_params=pltpu.CompilerParams(vmem_limit_bytes=24 * 1024 * 1024),
    )(*inputs)


def keys_kernel(
    key_in_ref, tokens_in_ref, cotangent_in_ref, out_ref, tokens_ref, cotangent_ref, key_ref, rows_ref, sems
):
    copies = [
        pltpu.make_async_copy(source, target, sems.at[i])
        for i, (source, target) in enumerate(
            [(key_in_ref, key_ref), (tokens_in_ref, tokens_ref), (cotangent_in_ref, cotangent_ref)]
        )
    ]
    for copy in copies:
        copy.start()
    width = key_ref.shape[1]
    copies[0].wait()
    rows_ref[...] = jnp.zeros_like(rows_ref)
    key = key_ref[...].astype(jnp.float32)
    for j in range(width // LANES):
        rows_ref[j : j + 1, :] = key[:, j * LANES : (j + 1) * LANES]
    block = rows_ref[...].astype(jnp.bfloat16)
    for i in range(out_ref.shape[0]):
        out_ref[i] = block
    copies[1].wait()
    copies[2].wait()


def sums_kernel(
    keys_ref, tokens_ref, tokens_other_ref, cotangent_ref, cotangent_other_ref,
    message_ref, logits_ref, comb_ref, keys_all_ref, keys_rows_ref, rows_ref,
):
    slots = keys_ref.shape[0]
    width = tokens_ref.shape[1]
    half = width // 2
    chunks = half // LANES
    first = pl.multiple_of(lax.rem(lax.axis_index("seq"), 2) * half, LANES)

    keys_rows_ref[...] = keys_ref[...].astype(jnp.float32)
    keys = jnp.concatenate(
        [keys_rows_ref[:, j, :] for j in range(width // LANES)], axis=1
    ).astype(jnp.bfloat16)
    keys_all_ref[...] = keys
    other_logits = dot(keys, tokens_other_ref[...], 1, 1)
    logits = jnp.concatenate([dot(keys, tokens_ref[...], 1, 1), other_logits], axis=1)
    logits_ref[...] = logits
    own = tokens_ref.shape[0]

    row_terms = jnp.exp(logits - jnp.max(logits, axis=0, keepdims=True))
    comb_prob = row_terms / jnp.sum(row_terms, axis=0, keepdims=True)
    comb_ref[...] = comb_prob
    combine = comb_prob.astype(jnp.bfloat16)
    grad_sums = dot(combine[:, :own], cotangent_ref[:, pl.ds(first, half)], 1, 0) + dot(
        combine[:, own:], cotangent_other_ref[:, pl.ds(first, half)], 1, 0
    )

    peak = jnp.max(logits, axis=1, keepdims=True)
    terms = jnp.exp(logits - peak)
    total = jnp.sum(terms, axis=1, keepdims=True)
    parts = jnp.concatenate(bf16_terms(terms, 2), axis=0).astype(jnp.bfloat16)
    sums = dot(parts[:, :own], tokens_ref[:, pl.ds(first, half)], 1, 0) + dot(
        parts[:, own:], tokens_other_ref[:, pl.ds(first, half)], 1, 0
    )
    high, low = bf16_terms(sums[:slots] + sums[slots:], 2)
    for j in range(chunks):
        columns = slice(j * LANES, (j + 1) * LANES)
        rows_ref[:, j, :] = high[:, columns]
        rows_ref[:, chunks + j, :] = low[:, columns]
        rows_ref[:, 2 * chunks + j, :] = grad_sums[:, columns]
    stats = in_lanes(bf16_terms(peak, 3) + bf16_terms(total, 3), lanes_of(slots))
    rows_ref[:, 3 * chunks, :] = stats
    for j in range(3 * chunks + 1, rows_ref.shape[1]):
        rows_ref[:, j, :] = jnp.zeros_like(stats)
    block = rows_ref[...].astype(jnp.bfloat16)
    for q in range(message_ref.shape[0] // slots):
        message_ref[q * slots : (q + 1) * slots] = block


def lane_sums_times(row, w_ref, first, count):
    row_chunks = [
        row[:, j * LANES : (j + 1) * LANES].astype(jnp.float32) for j in range(row.shape[1] // LANES)
    ]
    highs, lows = [], []
    for start in range(first, first + count, 16):
        total = None
        for j, chunk in enumerate(row_chunks):
            term = w_ref[start : start + 16, j * LANES : (j + 1) * LANES].astype(jnp.float32) * chunk
            total = term if total is None else total + term
        high = total.astype(jnp.bfloat16)
        highs.append(high)
        lows.append((total - high.astype(jnp.float32)).astype(jnp.bfloat16))
    ones = jnp.ones((8, LANES), jnp.bfloat16)
    sums = dot(ones, jnp.concatenate(highs, axis=0), 1, 1) + dot(ones, jnp.concatenate(lows, axis=0), 1, 1)
    return sums[:1]


def rows_times(pairs):
    results, taken = [], 0
    for row, w_ref in pairs:
        rows = w_ref.shape[0]
        block = LANES if rows % LANES == 0 else rows
        outs = []
        for first in range(0, rows, block):
            taken += VECTOR_SHARE
            if taken >= 1.0 and block == LANES:
                taken -= 1.0
                outs.append(lane_sums_times(row, w_ref, first, block))
            else:
                outs.append(dot(row, w_ref[first : first + block, :], 1, 1))
        results.append(jnp.concatenate(outs, axis=1))
    return results


def column_sums_times(row, w_ref, first, count):
    column = jnp.transpose(jnp.broadcast_to(row.astype(jnp.float32), (8, count)))[:, :1]
    total = None
    for start in range(0, count, 16):
        rows = w_ref[first + start : first + start + 16, :].astype(jnp.float32)
        term = rows * column[start : start + 16]
        total = term if total is None else total + term
    return total


def sums_times(pairs):
    results, taken = [], 0
    for row, w_ref in pairs:
        rows = w_ref.shape[0]
        block = LANES if rows % LANES == 0 else rows
        vector_total, matrix_blocks = None, []
        for first in range(0, rows, block):
            taken += SUM_SHARE
            if taken >= 1.0 and block == LANES:
                taken -= 1.0
                part = column_sums_times(row[:, first : first + block], w_ref, first, block)
                vector_total = part if vector_total is None else vector_total + part
            else:
                matrix_blocks.append(dot(row[:, first : first + block], w_ref[first : first + block, :], 1, 0))
        total = matrix_blocks[0]
        for part in matrix_blocks[1:]:
            total = total + part
        if vector_total is not None:
            total = total + jnp.sum(vector_total, axis=0, keepdims=True)
        results.append(total)
    return results


def expert_kernel(
    exp_size, parts_ref, w_in_ref, w_out_ref,
    message_ref, slot_in_ref, slot_out_grad_ref, hidden_rows_ref, parts_rows_ref, rows_ref,
):
    devices = parts_ref.shape[0]
    seq_size = devices // exp_size
    width = w_in_ref.shape[1]
    chunks = width // LANES
    per_side = chunks // 2
    parts_rows_ref[...] = parts_ref[...].astype(jnp.float32)
    stats = parts_rows_ref[:, 3 * per_side, :]
    lane = lanes_of(devices)
    peaks = from_lanes(stats, lane, 0, 3)
    totals = from_lanes(stats, lane, 3, 3)
    slot_peak = jnp.max(peaks, axis=0, keepdims=True)
    scale = jnp.exp(peaks - slot_peak)

    def of_side(values, side):
        total = values[side * exp_size : (side + 1) * exp_size]
        for q in range(side + 2, seq_size, 2):
            total = total + values[q * exp_size : (q + 1) * exp_size]
        return jnp.sum(total, axis=0, keepdims=True)

    slot_total = of_side(totals * scale, 0)
    slot_chunks, grad_chunks = [[], []], [[], []]
    for j in range(per_side):
        weighted = (parts_rows_ref[:, j, :] + parts_rows_ref[:, per_side + j, :]) * scale
        grads = parts_rows_ref[:, 2 * per_side + j, :]
        for side in range(2):
            slot_chunks[side].append(of_side(weighted, side))
            grad_chunks[side].append(of_side(grads, side))
    slot_row = jnp.concatenate(slot_chunks[0] + slot_chunks[1], axis=1) / slot_total
    slot_in = slot_row.astype(jnp.bfloat16)
    slot_out_grad = jnp.concatenate(grad_chunks[0] + grad_chunks[1], axis=1).astype(jnp.bfloat16)
    slot_in_ref[...] = slot_in
    slot_out_grad_ref[...] = slot_out_grad

    pre_act, act_grad = rows_times([(slot_in, w_in_ref), (slot_out_grad, w_out_ref)])
    value, slope = gelu_parts(pre_act)
    activation = value.astype(jnp.bfloat16)
    pre_grad = (act_grad * slope).astype(jnp.bfloat16)
    hidden_rows_ref[...] = jnp.concatenate([value, act_grad * slope], axis=0).astype(jnp.bfloat16)
    out_part, grad_part = sums_times([(activation, w_out_ref), (pre_grad, w_in_ref)])
    grad_part = grad_part.astype(jnp.bfloat16).astype(jnp.float32)
    correction = jnp.sum(slot_row * grad_part, axis=1, keepdims=True)
    stats = in_lanes(
        bf16_terms(slot_peak, 3) + bf16_terms(slot_total, 3) + bf16_terms(correction, 3), lanes_of(1)
    )
    rows_ref[0:1, :width] = out_part
    rows_ref[1:2, :width] = grad_part
    rows_ref[0:1, width:] = stats
    rows_ref[1:2, width:] = jnp.zeros_like(stats)
    block = rows_ref[...].astype(jnp.bfloat16)
    for i in range(devices):
        message_ref[i] = block


def grads_kernel(
    parts_ref, logits_ref, comb_ref, tokens_ref, tokens_other_ref, cotangent_ref, cotangent_other_ref,
    message_ref, slot_out_ref, slot_in_grad_ref, factors_ref, parts_rows_ref,
):
    devices = parts_ref.shape[0]
    slots, _ = logits_ref.shape
    seq_size = devices // slots
    own, width = tokens_ref.shape
    half = width // 2
    chunks = width // LANES
    first = pl.multiple_of(lax.rem(lax.axis_index("seq"), 2) * half, LANES)
    parts_rows_ref[...] = parts_ref[...].astype(jnp.float32)
    out_rows = parts_rows_ref[:, 0, :width]
    grad_rows = parts_rows_ref[:, 1, :width]
    stats = parts_rows_ref[:, 0, width:]
    lane = lanes_of(slots)

    def over_seq(values):
        total = values[:slots]
        for q in range(1, seq_size):
            total = total + values[q * slots : (q + 1) * slots]
        return total

    peak = from_lanes(stats[:slots], lane, 0, 3)
    total = from_lanes(stats[:slots], lane, 3, 3)
    correction = from_lanes(over_seq(stats), lane, 6, 3)
    slot_out_ref[...] = over_seq(out_rows).astype(jnp.bfloat16)
    slot_in_grad_ref[...] = over_seq(grad_rows).astype(jnp.bfloat16)
    out_rows = out_rows.astype(jnp.bfloat16)
    grad_rows = grad_rows.astype(jnp.bfloat16)
    comb_grad = over_seq(
        jnp.concatenate(
            [dot(out_rows, cotangent_ref[...], 1, 1), dot(out_rows, cotangent_other_ref[...], 1, 1)], axis=1
        )
    )
    disp_grad = over_seq(
        jnp.concatenate(
            [dot(grad_rows, tokens_ref[...], 1, 1), dot(grad_rows, tokens_other_ref[...], 1, 1)], axis=1
        )
    )
    comb_prob = comb_ref[...]
    disp_prob = jnp.exp(logits_ref[...] - peak) / total
    comb_mean = jnp.sum(comb_prob * comb_grad, axis=0, keepdims=True)
    logit_grad = (
        comb_prob * (comb_grad - comb_mean) + disp_prob * (disp_grad - correction)
    ).astype(jnp.bfloat16)
    factors = [comb_prob[:, :own], disp_prob[:, :own], logit_grad[:, :own]]
    for i, factor in enumerate(factors):
        factors_ref[i * slots : (i + 1) * slots] = factor.astype(jnp.bfloat16).astype(jnp.float32)
    keys_part = dot(logit_grad[:, :own], tokens_ref[:, pl.ds(first, half)], 1, 0) + dot(
        logit_grad[:, own:], tokens_other_ref[:, pl.ds(first, half)], 1, 0
    )
    for s in range(slots):
        for q in range(seq_size):
            message_ref[q * slots + s] = keys_part[s : s + 1]


def block_of(rows):
    return 128 if rows % 128 == 0 else rows


def weight_grads_kernel(hidden_rows_ref, slot_in_ref, slot_out_grad_ref, w_in_grad_ref, w_out_grad_ref, near_ref, sems):
    hidden = near_ref.shape[1]
    block = block_of(hidden)
    hidden_rows = hidden_rows_ref[...].astype(jnp.float32)
    copies = []
    for w, (hidden_index, row_ref, far_ref) in enumerate(
        [(0, slot_out_grad_ref, w_out_grad_ref), (1, slot_in_ref, w_in_grad_ref)]
    ):
        row = row_ref[...].astype(jnp.float32)
        for i in range(hidden // block):
            rows = pl.ds(i * block, block)
            part = hidden_rows[hidden_index : hidden_index + 1, i * block : (i + 1) * block]
            column = jnp.transpose(jnp.broadcast_to(part, (8, block)))[:, :1]
            near_ref[w, rows, :] = (column * row).astype(jnp.bfloat16)
            copy = pltpu.make_async_copy(near_ref.at[w, rows], far_ref.at[0, rows], sems.at[w, i])
            copy.start()
            copies.append(copy)
    for copy in copies:
        copy.wait()


def outputs_kernel(
    keys_parts_ref, factors_ref, slot_out_ref, slot_in_grad_ref, keys_ref,
    layer_out_ref, tokens_grad_ref, keys_grad_ref, layer_near_ref, tokens_near_ref, keys_near_ref, sems,
):
    slots = slot_out_ref.shape[0]
    half = keys_parts_ref.shape[2]
    copies = [
        pltpu.make_async_copy(near, far, sems.at[i])
        for i, (near, far) in enumerate(
            [(layer_near_ref, layer_out_ref), (tokens_near_ref, tokens_grad_ref), (keys_near_ref, keys_grad_ref)]
        )
    ]
    for side in range(2):
        total = keys_parts_ref[side * slots : (side + 1) * slots, 0, :]
        for first in range((side + 2) * slots, keys_parts_ref.shape[0], 2 * slots):
            total = total + keys_parts_ref[first : first + slots, 0, :]
        keys_near_ref[:, side * half : (side + 1) * half] = jnp.sum(total, axis=0, keepdims=True)
    copies[2].start()
    combine = jnp.transpose(factors_ref[:slots, :]).astype(jnp.bfloat16)
    layer_near_ref[...] = dot(combine, slot_out_ref[...], 1, 0).astype(jnp.bfloat16)
    copies[0].start()
    others = jnp.transpose(factors_ref[slots:, :]).astype(jnp.bfloat16)
    rows = jnp.concatenate(
        [slot_in_grad_ref[...].astype(jnp.float32), keys_ref[...].astype(jnp.float32)], axis=0
    ).astype(jnp.bfloat16)
    tokens_near_ref[...] = dot(others, rows, 1, 0).astype(jnp.bfloat16)
    copies[1].start()
    for copy in copies:
        copy.wait()


def local(tokens, slot_keys, w_in, w_out, cotangent):
    both = ("seq", "exp")
    seq_size, exp_size = lax.axis_size("seq"), lax.axis_size("exp")
    devices = seq_size * exp_size
    experts, hidden, width = w_in.shape
    assert experts == 1 and seq_size % 2 == 0
    slots = exp_size
    half = width // 2
    own = tokens.shape[0]
    swap = [(i, i ^ 1) for i in range(seq_size)]
    f32, bf16 = jnp.float32, jnp.bfloat16
    shape = jax.ShapeDtypeStruct

    key_rows = padded(width // LANES, 16)
    key_message, tokens_near, cotangent_near = call(
        keys_kernel,
        (
            shape((exp_size, key_rows, LANES), bf16),
            shape(tokens.shape, bf16),
            shape(cotangent.shape, bf16),
        ),
        [pltpu.VMEM((1, width), bf16), pltpu.VMEM((key_rows, LANES), f32), pltpu.SemaphoreType.DMA((3,))],
        [slot_keys.T, tokens, cotangent],
        far=3,
    )
    tokens_other = lax.ppermute(tokens, "seq", swap)
    cotangent_other = lax.ppermute(cotangent, "seq", swap)
    keys = lax.all_to_all(key_message, "exp", 0, 0, tiled=True)
    keys, w_in_late, w_out_late, tokens_other, cotangent_other = lax.optimization_barrier((keys, w_in, w_out, tokens_other, cotangent_other))
    w_in_other = lax.ppermute(w_in_late, "seq", swap)
    w_out_other = lax.ppermute(w_out_late, "seq", swap)

    sum_rows = padded(3 * half // LANES + 1, 16)
    message, logits, comb_prob, keys_all = call(
        sums_kernel,
        (
            shape((devices, sum_rows, LANES), bf16),
            shape((slots, 2 * own), f32),
            shape((slots, 2 * own), f32),
            shape((slots, width), bf16),
        ),
        [
            pltpu.VMEM((slots, key_rows, LANES), f32),
            pltpu.VMEM((slots, sum_rows, LANES), f32),
        ],
        [keys, tokens_near, tokens_other, cotangent_near, cotangent_other],
    )
    parts = lax.all_to_all(message, both, 0, 0, tiled=True)

    message, slot_in, slot_out_grad, hidden_rows = call(
        functools.partial(expert_kernel, exp_size),
        (
            shape((devices, 2, width + LANES), bf16),
            shape((1, width), bf16),
            shape((1, width), bf16),
            shape((2, hidden), bf16),
        ),
        [pltpu.VMEM((devices, sum_rows, LANES), f32), pltpu.VMEM((2, width + LANES), f32)],
        [parts, w_in_other[0], w_out_other[0]],
    )
    gathered = lax.all_to_all(message, both, 0, 0, tiled=True)
    own_rows = lax.ppermute(hidden_rows, "seq", swap)
    w_in_grad, w_out_grad = call(
        weight_grads_kernel,
        (shape((1, hidden, width), bf16), shape((1, hidden, width), bf16)),
        [
            pltpu.VMEM((2, hidden, width), bf16),
            pltpu.SemaphoreType.DMA((2, hidden // block_of(hidden))),
        ],
        [own_rows, slot_in, slot_out_grad],
        far_out=2,
    )
    gathered, w_in_grad, w_out_grad = lax.optimization_barrier((gathered, w_in_grad, w_out_grad))

    message, slot_out, slot_in_grad, factors = call(
        grads_kernel,
        (
            shape((devices, 1, half), f32),
            shape((slots, width), bf16),
            shape((slots, width), bf16),
            shape((3 * slots, own), f32),
        ),
        [pltpu.VMEM((devices, 2, width + LANES), f32)],
        [gathered, logits, comb_prob, tokens_near, tokens_other, cotangent_near, cotangent_other],
    )
    keys_parts = lax.all_to_all(message, both, 0, 0, tiled=True)
    layer_out, tokens_grad, keys_grad = call(
        outputs_kernel,
        (shape((own, width), bf16), shape((own, width), bf16), shape((1, width), f32)),
        [
            pltpu.VMEM((own, width), bf16),
            pltpu.VMEM((own, width), bf16),
            pltpu.VMEM((1, width), f32),
            pltpu.SemaphoreType.DMA((3,)),
        ],
        [keys_parts, factors, slot_out, slot_in_grad, keys_all],
        far_out=3,
    )
    return (layer_out, tokens_grad, keys_grad.T, w_in_grad, w_out_grad)


def solution(mesh):
    return jax.shard_map(
        local,
        mesh=mesh,
        in_specs=(
            P(("seq", "exp"), None),
            P(None, "exp"),
            P("exp", "seq", None),
            P("exp", "seq", None),
            P(("seq", "exp"), None),
        ),
        out_specs=(
            P(("seq", "exp"), None),
            P(("seq", "exp"), None),
            P(None, "exp"),
            P("exp", "seq", None),
            P("exp", "seq", None),
        ),
        check_vma=False,
    )
```

```python
import functools

import jax
import jax.numpy as jnp
from jax import lax
from jax.experimental import pallas as pl
from jax.experimental.pallas import tpu as pltpu
from jax.sharding import PartitionSpec as P

tanh_coeff = 0.7978845608028654
cubic_coeff = 0.044715
LANES = 128
VECTOR_SHARE = 0.65
SUM_SHARE = 0.25


def dot(left, right, left_dim, right_dim):
    return lax.dot_general(
        left, right, (((left_dim,), (right_dim,)), ((), ())), preferred_element_type=jnp.float32
    )


def gelu_parts(values):
    tanh_part = jnp.tanh(tanh_coeff * (values + cubic_coeff * values * values * values))
    value = 0.5 * values * (1.0 + tanh_part)
    slope = 0.5 * (1.0 + tanh_part) + 0.5 * values * (1.0 - tanh_part * tanh_part) * tanh_coeff * (
        1.0 + 3.0 * cubic_coeff * values * values
    )
    return value, slope


def padded(rows, multiple):
    return -(-rows // multiple) * multiple


def bf16_terms(values, count):
    terms = []
    for _ in range(count):
        term = values.astype(jnp.bfloat16).astype(jnp.float32)
        terms.append(term)
        values = values - term
    return terms


def in_lanes(columns, lane):
    row = jnp.zeros((columns[0].shape[0], LANES), jnp.float32)
    for i, column in enumerate(columns):
        row = jnp.where(lane == i, column, row)
    return row


def from_lanes(row, lane, first, count):
    keep = (lane >= first) & (lane < first + count)
    return jnp.sum(jnp.where(keep, row, 0.0), axis=1, keepdims=True)


def lanes_of(rows):
    return lax.broadcasted_iota(jnp.int32, (rows, LANES), 1)


def call(kernel, out_shape, scratch_shapes, inputs, far=0, far_out=0):
    near = len(inputs) - far
    spaces = [pltpu.VMEM] * near + [pltpu.HBM] * far
    inputs = inputs[:near] + [pltpu.with_memory_space_constraint(x, pltpu.HBM) for x in inputs[near:]]
    outs = len(out_shape)
    out_spaces = [pltpu.VMEM] * (outs - far_out) + [pltpu.HBM] * far_out
    return pl.pallas_call(
        kernel,
        out_shape=out_shape,
        in_specs=[pl.BlockSpec(memory_space=space) for space in spaces],
        out_specs=tuple(pl.BlockSpec(memory_space=space) for space in out_spaces),
        scratch_shapes=scratch_shapes,
        compiler_params=pltpu.CompilerParams(vmem_limit_bytes=24 * 1024 * 1024),
    )(*inputs)


def keys_kernel(
    key_in_ref, tokens_in_ref, cotangent_in_ref, out_ref, tokens_ref, cotangent_ref, key_ref, rows_ref, sems
):
    copies = [
        pltpu.make_async_copy(source, target, sems.at[i])
        for i, (source, target) in enumerate(
            [(key_in_ref, key_ref), (tokens_in_ref, tokens_ref), (cotangent_in_ref, cotangent_ref)]
        )
    ]
    for copy in copies:
        copy.start()
    width = key_ref.shape[1]
    copies[0].wait()
    key = key_ref[...].astype(jnp.float32)
    rows_ref[0:1, :] = key[:, : width // 2]
    rows_ref[1:2, :] = key[:, width // 2 :]
    block = rows_ref[...].astype(jnp.bfloat16)
    for i in range(out_ref.shape[0]):
        out_ref[i] = block
    copies[1].wait()
    copies[2].wait()


def sums_kernel(
    keys_ref, tokens_ref, tokens_other_ref, cotangent_ref, cotangent_other_ref,
    message_ref, logits_ref, comb_ref, keys_all_ref, keys_rows_ref, rows_ref,
):
    slots = keys_ref.shape[0]
    width = tokens_ref.shape[1]
    half = width // 2
    chunks = half // LANES
    first = pl.multiple_of(lax.rem(lax.axis_index("seq"), 2) * half, LANES)

    keys_rows_ref[...] = keys_ref[...].astype(jnp.float32)
    keys = jnp.concatenate([keys_rows_ref[:, 0, :], keys_rows_ref[:, 1, :]], axis=1).astype(jnp.bfloat16)
    keys_all_ref[...] = keys
    other_logits = dot(keys, tokens_other_ref[...], 1, 1)
    logits = jnp.concatenate([dot(keys, tokens_ref[...], 1, 1), other_logits], axis=1)
    logits_ref[...] = logits
    own = tokens_ref.shape[0]

    row_terms = jnp.exp(logits - jnp.max(logits, axis=0, keepdims=True))
    comb_prob = row_terms / jnp.sum(row_terms, axis=0, keepdims=True)
    comb_ref[...] = comb_prob
    combine = comb_prob.astype(jnp.bfloat16)
    grad_sums = dot(combine[:, :own], cotangent_ref[:, pl.ds(first, half)], 1, 0) + dot(
        combine[:, own:], cotangent_other_ref[:, pl.ds(first, half)], 1, 0
    )

    peak = jnp.max(logits, axis=1, keepdims=True)
    terms = jnp.exp(logits - peak)
    total = jnp.sum(terms, axis=1, keepdims=True)
    parts = jnp.concatenate(bf16_terms(terms, 2), axis=0).astype(jnp.bfloat16)
    sums = dot(parts[:, :own], tokens_ref[:, pl.ds(first, half)], 1, 0) + dot(
        parts[:, own:], tokens_other_ref[:, pl.ds(first, half)], 1, 0
    )
    high, low = bf16_terms(sums[:slots] + sums[slots:], 2)
    for j in range(chunks):
        columns = slice(j * LANES, (j + 1) * LANES)
        rows_ref[:, j, :] = high[:, columns]
        rows_ref[:, chunks + j, :] = low[:, columns]
        rows_ref[:, 2 * chunks + j, :] = grad_sums[:, columns]
    stats = in_lanes(bf16_terms(peak, 3) + bf16_terms(total, 3), lanes_of(slots))
    rows_ref[:, 3 * chunks, :] = stats
    for j in range(3 * chunks + 1, rows_ref.shape[1]):
        rows_ref[:, j, :] = jnp.zeros_like(stats)
    block = rows_ref[...].astype(jnp.bfloat16)
    for q in range(message_ref.shape[0] // slots):
        message_ref[q * slots : (q + 1) * slots] = block


def lane_sums_times(row, w_ref, first, count):
    row_chunks = [
        row[:, j * LANES : (j + 1) * LANES].astype(jnp.float32) for j in range(row.shape[1] // LANES)
    ]
    highs, lows = [], []
    for start in range(first, first + count, 16):
        total = None
        for j, chunk in enumerate(row_chunks):
            term = w_ref[start : start + 16, j * LANES : (j + 1) * LANES].astype(jnp.float32) * chunk
            total = term if total is None else total + term
        high = total.astype(jnp.bfloat16)
        highs.append(high)
        lows.append((total - high.astype(jnp.float32)).astype(jnp.bfloat16))
    ones = jnp.ones((8, LANES), jnp.bfloat16)
    sums = dot(ones, jnp.concatenate(highs, axis=0), 1, 1) + dot(ones, jnp.concatenate(lows, axis=0), 1, 1)
    return sums[:1]


def rows_times(pairs):
    results, taken = [], 0
    for row, w_ref in pairs:
        rows = w_ref.shape[0]
        block = LANES if rows % LANES == 0 else rows
        outs = []
        for first in range(0, rows, block):
            taken += VECTOR_SHARE
            if taken >= 1.0 and block == LANES:
                taken -= 1.0
                outs.append(lane_sums_times(row, w_ref, first, block))
            else:
                outs.append(dot(row, w_ref[first : first + block, :], 1, 1))
        results.append(jnp.concatenate(outs, axis=1))
    return results


def column_sums_times(row, w_ref, first, count):
    column = jnp.transpose(jnp.broadcast_to(row.astype(jnp.float32), (8, count)))[:, :1]
    total = None
    for start in range(0, count, 16):
        rows = w_ref[first + start : first + start + 16, :].astype(jnp.float32)
        term = rows * column[start : start + 16]
        total = term if total is None else total + term
    return total


def sums_times(pairs):
    results, taken = [], 0
    for row, w_ref in pairs:
        rows = w_ref.shape[0]
        block = LANES if rows % LANES == 0 else rows
        vector_total, matrix_blocks = None, []
        for first in range(0, rows, block):
            taken += SUM_SHARE
            if taken >= 1.0 and block == LANES:
                taken -= 1.0
                part = column_sums_times(row[:, first : first + block], w_ref, first, block)
                vector_total = part if vector_total is None else vector_total + part
            else:
                matrix_blocks.append(dot(row[:, first : first + block], w_ref[first : first + block, :], 1, 0))
        total = matrix_blocks[0]
        for part in matrix_blocks[1:]:
            total = total + part
        if vector_total is not None:
            total = total + jnp.sum(vector_total, axis=0, keepdims=True)
        results.append(total)
    return results


def expert_kernel(
    exp_size, parts_ref, w_in_ref, w_out_ref,
    message_ref, slot_in_ref, slot_out_grad_ref, hidden_rows_ref, parts_rows_ref, rows_ref,
):
    devices = parts_ref.shape[0]
    seq_size = devices // exp_size
    width = w_in_ref.shape[1]
    chunks = width // LANES
    per_side = chunks // 2
    parts_rows_ref[...] = parts_ref[...].astype(jnp.float32)
    stats = parts_rows_ref[:, 3 * per_side, :]
    lane = lanes_of(devices)
    peaks = from_lanes(stats, lane, 0, 3)
    totals = from_lanes(stats, lane, 3, 3)
    slot_peak = jnp.max(peaks, axis=0, keepdims=True)
    scale = jnp.exp(peaks - slot_peak)

    def of_side(values, side):
        total = values[side * exp_size : (side + 1) * exp_size]
        for q in range(side + 2, seq_size, 2):
            total = total + values[q * exp_size : (q + 1) * exp_size]
        return jnp.sum(total, axis=0, keepdims=True)

    slot_total = of_side(totals * scale, 0)
    slot_chunks, grad_chunks = [[], []], [[], []]
    for j in range(per_side):
        weighted = (parts_rows_ref[:, j, :] + parts_rows_ref[:, per_side + j, :]) * scale
        grads = parts_rows_ref[:, 2 * per_side + j, :]
        for side in range(2):
            slot_chunks[side].append(of_side(weighted, side))
            grad_chunks[side].append(of_side(grads, side))
    slot_row = jnp.concatenate(slot_chunks[0] + slot_chunks[1], axis=1) / slot_total
    slot_in = slot_row.astype(jnp.bfloat16)
    slot_out_grad = jnp.concatenate(grad_chunks[0] + grad_chunks[1], axis=1).astype(jnp.bfloat16)
    slot_in_ref[...] = slot_in
    slot_out_grad_ref[...] = slot_out_grad

    pre_act, act_grad = rows_times([(slot_in, w_in_ref), (slot_out_grad, w_out_ref)])
    value, slope = gelu_parts(pre_act)
    activation = value.astype(jnp.bfloat16)
    pre_grad = (act_grad * slope).astype(jnp.bfloat16)
    hidden_rows_ref[...] = jnp.concatenate([value, act_grad * slope], axis=0).astype(jnp.bfloat16)
    out_part, grad_part = sums_times([(activation, w_out_ref), (pre_grad, w_in_ref)])
    grad_part = grad_part.astype(jnp.bfloat16).astype(jnp.float32)
    correction = jnp.sum(slot_row * grad_part, axis=1, keepdims=True)
    stats = in_lanes(
        bf16_terms(slot_peak, 3) + bf16_terms(slot_total, 3) + bf16_terms(correction, 3), lanes_of(1)
    )
    rows_ref[0:1, :width] = out_part
    rows_ref[1:2, :width] = grad_part
    rows_ref[0:1, width:] = stats
    rows_ref[1:2, width:] = jnp.zeros_like(stats)
    block = rows_ref[...].astype(jnp.bfloat16)
    for i in range(devices):
        message_ref[i] = block


def grads_kernel(
    parts_ref, logits_ref, comb_ref, tokens_ref, tokens_other_ref, cotangent_ref, cotangent_other_ref,
    message_ref, slot_out_ref, slot_in_grad_ref, factors_ref, parts_rows_ref,
):
    devices = parts_ref.shape[0]
    slots, _ = logits_ref.shape
    seq_size = devices // slots
    own, width = tokens_ref.shape
    half = width // 2
    chunks = width // LANES
    first = pl.multiple_of(lax.rem(lax.axis_index("seq"), 2) * half, LANES)
    parts_rows_ref[...] = parts_ref[...].astype(jnp.float32)
    out_rows = parts_rows_ref[:, 0, :width]
    grad_rows = parts_rows_ref[:, 1, :width]
    stats = parts_rows_ref[:, 0, width:]
    lane = lanes_of(slots)

    def over_seq(values):
        total = values[:slots]
        for q in range(1, seq_size):
            total = total + values[q * slots : (q + 1) * slots]
        return total

    peak = from_lanes(stats[:slots], lane, 0, 3)
    total = from_lanes(stats[:slots], lane, 3, 3)
    correction = from_lanes(over_seq(stats), lane, 6, 3)
    slot_out_ref[...] = over_seq(out_rows).astype(jnp.bfloat16)
    slot_in_grad_ref[...] = over_seq(grad_rows).astype(jnp.bfloat16)
    out_rows = out_rows.astype(jnp.bfloat16)
    grad_rows = grad_rows.astype(jnp.bfloat16)
    comb_grad = over_seq(
        jnp.concatenate(
            [dot(out_rows, cotangent_ref[...], 1, 1), dot(out_rows, cotangent_other_ref[...], 1, 1)], axis=1
        )
    )
    disp_grad = over_seq(
        jnp.concatenate(
            [dot(grad_rows, tokens_ref[...], 1, 1), dot(grad_rows, tokens_other_ref[...], 1, 1)], axis=1
        )
    )
    comb_prob = comb_ref[...]
    disp_prob = jnp.exp(logits_ref[...] - peak) / total
    comb_mean = jnp.sum(comb_prob * comb_grad, axis=0, keepdims=True)
    logit_grad = (
        comb_prob * (comb_grad - comb_mean) + disp_prob * (disp_grad - correction)
    ).astype(jnp.bfloat16)
    factors = [comb_prob[:, :own], disp_prob[:, :own], logit_grad[:, :own]]
    for i, factor in enumerate(factors):
        factors_ref[i * slots : (i + 1) * slots] = factor.astype(jnp.bfloat16).astype(jnp.float32)
    keys_part = dot(logit_grad[:, :own], tokens_ref[:, pl.ds(first, half)], 1, 0) + dot(
        logit_grad[:, own:], tokens_other_ref[:, pl.ds(first, half)], 1, 0
    )
    for s in range(slots):
        for q in range(seq_size):
            message_ref[q * slots + s] = keys_part[s : s + 1]


def block_of(rows):
    return 128 if rows % 128 == 0 else rows


def weight_grads_kernel(hidden_rows_ref, slot_in_ref, slot_out_grad_ref, w_in_grad_ref, w_out_grad_ref, near_ref, sems):
    hidden = near_ref.shape[1]
    block = block_of(hidden)
    hidden_rows = hidden_rows_ref[...].astype(jnp.float32)
    copies = []
    for w, (hidden_index, row_ref, far_ref) in enumerate(
        [(0, slot_out_grad_ref, w_out_grad_ref), (1, slot_in_ref, w_in_grad_ref)]
    ):
        row = row_ref[...].astype(jnp.float32)
        for i in range(hidden // block):
            rows = pl.ds(i * block, block)
            part = hidden_rows[hidden_index : hidden_index + 1, i * block : (i + 1) * block]
            column = jnp.transpose(jnp.broadcast_to(part, (8, block)))[:, :1]
            near_ref[w, rows, :] = (column * row).astype(jnp.bfloat16)
            copy = pltpu.make_async_copy(near_ref.at[w, rows], far_ref.at[0, rows], sems.at[w, i])
            copy.start()
            copies.append(copy)
    for copy in copies:
        copy.wait()


def outputs_kernel(
    keys_parts_ref, factors_ref, slot_out_ref, slot_in_grad_ref, keys_ref,
    layer_out_ref, tokens_grad_ref, keys_grad_ref, layer_near_ref, tokens_near_ref, keys_near_ref, sems,
):
    slots = slot_out_ref.shape[0]
    half = keys_parts_ref.shape[2]
    copies = [
        pltpu.make_async_copy(near, far, sems.at[i])
        for i, (near, far) in enumerate(
            [(layer_near_ref, layer_out_ref), (tokens_near_ref, tokens_grad_ref), (keys_near_ref, keys_grad_ref)]
        )
    ]
    combine = jnp.transpose(factors_ref[:slots, :]).astype(jnp.bfloat16)
    layer_near_ref[...] = dot(combine, slot_out_ref[...], 1, 0).astype(jnp.bfloat16)
    copies[0].start()
    others = jnp.transpose(factors_ref[slots:, :]).astype(jnp.bfloat16)
    rows = jnp.concatenate(
        [slot_in_grad_ref[...].astype(jnp.float32), keys_ref[...].astype(jnp.float32)], axis=0
    ).astype(jnp.bfloat16)
    tokens_near_ref[...] = dot(others, rows, 1, 0).astype(jnp.bfloat16)
    copies[1].start()
    for side in range(2):
        total = keys_parts_ref[side * slots : (side + 1) * slots, 0, :]
        for first in range((side + 2) * slots, keys_parts_ref.shape[0], 2 * slots):
            total = total + keys_parts_ref[first : first + slots, 0, :]
        keys_near_ref[:, side * half : (side + 1) * half] = jnp.sum(total, axis=0, keepdims=True)
    copies[2].start()
    for copy in copies:
        copy.wait()


def local(tokens, slot_keys, w_in, w_out, cotangent):
    both = ("seq", "exp")
    seq_size, exp_size = lax.axis_size("seq"), lax.axis_size("exp")
    devices = seq_size * exp_size
    experts, hidden, width = w_in.shape
    assert experts == 1 and seq_size % 2 == 0
    slots = exp_size
    half = width // 2
    own = tokens.shape[0]
    swap = [(i, i ^ 1) for i in range(seq_size)]
    f32, bf16 = jnp.float32, jnp.bfloat16
    shape = jax.ShapeDtypeStruct

    key_message, tokens_near, cotangent_near = call(
        keys_kernel,
        (
            shape((exp_size, 2, half), bf16),
            shape(tokens.shape, bf16),
            shape(cotangent.shape, bf16),
        ),
        [pltpu.VMEM((1, width), bf16), pltpu.VMEM((2, half), f32), pltpu.SemaphoreType.DMA((3,))],
        [slot_keys.T, tokens, cotangent],
        far=3,
    )
    tokens_other = lax.ppermute(tokens, "seq", swap)
    cotangent_other = lax.ppermute(cotangent, "seq", swap)
    keys = lax.all_to_all(key_message, "exp", 0, 0, tiled=True)
    keys, w_in_late, w_out_late, tokens_other, cotangent_other = lax.optimization_barrier((keys, w_in, w_out, tokens_other, cotangent_other))
    w_in_other = lax.ppermute(w_in_late, "seq", swap)
    w_out_other = lax.ppermute(w_out_late, "seq", swap)

    sum_rows = padded(3 * half // LANES + 1, 16)
    message, logits, comb_prob, keys_all = call(
        sums_kernel,
        (
            shape((devices, sum_rows, LANES), bf16),
            shape((slots, 2 * own), f32),
            shape((slots, 2 * own), f32),
            shape((slots, width), bf16),
        ),
        [
            pltpu.VMEM((slots, 2, half), f32),
            pltpu.VMEM((slots, sum_rows, LANES), f32),
        ],
        [keys, tokens_near, tokens_other, cotangent_near, cotangent_other],
    )
    parts = lax.all_to_all(message, both, 0, 0, tiled=True)

    message, slot_in, slot_out_grad, hidden_rows = call(
        functools.partial(expert_kernel, exp_size),
        (
            shape((devices, 2, width + LANES), bf16),
            shape((1, width), bf16),
            shape((1, width), bf16),
            shape((2, hidden), bf16),
        ),
        [pltpu.VMEM((devices, sum_rows, LANES), f32), pltpu.VMEM((2, width + LANES), f32)],
        [parts, w_in_other[0], w_out_other[0]],
    )
    gathered = lax.all_to_all(message, both, 0, 0, tiled=True)
    own_rows = lax.ppermute(hidden_rows, "seq", swap)
    w_in_grad, w_out_grad = call(
        weight_grads_kernel,
        (shape((1, hidden, width), bf16), shape((1, hidden, width), bf16)),
        [
            pltpu.VMEM((2, hidden, width), bf16),
            pltpu.SemaphoreType.DMA((2, hidden // block_of(hidden))),
        ],
        [own_rows, slot_in, slot_out_grad],
        far_out=2,
    )
    gathered, w_in_grad, w_out_grad = lax.optimization_barrier((gathered, w_in_grad, w_out_grad))

    message, slot_out, slot_in_grad, factors = call(
        grads_kernel,
        (
            shape((devices, 1, half), f32),
            shape((slots, width), bf16),
            shape((slots, width), bf16),
            shape((3 * slots, own), f32),
        ),
        [pltpu.VMEM((devices, 2, width + LANES), f32)],
        [gathered, logits, comb_prob, tokens_near, tokens_other, cotangent_near, cotangent_other],
    )
    keys_parts = lax.all_to_all(message, both, 0, 0, tiled=True)
    layer_out, tokens_grad, keys_grad = call(
        outputs_kernel,
        (shape((own, width), bf16), shape((own, width), bf16), shape((1, width), f32)),
        [
            pltpu.VMEM((own, width), bf16),
            pltpu.VMEM((own, width), bf16),
            pltpu.VMEM((1, width), f32),
            pltpu.SemaphoreType.DMA((3,)),
        ],
        [keys_parts, factors, slot_out, slot_in_grad, keys_all],
        far_out=3,
    )
    return (layer_out, tokens_grad, keys_grad.T, w_in_grad, w_out_grad)


def solution(mesh):
    return jax.shard_map(
        local,
        mesh=mesh,
        in_specs=(
            P(("seq", "exp"), None),
            P(None, "exp"),
            P("exp", "seq", None),
            P("exp", "seq", None),
            P(("seq", "exp"), None),
        ),
        out_specs=(
            P(("seq", "exp"), None),
            P(("seq", "exp"), None),
            P(None, "exp"),
            P("exp", "seq", None),
            P("exp", "seq", None),
        ),
        check_vma=False,
    )
```

```python
import functools

import jax
import jax.numpy as jnp
from jax import lax
from jax.experimental import pallas as pl
from jax.experimental.pallas import tpu as pltpu
from jax.sharding import PartitionSpec as P

tanh_coeff = 0.7978845608028654
cubic_coeff = 0.044715
LANES = 128
VECTOR_SHARE = 0.65
SUM_SHARE = 0.25


def dot(left, right, left_dim, right_dim):
    return lax.dot_general(
        left, right, (((left_dim,), (right_dim,)), ((), ())), preferred_element_type=jnp.float32
    )


def gelu_parts(values):
    tanh_part = jnp.tanh(tanh_coeff * (values + cubic_coeff * values * values * values))
    value = 0.5 * values * (1.0 + tanh_part)
    slope = 0.5 * (1.0 + tanh_part) + 0.5 * values * (1.0 - tanh_part * tanh_part) * tanh_coeff * (
        1.0 + 3.0 * cubic_coeff * values * values
    )
    return value, slope


def padded(rows, multiple):
    return -(-rows // multiple) * multiple


def bf16_terms(values, count):
    terms = []
    for _ in range(count):
        term = values.astype(jnp.bfloat16).astype(jnp.float32)
        terms.append(term)
        values = values - term
    return terms


def in_lanes(columns, lane):
    row = jnp.zeros((columns[0].shape[0], LANES), jnp.float32)
    for i, column in enumerate(columns):
        row = jnp.where(lane == i, column, row)
    return row


def from_lanes(row, lane, first, count):
    keep = (lane >= first) & (lane < first + count)
    return jnp.sum(jnp.where(keep, row, 0.0), axis=1, keepdims=True)


def lanes_of(rows):
    return lax.broadcasted_iota(jnp.int32, (rows, LANES), 1)


def call(kernel, out_shape, scratch_shapes, inputs, far=0, far_out=0):
    near = len(inputs) - far
    spaces = [pltpu.VMEM] * near + [pltpu.HBM] * far
    inputs = inputs[:near] + [pltpu.with_memory_space_constraint(x, pltpu.HBM) for x in inputs[near:]]
    outs = len(out_shape)
    out_spaces = [pltpu.VMEM] * (outs - far_out) + [pltpu.HBM] * far_out
    return pl.pallas_call(
        kernel,
        out_shape=out_shape,
        in_specs=[pl.BlockSpec(memory_space=space) for space in spaces],
        out_specs=tuple(pl.BlockSpec(memory_space=space) for space in out_spaces),
        scratch_shapes=scratch_shapes,
        compiler_params=pltpu.CompilerParams(vmem_limit_bytes=24 * 1024 * 1024),
    )(*inputs)


def keys_kernel(
    key_in_ref, tokens_in_ref, cotangent_in_ref, out_ref, tokens_ref, cotangent_ref, key_ref, rows_ref, sems
):
    copies = [
        pltpu.make_async_copy(source, target, sems.at[i])
        for i, (source, target) in enumerate(
            [(key_in_ref, key_ref), (tokens_in_ref, tokens_ref), (cotangent_in_ref, cotangent_ref)]
        )
    ]
    for copy in copies:
        copy.start()
    width = key_ref.shape[1]
    copies[0].wait()
    key = key_ref[...].astype(jnp.float32)
    rows_ref[0:1, :] = key[:, : width // 2]
    rows_ref[1:2, :] = key[:, width // 2 :]
    block = rows_ref[...].astype(jnp.bfloat16)
    for i in range(out_ref.shape[0]):
        out_ref[i] = block
    copies[1].wait()
    copies[2].wait()


def sums_kernel(
    keys_ref, tokens_ref, tokens_other_ref, cotangent_ref, cotangent_other_ref,
    message_ref, logits_ref, comb_ref, keys_all_ref, keys_rows_ref, rows_ref,
):
    slots = keys_ref.shape[0]
    width = tokens_ref.shape[1]
    half = width // 2
    chunks = half // LANES
    first = pl.multiple_of(lax.rem(lax.axis_index("seq"), 2) * half, LANES)

    keys_rows_ref[...] = keys_ref[...].astype(jnp.float32)
    keys = jnp.concatenate([keys_rows_ref[:, 0, :], keys_rows_ref[:, 1, :]], axis=1).astype(jnp.bfloat16)
    keys_all_ref[...] = keys
    other_logits = dot(keys, tokens_other_ref[...], 1, 1)
    logits = jnp.concatenate([dot(keys, tokens_ref[...], 1, 1), other_logits], axis=1)
    logits_ref[...] = logits
    own = tokens_ref.shape[0]

    row_terms = jnp.exp(logits - jnp.max(logits, axis=0, keepdims=True))
    comb_prob = row_terms / jnp.sum(row_terms, axis=0, keepdims=True)
    comb_ref[...] = comb_prob
    combine = comb_prob.astype(jnp.bfloat16)
    grad_sums = dot(combine[:, :own], cotangent_ref[:, pl.ds(first, half)], 1, 0) + dot(
        combine[:, own:], cotangent_other_ref[:, pl.ds(first, half)], 1, 0
    )

    peak = jnp.max(logits, axis=1, keepdims=True)
    terms = jnp.exp(logits - peak)
    total = jnp.sum(terms, axis=1, keepdims=True)
    parts = jnp.concatenate(bf16_terms(terms, 2), axis=0).astype(jnp.bfloat16)
    sums = dot(parts[:, :own], tokens_ref[:, pl.ds(first, half)], 1, 0) + dot(
        parts[:, own:], tokens_other_ref[:, pl.ds(first, half)], 1, 0
    )
    high, low = bf16_terms(sums[:slots] + sums[slots:], 2)
    for j in range(chunks):
        columns = slice(j * LANES, (j + 1) * LANES)
        rows_ref[:, j, :] = high[:, columns]
        rows_ref[:, chunks + j, :] = low[:, columns]
        rows_ref[:, 2 * chunks + j, :] = grad_sums[:, columns]
    stats = in_lanes(bf16_terms(peak, 3) + bf16_terms(total, 3), lanes_of(slots))
    rows_ref[:, 3 * chunks, :] = stats
    for j in range(3 * chunks + 1, rows_ref.shape[1]):
        rows_ref[:, j, :] = jnp.zeros_like(stats)
    block = rows_ref[...].astype(jnp.bfloat16)
    for q in range(message_ref.shape[0] // slots):
        message_ref[q * slots : (q + 1) * slots] = block


def lane_sums_times(row, w_ref, first, count):
    row_chunks = [
        row[:, j * LANES : (j + 1) * LANES].astype(jnp.float32) for j in range(row.shape[1] // LANES)
    ]
    highs, lows = [], []
    for start in range(first, first + count, 16):
        total = None
        for j, chunk in enumerate(row_chunks):
            term = w_ref[start : start + 16, j * LANES : (j + 1) * LANES].astype(jnp.float32) * chunk
            total = term if total is None else total + term
        high = total.astype(jnp.bfloat16)
        highs.append(high)
        lows.append((total - high.astype(jnp.float32)).astype(jnp.bfloat16))
    ones = jnp.ones((8, LANES), jnp.bfloat16)
    sums = dot(ones, jnp.concatenate(highs, axis=0), 1, 1) + dot(ones, jnp.concatenate(lows, axis=0), 1, 1)
    return sums[:1]


def rows_times(pairs):
    results, taken = [], 0
    for row, w_ref in pairs:
        rows = w_ref.shape[0]
        block = LANES if rows % LANES == 0 else rows
        outs = []
        for first in range(0, rows, block):
            taken += VECTOR_SHARE
            if taken >= 1.0 and block == LANES:
                taken -= 1.0
                outs.append(lane_sums_times(row, w_ref, first, block))
            else:
                outs.append(dot(row, w_ref[first : first + block, :], 1, 1))
        results.append(jnp.concatenate(outs, axis=1))
    return results


def column_sums_times(row, w_ref, first, count):
    column = jnp.transpose(jnp.broadcast_to(row.astype(jnp.float32), (8, count)))[:, :1]
    total = None
    for start in range(0, count, 16):
        rows = w_ref[first + start : first + start + 16, :].astype(jnp.float32)
        term = rows * column[start : start + 16]
        total = term if total is None else total + term
    return total


def sums_times(pairs):
    results, taken = [], 0
    for row, w_ref in pairs:
        rows = w_ref.shape[0]
        block = LANES if rows % LANES == 0 else rows
        vector_total, matrix_blocks = None, []
        for first in range(0, rows, block):
            taken += SUM_SHARE
            if taken >= 1.0 and block == LANES:
                taken -= 1.0
                part = column_sums_times(row[:, first : first + block], w_ref, first, block)
                vector_total = part if vector_total is None else vector_total + part
            else:
                matrix_blocks.append(dot(row[:, first : first + block], w_ref[first : first + block, :], 1, 0))
        total = matrix_blocks[0]
        for part in matrix_blocks[1:]:
            total = total + part
        if vector_total is not None:
            total = total + jnp.sum(vector_total, axis=0, keepdims=True)
        results.append(total)
    return results


def expert_kernel(
    exp_size, parts_ref, w_in_ref, w_out_ref,
    message_ref, slot_in_ref, slot_out_grad_ref, hidden_rows_ref, parts_rows_ref, rows_ref,
):
    devices = parts_ref.shape[0]
    seq_size = devices // exp_size
    width = w_in_ref.shape[1]
    chunks = width // LANES
    per_side = chunks // 2
    parts_rows_ref[...] = parts_ref[...].astype(jnp.float32)
    stats = parts_rows_ref[:, 3 * per_side, :]
    lane = lanes_of(devices)
    peaks = from_lanes(stats, lane, 0, 3)
    totals = from_lanes(stats, lane, 3, 3)
    slot_peak = jnp.max(peaks, axis=0, keepdims=True)
    scale = jnp.exp(peaks - slot_peak)

    def of_side(values, side):
        total = values[side * exp_size : (side + 1) * exp_size]
        for q in range(side + 2, seq_size, 2):
            total = total + values[q * exp_size : (q + 1) * exp_size]
        return jnp.sum(total, axis=0, keepdims=True)

    slot_total = of_side(totals * scale, 0)
    slot_chunks, grad_chunks = [[], []], [[], []]
    for j in range(per_side):
        weighted = (parts_rows_ref[:, j, :] + parts_rows_ref[:, per_side + j, :]) * scale
        grads = parts_rows_ref[:, 2 * per_side + j, :]
        for side in range(2):
            slot_chunks[side].append(of_side(weighted, side))
            grad_chunks[side].append(of_side(grads, side))
    slot_row = jnp.concatenate(slot_chunks[0] + slot_chunks[1], axis=1) / slot_total
    slot_in = slot_row.astype(jnp.bfloat16)
    slot_out_grad = jnp.concatenate(grad_chunks[0] + grad_chunks[1], axis=1).astype(jnp.bfloat16)
    slot_in_ref[...] = slot_in
    slot_out_grad_ref[...] = slot_out_grad

    pre_act, act_grad = rows_times([(slot_in, w_in_ref), (slot_out_grad, w_out_ref)])
    value, slope = gelu_parts(pre_act)
    activation = value.astype(jnp.bfloat16)
    pre_grad = (act_grad * slope).astype(jnp.bfloat16)
    hidden_rows_ref[...] = jnp.concatenate([value, act_grad * slope], axis=0).astype(jnp.bfloat16)
    out_part, grad_part = sums_times([(activation, w_out_ref), (pre_grad, w_in_ref)])
    grad_part = grad_part.astype(jnp.bfloat16).astype(jnp.float32)
    correction = jnp.sum(slot_row * grad_part, axis=1, keepdims=True)
    stats = in_lanes(
        bf16_terms(slot_peak, 3) + bf16_terms(slot_total, 3) + bf16_terms(correction, 3), lanes_of(1)
    )
    rows_ref[0:1, :width] = out_part
    rows_ref[1:2, :width] = grad_part
    rows_ref[0:1, width:] = stats
    rows_ref[1:2, width:] = jnp.zeros_like(stats)
    block = rows_ref[...].astype(jnp.bfloat16)
    for i in range(devices):
        message_ref[i] = block


def grads_kernel(
    parts_ref, logits_ref, comb_ref, tokens_ref, tokens_other_ref, cotangent_ref, cotangent_other_ref,
    message_ref, slot_out_ref, slot_in_grad_ref, factors_ref, parts_rows_ref,
):
    devices = parts_ref.shape[0]
    slots, _ = logits_ref.shape
    seq_size = devices // slots
    own, width = tokens_ref.shape
    half = width // 2
    chunks = width // LANES
    first = pl.multiple_of(lax.rem(lax.axis_index("seq"), 2) * half, LANES)
    parts_rows_ref[...] = parts_ref[...].astype(jnp.float32)
    out_rows = parts_rows_ref[:, 0, :width]
    grad_rows = parts_rows_ref[:, 1, :width]
    stats = parts_rows_ref[:, 0, width:]
    lane = lanes_of(slots)

    def over_seq(values):
        total = values[:slots]
        for q in range(1, seq_size):
            total = total + values[q * slots : (q + 1) * slots]
        return total

    peak = from_lanes(stats[:slots], lane, 0, 3)
    total = from_lanes(stats[:slots], lane, 3, 3)
    correction = from_lanes(over_seq(stats), lane, 6, 3)
    slot_out_ref[...] = over_seq(out_rows).astype(jnp.bfloat16)
    slot_in_grad_ref[...] = over_seq(grad_rows).astype(jnp.bfloat16)
    out_rows = out_rows.astype(jnp.bfloat16)
    grad_rows = grad_rows.astype(jnp.bfloat16)
    comb_grad = over_seq(
        jnp.concatenate(
            [dot(out_rows, cotangent_ref[...], 1, 1), dot(out_rows, cotangent_other_ref[...], 1, 1)], axis=1
        )
    )
    disp_grad = over_seq(
        jnp.concatenate(
            [dot(grad_rows, tokens_ref[...], 1, 1), dot(grad_rows, tokens_other_ref[...], 1, 1)], axis=1
        )
    )
    comb_prob = comb_ref[...]
    disp_prob = jnp.exp(logits_ref[...] - peak) / total
    comb_mean = jnp.sum(comb_prob * comb_grad, axis=0, keepdims=True)
    logit_grad = (
        comb_prob * (comb_grad - comb_mean) + disp_prob * (disp_grad - correction)
    ).astype(jnp.bfloat16)
    factors = [comb_prob[:, :own], disp_prob[:, :own], logit_grad[:, :own]]
    for i, factor in enumerate(factors):
        factors_ref[i * slots : (i + 1) * slots] = factor.astype(jnp.bfloat16).astype(jnp.float32)
    keys_part = dot(logit_grad[:, :own], tokens_ref[:, pl.ds(first, half)], 1, 0) + dot(
        logit_grad[:, own:], tokens_other_ref[:, pl.ds(first, half)], 1, 0
    )
    for s in range(slots):
        for q in range(seq_size):
            message_ref[q * slots + s] = keys_part[s : s + 1]


def block_of(rows):
    return 128 if rows % 128 == 0 else rows


def weight_grads_kernel(hidden_rows_ref, slot_in_ref, slot_out_grad_ref, w_in_grad_ref, w_out_grad_ref, near_ref, sems):
    hidden = near_ref.shape[1]
    block = block_of(hidden)
    hidden_rows = hidden_rows_ref[...].astype(jnp.float32)
    copies = []
    for w, (hidden_index, row_ref, far_ref) in enumerate(
        [(0, slot_out_grad_ref, w_out_grad_ref), (1, slot_in_ref, w_in_grad_ref)]
    ):
        row = row_ref[...].astype(jnp.float32)
        for i in range(hidden // block):
            rows = pl.ds(i * block, block)
            part = hidden_rows[hidden_index : hidden_index + 1, i * block : (i + 1) * block]
            column = jnp.transpose(jnp.broadcast_to(part, (8, block)))[:, :1]
            near_ref[w, rows, :] = (column * row).astype(jnp.bfloat16)
            copy = pltpu.make_async_copy(near_ref.at[w, rows], far_ref.at[0, rows], sems.at[w, i])
            copy.start()
            copies.append(copy)
    for copy in copies:
        copy.wait()


def outputs_kernel(
    keys_parts_ref, factors_ref, slot_out_ref, slot_in_grad_ref, keys_ref,
    layer_out_ref, tokens_grad_ref, keys_grad_ref, layer_near_ref, tokens_near_ref, keys_near_ref, sems,
):
    slots = slot_out_ref.shape[0]
    half = keys_parts_ref.shape[2]
    copies = [
        pltpu.make_async_copy(near, far, sems.at[i])
        for i, (near, far) in enumerate(
            [(layer_near_ref, layer_out_ref), (tokens_near_ref, tokens_grad_ref), (keys_near_ref, keys_grad_ref)]
        )
    ]
    for side in range(2):
        total = keys_parts_ref[side * slots : (side + 1) * slots, 0, :]
        for first in range((side + 2) * slots, keys_parts_ref.shape[0], 2 * slots):
            total = total + keys_parts_ref[first : first + slots, 0, :]
        keys_near_ref[:, side * half : (side + 1) * half] = jnp.sum(total, axis=0, keepdims=True)
    copies[2].start()
    combine = jnp.transpose(factors_ref[:slots, :]).astype(jnp.bfloat16)
    layer_near_ref[...] = dot(combine, slot_out_ref[...], 1, 0).astype(jnp.bfloat16)
    copies[0].start()
    others = jnp.transpose(factors_ref[slots:, :]).astype(jnp.bfloat16)
    rows = jnp.concatenate(
        [slot_in_grad_ref[...].astype(jnp.float32), keys_ref[...].astype(jnp.float32)], axis=0
    ).astype(jnp.bfloat16)
    tokens_near_ref[...] = dot(others, rows, 1, 0).astype(jnp.bfloat16)
    copies[1].start()
    for copy in copies:
        copy.wait()


def local(tokens, slot_keys, w_in, w_out, cotangent):
    both = ("seq", "exp")
    seq_size, exp_size = lax.axis_size("seq"), lax.axis_size("exp")
    devices = seq_size * exp_size
    experts, hidden, width = w_in.shape
    assert experts == 1 and seq_size % 2 == 0
    slots = exp_size
    half = width // 2
    own = tokens.shape[0]
    swap = [(i, i ^ 1) for i in range(seq_size)]
    f32, bf16 = jnp.float32, jnp.bfloat16
    shape = jax.ShapeDtypeStruct

    key_message, tokens_near, cotangent_near = call(
        keys_kernel,
        (
            shape((exp_size, 2, half), bf16),
            shape(tokens.shape, bf16),
            shape(cotangent.shape, bf16),
        ),
        [pltpu.VMEM((1, width), bf16), pltpu.VMEM((2, half), f32), pltpu.SemaphoreType.DMA((3,))],
        [slot_keys.T, tokens, cotangent],
        far=3,
    )
    tokens_other = lax.ppermute(tokens, "seq", swap)
    cotangent_other = lax.ppermute(cotangent, "seq", swap)
    keys = lax.all_to_all(key_message, "exp", 0, 0, tiled=True)
    keys, w_in_late, w_out_late, tokens_other, cotangent_other = lax.optimization_barrier((keys, w_in, w_out, tokens_other, cotangent_other))
    w_in_other = lax.ppermute(w_in_late, "seq", swap)
    w_out_other = lax.ppermute(w_out_late, "seq", swap)

    sum_rows = padded(3 * half // LANES + 1, 16)
    message, logits, comb_prob, keys_all = call(
        sums_kernel,
        (
            shape((devices, sum_rows, LANES), bf16),
            shape((slots, 2 * own), f32),
            shape((slots, 2 * own), f32),
            shape((slots, width), bf16),
        ),
        [
            pltpu.VMEM((slots, 2, half), f32),
            pltpu.VMEM((slots, sum_rows, LANES), f32),
        ],
        [keys, tokens_near, tokens_other, cotangent_near, cotangent_other],
    )
    parts = lax.all_to_all(message, both, 0, 0, tiled=True)

    message, slot_in, slot_out_grad, hidden_rows = call(
        functools.partial(expert_kernel, exp_size),
        (
            shape((devices, 2, width + LANES), bf16),
            shape((1, width), bf16),
            shape((1, width), bf16),
            shape((2, hidden), bf16),
        ),
        [pltpu.VMEM((devices, sum_rows, LANES), f32), pltpu.VMEM((2, width + LANES), f32)],
        [parts, w_in_other[0], w_out_other[0]],
    )
    gathered = lax.all_to_all(message, both, 0, 0, tiled=True)
    own_rows = lax.ppermute(hidden_rows, "seq", swap)
    w_in_grad, w_out_grad = call(
        weight_grads_kernel,
        (shape((1, hidden, width), bf16), shape((1, hidden, width), bf16)),
        [
            pltpu.VMEM((2, hidden, width), bf16),
            pltpu.SemaphoreType.DMA((2, hidden // block_of(hidden))),
        ],
        [own_rows, slot_in, slot_out_grad],
        far_out=2,
    )
    gathered, w_in_grad, w_out_grad = lax.optimization_barrier((gathered, w_in_grad, w_out_grad))

    message, slot_out, slot_in_grad, factors = call(
        grads_kernel,
        (
            shape((devices, 1, half), f32),
            shape((slots, width), bf16),
            shape((slots, width), bf16),
            shape((3 * slots, own), f32),
        ),
        [pltpu.VMEM((devices, 2, width + LANES), f32)],
        [gathered, logits, comb_prob, tokens_near, tokens_other, cotangent_near, cotangent_other],
    )
    keys_parts = lax.all_to_all(message, both, 0, 0, tiled=True)
    layer_out, tokens_grad, keys_grad = call(
        outputs_kernel,
        (shape((own, width), bf16), shape((own, width), bf16), shape((1, width), f32)),
        [
            pltpu.VMEM((own, width), bf16),
            pltpu.VMEM((own, width), bf16),
            pltpu.VMEM((1, width), f32),
            pltpu.SemaphoreType.DMA((3,)),
        ],
        [keys_parts, factors, slot_out, slot_in_grad, keys_all],
        far_out=3,
    )
    return (layer_out, tokens_grad, keys_grad.T, w_in_grad, w_out_grad)


def solution(mesh):
    return jax.shard_map(
        local,
        mesh=mesh,
        in_specs=(
            P(("seq", "exp"), None),
            P(None, "exp"),
            P("exp", "seq", None),
            P("exp", "seq", None),
            P(("seq", "exp"), None),
        ),
        out_specs=(
            P(("seq", "exp"), None),
            P(("seq", "exp"), None),
            P(None, "exp"),
            P("exp", "seq", None),
            P("exp", "seq", None),
        ),
        check_vma=False,
    )
```
